32 devices in a mesh: band: 16 (over z, y, core), batch: 2 (over x).
Axes of the slice: x: 2, y: 2, z: 4, core: 2. Of those that a mesh axis runs over, the one named last changes fastest.
Arguments:
- tokens_in: bfloat16 [2, 2, 112, 112, 256], P(None, 'batch', 'band'), may hold values from -6 to 6
- cotangent: bfloat16 [2, 2, 112, 112, 256], P(None, 'batch', 'band'), may hold values from -6 to 6
- owners: int32 [4], replicated, may hold values from 0 to 31
- weight_qkv: float32 [32, 256, 768], P(('band', 'batch')), may hold values from -0.375 to 0.375
- weight_proj: float32 [32, 256, 256], P(('band', 'batch')), may hold values from -0.75 to 0.75
- weight_fc1: float32 [32, 256, 1024], P(('band', 'batch')), may hold values from -0.375 to 0.375
- weight_fc2: float32 [32, 1024, 256], P(('band', 'batch')), may hold values from -0.1875 to 0.1875
- first_qkv: float32 [32, 256, 768], P(('band', 'batch')), may hold values from -384 to 384
- second_qkv: float32 [32, 256, 768], P(('band', 'batch')), may hold values from 3010.56 to 12042.24
- first_proj: float32 [32, 256, 256], P(('band', 'batch')), may hold values from -384 to 384
- second_proj: float32 [32, 256, 256], P(('band', 'batch')), may hold values from 3010.56 to 12042.24
- first_fc1: float32 [32, 256, 1024], P(('band', 'batch')), may hold values from -384 to 384
- second_fc1: float32 [32, 256, 1024], P(('band', 'batch')), may hold values from 3010.56 to 12042.24
- first_fc2: float32 [32, 1024, 256], P(('band', 'batch')), may hold values from -384 to 384
- second_fc2: float32 [32, 1024, 256], P(('band', 'batch')), may hold values from 3010.56 to 12042.24
- left_qkv: float32 [256, 256], replicated, may hold values from -1 to 1, as said below
- right_qkv: float32 [768, 768], replicated, may hold values from -1 to 1, as said below
- left_proj: float32 [256, 256], replicated, may hold values from -1 to 1, as said below
- right_proj: float32 [256, 256], replicated, may hold values from -1 to 1, as said below
- left_fc1: float32 [256, 256], replicated, may hold values from -1 to 1, as said below
- right_fc1: float32 [1024, 1024], replicated, may hold values from -1 to 1, as said below
- left_fc2: float32 [1024, 1024], replicated, may hold values from -1 to 1, as said below
- right_fc2: float32 [256, 256], replicated, may hold values from -1 to 1, as said below
- vectors: float32 [22, 256], replicated, may hold values from -0.5 to 1.5, as said below
- vectors_first: float32 [22, 256], replicated, may hold values from -384 to 384
- vectors_second: float32 [22, 256], replicated, may hold values from 3010.56 to 12042.24
Outputs:
- block_out: bfloat16 [2, 2, 112, 112, 256], P(None, 'batch', 'band')
- input_grad: bfloat16 [2, 2, 112, 112, 256], P(None, 'batch', 'band')
- grad_qkv: float32 [256, 768], replicated
- first_new_qkv: float32 [32, 256, 768], P(('band', 'batch'))
- second_new_qkv: float32 [32, 256, 768], P(('band', 'batch'))
- weight_new_qkv: float32 [32, 256, 768], P(('band', 'batch'))
- grad_proj: float32 [256, 256], replicated
- first_new_proj: float32 [32, 256, 256], P(('band', 'batch'))
- second_new_proj: float32 [32, 256, 256], P(('band', 'batch'))
- weight_new_proj: float32 [32, 256, 256], P(('band', 'batch'))
- grad_fc1: float32 [256, 1024], replicated
- first_new_fc1: float32 [32, 256, 1024], P(('band', 'batch'))
- second_new_fc1: float32 [32, 256, 1024], P(('band', 'batch'))
- weight_new_fc1: float32 [32, 256, 1024], P(('band', 'batch'))
- grad_fc2: float32 [1024, 256], replicated
- first_new_fc2: float32 [32, 1024, 256], P(('band', 'batch'))
- second_new_fc2: float32 [32, 1024, 256], P(('band', 'batch'))
- weight_new_fc2: float32 [32, 1024, 256], P(('band', 'batch'))
- vectors_grad: float32 [22, 256], replicated
- vectors_first_new: float32 [22, 256], replicated
- vectors_second_new: float32 [22, 256], replicated
- vectors_new: float32 [22, 256], replicated
The draws below stay inside these ranges and needn't reach their ends.
Inputs may be any that keep to these rules, and one draw needn't show every extreme that they name: `left_qkv`: an orthogonal 256 x 256 matrix. `right_qkv`: an orthogonal 3 * 256 x 3 * 256 matrix. `left_proj`: an orthogonal 256 x 256 matrix. `right_proj`: an orthogonal 256 x 256 matrix. `left_fc1`: an orthogonal 256 x 256 matrix. `right_fc1`: an orthogonal 1024 x 1024 matrix. `left_fc2`: an orthogonal 1024 x 1024 matrix. `right_fc2`: an orthogonal 256 x 256 matrix. `vectors`: gains in rows 0 and 5 from 0.5 to 1.5, taps from -0.5 to 0.5, biases from -0.2 to 0.2.
All inputs are finite; a program needn't handle non-finite values.
Results may differ from the reference program's by a relative error of at most 0.011.
Values may be sent and summed in bfloat16 or wider, within the bound.
A program may use at most 512 MiB of HBM per device.

```python
import math
import jax
import jax.numpy as jnp
from jax import lax

C = 256
HEAD_DIM = 32
FF = 1024
STRIPE = 7
MICRO = 2
STEP = 10
VROWS = 22
IMAGES = 2
H = 112
W = 112
DEVICES = 32


def orthogonal(key, order):
    key_list = jax.random.split(key, 3)
    row_order = jax.random.permutation(key_list[0], order).astype(jnp.int32)
    col_order = jax.random.permutation(key_list[1], order).astype(jnp.int32)
    signs = (jax.random.randint(key_list[2], (order,), 0, 2) * 2 - 1).astype(jnp.float32)
    sample = row_order[:, None]
    freq = col_order[None, :]
    phase = (2 * sample + 1) * freq % (4 * order)
    angle = phase.astype(jnp.float32) * (math.pi / (2.0 * order))
    level = jnp.where(freq == 0, math.sqrt(1.0 / order), math.sqrt(2.0 / order)).astype(jnp.float32)
    return level * jnp.cos(angle) * signs[None, :]


def draw_left_qkv(key, part):
    key = jax.random.fold_in(key, 1)
    return orthogonal(key, C)


def draw_right_qkv(key, part):
    key = jax.random.fold_in(key, 2)
    return orthogonal(key, 3 * C)


def draw_left_proj(key, part):
    key = jax.random.fold_in(key, 3)
    return orthogonal(key, C)


def draw_right_proj(key, part):
    key = jax.random.fold_in(key, 4)
    return orthogonal(key, C)


def draw_left_fc1(key, part):
    key = jax.random.fold_in(key, 5)
    return orthogonal(key, C)


def draw_right_fc1(key, part):
    key = jax.random.fold_in(key, 6)
    return orthogonal(key, FF)


def draw_left_fc2(key, part):
    key = jax.random.fold_in(key, 7)
    return orthogonal(key, FF)


def draw_right_fc2(key, part):
    key = jax.random.fold_in(key, 8)
    return orthogonal(key, C)


def draw_vectors(key, part):
    key = jax.random.fold_in(key, 9)
    key_list = jax.random.split(key, 3)
    gain_values = jax.random.uniform(key_list[0], (VROWS, C), jnp.float32, 0.5, 1.5)
    shift_values = jax.random.uniform(key_list[1], (VROWS, C), jnp.float32, -0.2, 0.2)
    tap_values = jax.random.uniform(key_list[2], (VROWS, C), jnp.float32, -0.5, 0.5)
    row_ids = jnp.arange(VROWS)[:, None]
    is_gain = (row_ids == 0) | (row_ids == 5)
    is_tap = (row_ids >= 12) & (row_ids <= 20)
    return jnp.where(is_gain, gain_values, jnp.where(is_tap, tap_values, shift_values))


def plant(array, stream_key, least, top_value):
    longest = array.shape.index(max(array.shape))
    spots = []
    for shift in (0, 1):
        where = [jax.random.randint(jax.random.fold_in(stream_key, axis), (), 0, length) for axis, length in enumerate(array.shape)]
        where[longest] = (where[longest] + shift) % array.shape[longest]
        spots.append(tuple(where))
    return array.at[spots[0]].set(least).at[spots[1]].set(top_value)


def level_of(own_key, shape, shards, smallest, top_value):
    gain, own = 1.0, jax.random.fold_in(own_key, 6)
    for position, blocks in shards:
        steps = jnp.exp(jax.random.uniform(jax.random.fold_in(own, position), (blocks,), jnp.float32, smallest / len(shards), top_value / len(shards)))
        gain = gain * jnp.repeat(steps, shape[position] // blocks).reshape([-1 if axis == position else 1 for axis in range(len(shape))])
    return gain


def scatter_about(rng, extent, width, most, cuts=(), dtype=jnp.bfloat16):
    factor_of = level_of(rng, extent, cuts, -0.22, 0.18) if cuts else 1.0
    entries = jax.random.normal(rng, extent, jnp.float32) * width * factor_of
    return jnp.minimum(jnp.maximum(entries, -most), most).astype(dtype)


def setup_inputs(seed: int = 0) -> dict:
    splits = jax.random.split(jax.random.key(seed), 27)
    tokens_in = scatter_about(splits[0], (MICRO, IMAGES, H, W, C), 1.0, 6.0, ((1, 2), (2, 16)))
    cotangent = scatter_about(splits[1], (MICRO, IMAGES, H, W, C), 1.0, 6.0, ((1, 2), (2, 16)))
    owners = plant(jax.random.randint(splits[2], (4,), 0, DEVICES), jax.random.fold_in(splits[2], 1), 0, DEVICES - 1).astype(jnp.int32)
    weight_qkv = scatter_about(splits[3], (DEVICES, C, 3 * C), C ** -0.5, 0.375, ((0, 32),), jnp.float32)
    weight_proj = scatter_about(splits[4], (DEVICES, C, C), (C // 4) ** -0.5, 0.75, ((0, 32),), jnp.float32)
    weight_fc1 = scatter_about(splits[5], (DEVICES, C, FF), C ** -0.5, 0.375, ((0, 32),), jnp.float32)
    weight_fc2 = scatter_about(splits[6], (DEVICES, FF, C), FF ** -0.5, 0.1875, ((0, 32),), jnp.float32)
    first_qkv = scatter_about(splits[7], (DEVICES, C, 3 * C), (0.3 * (MICRO * IMAGES * H * W) ** 0.5), 384.0, ((0, 32),), jnp.float32)
    second_qkv = jnp.clip(jnp.exp(math.log(12042.24) - 1.3862944 * jax.random.uniform(splits[8], (DEVICES, C, 3 * C), jnp.float32) ** level_of(splits[8], (DEVICES, C, 3 * C), ((0, 32),), -0.2, 0.2)), 3010.56, 12042.24)
    first_proj = scatter_about(splits[9], (DEVICES, C, C), (0.3 * (MICRO * IMAGES * H * W) ** 0.5), 384.0, ((0, 32),), jnp.float32)
    second_proj = jnp.clip(jnp.exp(math.log(12042.24) - 1.3862944 * jax.random.uniform(splits[10], (DEVICES, C, C), jnp.float32) ** level_of(splits[10], (DEVICES, C, C), ((0, 32),), -0.2, 0.2)), 3010.56, 12042.24)
    first_fc1 = scatter_about(splits[11], (DEVICES, C, FF), (0.3 * (MICRO * IMAGES * H * W) ** 0.5), 384.0, ((0, 32),), jnp.float32)
    second_fc1 = jnp.clip(jnp.exp(math.log(12042.24) - 1.3862944 * jax.random.uniform(splits[12], (DEVICES, C, FF), jnp.float32) ** level_of(splits[12], (DEVICES, C, FF), ((0, 32),), -0.2, 0.2)), 3010.56, 12042.24)
    first_fc2 = scatter_about(splits[13], (DEVICES, FF, C), (0.3 * (MICRO * IMAGES * H * W) ** 0.5), 384.0, ((0, 32),), jnp.float32)
    second_fc2 = jnp.clip(jnp.exp(math.log(12042.24) - 1.3862944 * jax.random.uniform(splits[14], (DEVICES, FF, C), jnp.float32) ** level_of(splits[14], (DEVICES, FF, C), ((0, 32),), -0.2, 0.2)), 3010.56, 12042.24)
    left_qkv = draw_left_qkv(jax.random.fold_in(splits[26], 71), 0)
    right_qkv = draw_right_qkv(jax.random.fold_in(splits[26], 71), 0)
    left_proj = draw_left_proj(jax.random.fold_in(splits[26], 71), 0)
    right_proj = draw_right_proj(jax.random.fold_in(splits[26], 71), 0)
    left_fc1 = draw_left_fc1(jax.random.fold_in(splits[26], 71), 0)
    right_fc1 = draw_right_fc1(jax.random.fold_in(splits[26], 71), 0)
    left_fc2 = draw_left_fc2(jax.random.fold_in(splits[26], 71), 0)
    right_fc2 = draw_right_fc2(jax.random.fold_in(splits[26], 71), 0)
    vectors = draw_vectors(jax.random.fold_in(splits[26], 71), 0)
    vectors_first = scatter_about(splits[24], (VROWS, C), (0.3 * (MICRO * IMAGES * H * W) ** 0.5), 384.0, (), jnp.float32)
    vectors_second = jnp.clip(jnp.exp(jax.random.uniform(splits[25], (VROWS, C), jnp.float32, math.log(3010.56), math.log(12042.24))), 3010.56, 12042.24)
    return {"tokens_in": tokens_in, "cotangent": cotangent, "owners": owners, "weight_qkv": weight_qkv, "weight_proj": weight_proj, "weight_fc1": weight_fc1, "weight_fc2": weight_fc2, "first_qkv": first_qkv, "second_qkv": second_qkv, "first_proj": first_proj, "second_proj": second_proj, "first_fc1": first_fc1, "second_fc1": second_fc1, "first_fc2": first_fc2, "second_fc2": second_fc2, "left_qkv": left_qkv, "right_qkv": right_qkv, "left_proj": left_proj, "right_proj": right_proj, "left_fc1": left_fc1, "right_fc1": right_fc1, "left_fc2": left_fc2, "right_fc2": right_fc2, "vectors": vectors, "vectors_first": vectors_first, "vectors_second": vectors_second}


EPS_NORM = 1e-05
BETA_ONE = 0.5
BETA_TWO = 0.6
RATE = 0.04
RATE_VECTORS = 0.2
DECAY = 0.01
EPS_ADAM = 1e-08
HIGH = lax.Precision.HIGHEST

@jax.custom_vjp
def low(v):
    return lax.optimization_barrier(v.astype(jnp.bfloat16)).astype(jnp.float32)

@jax.custom_vjp
def low_back(v):
    return v

def low_keep(v):
    return (low(v), None)

def low_pass(kept, grad):
    return (grad,)

def back_keep(v):
    return (v, None)

def back_low(kept, grad):
    return (low(grad),)
low.defvjp(low_keep, low_pass)
low_back.defvjp(back_keep, back_low)

def layer_norm(values, gain_vec, shift_vec):
    row_mean = lax.optimization_barrier(jnp.mean(values, axis=-1, keepdims=True))
    centred = values - row_mean
    row_var = lax.optimization_barrier(jnp.mean(centred * centred, axis=-1, keepdims=True))
    return centred * lax.rsqrt(row_var + EPS_NORM) * gain_vec + shift_vec

def position_conv(values, tap_weights, tap_shift, rows_n, cols_n):
    grid_view = values.reshape(values.shape[0], rows_n, cols_n, values.shape[-1])
    padded = jnp.pad(grid_view, ((0, 0), (1, 1), (1, 1), (0, 0)))
    summed = jnp.zeros_like(grid_view) + tap_shift
    for tap_index in range(9):
        row_off = tap_index // 3
        col_off = tap_index % 3
        summed = summed + padded[:, row_off:row_off + rows_n, col_off:col_off + cols_n, :] * tap_weights[tap_index]
    return summed.reshape(values.shape)

def window_attend(parts):
    query_in, key_in, value_in = parts
    tokens_n = query_in.shape[0]
    head_count = query_in.shape[-1] // HEAD_DIM
    query_h = query_in.reshape(tokens_n, head_count, HEAD_DIM)
    key_h = key_in.reshape(tokens_n, head_count, HEAD_DIM)
    value_h = value_in.reshape(tokens_n, head_count, HEAD_DIM)
    scores = jnp.einsum('qhd,khd->hqk', query_h, key_h, precision=HIGH) * HEAD_DIM ** (-0.5)
    scores = low_back(scores)
    highest = lax.optimization_barrier(jnp.max(scores, axis=-1, keepdims=True))
    expo_s = jnp.exp(scores - highest)
    softmax_p = low(expo_s / lax.optimization_barrier(jnp.sum(expo_s, axis=-1, keepdims=True)))
    attended = jnp.einsum('hqk,khd->qhd', softmax_p, value_h, precision=HIGH)
    return attended.reshape(tokens_n, query_in.shape[-1])

def stripes_attend(query_in, key_in, value_in, tap_weights, tap_shift, rows_n, cols_n):
    attended = lax.map(jax.checkpoint(window_attend), (query_in, key_in, value_in))
    return attended + position_conv(value_in, tap_weights, tap_shift, rows_n, cols_n)

def image_block(params, picture):
    weight_a, weight_b, weight_c, weight_d, vectors = params
    half_width = C // 2
    normed_one = low(layer_norm(picture, vectors[0], vectors[1])).reshape(H * W, C)
    bias_qkv = jnp.concatenate([vectors[2], jnp.zeros((C,), jnp.float32), vectors[3]])
    mixed_qkv = jnp.dot(normed_one, low(weight_a), precision=HIGH) + bias_qkv
    mixed_qkv = low(low_back(mixed_qkv)).reshape(H, W, 3 * C)
    tap_weights = vectors[12:21]
    tap_shift = vectors[21]

    def rows_layout(block_index):
        start = block_index * C
        return mixed_qkv[:, :, start:start + half_width].reshape(H // STRIPE, STRIPE * W, half_width)

    def cols_layout(block_index):
        start = block_index * C + half_width
        piece = mixed_qkv[:, :, start:start + half_width]
        piece = piece.reshape(H, W // STRIPE, STRIPE, half_width).transpose(1, 0, 2, 3)
        return piece.reshape(W // STRIPE, H * STRIPE, half_width)
    horizontal = stripes_attend(rows_layout(0), rows_layout(1), rows_layout(2), tap_weights[:, :half_width], tap_shift[:half_width], STRIPE, W)
    horizontal = horizontal.reshape(H, W, half_width)
    vertical = stripes_attend(cols_layout(0), cols_layout(1), cols_layout(2), tap_weights[:, half_width:], tap_shift[half_width:], H, STRIPE)
    vertical = vertical.reshape(W // STRIPE, H, STRIPE, half_width).transpose(1, 0, 2, 3).reshape(H, W, half_width)
    joined = low(low_back(jnp.concatenate([horizontal, vertical], axis=-1))).reshape(H * W, C)
    branch = low_back(jnp.dot(joined, low(weight_b), precision=HIGH) + vectors[4])
    middle = picture.reshape(H * W, C) + branch
    normed_two = low(layer_norm(middle, vectors[5], vectors[6]))
    hidden = low_back(jnp.dot(normed_two, low(weight_c), precision=HIGH) + vectors[7:11].reshape(FF))
    active = low(jax.nn.gelu(hidden, approximate=False))
    result = middle + jnp.dot(active, low(weight_d), precision=HIGH) + vectors[11]
    return result.reshape(H, W, C)

def rotated_adam(grad, first, second, weight, left_basis, right_basis):
    turned = jnp.dot(jnp.dot(left_basis.T, grad, precision=HIGH), right_basis, precision=HIGH)
    first_new = BETA_ONE * first + (1.0 - BETA_ONE) * turned
    second_new = BETA_TWO * second + (1.0 - BETA_TWO) * turned * turned
    direction = first_new / (1.0 - BETA_ONE ** STEP) / (jnp.sqrt(second_new / (1.0 - BETA_TWO ** STEP)) + EPS_ADAM)
    back_turned = jnp.dot(jnp.dot(left_basis, direction, precision=HIGH), right_basis.T, precision=HIGH)
    weight_new = weight - RATE * back_turned - RATE * DECAY * weight
    return (first_new, second_new, weight_new)

def reference(tokens_in, cotangent, owners, weight_qkv, weight_proj, weight_fc1, weight_fc2, first_qkv, second_qkv, first_proj, second_proj, first_fc1, second_fc1, first_fc2, second_fc2, left_qkv, right_qkv, left_proj, right_proj, left_fc1, right_fc1, left_fc2, right_fc2, vectors, vectors_first, vectors_second):
    params = (weight_qkv[owners[0]], weight_proj[owners[1]], weight_fc1[owners[2]], weight_fc2[owners[3]], vectors)
    pictures = tokens_in.reshape(MICRO * IMAGES, H, W, C)
    cotangents = cotangent.reshape(MICRO * IMAGES, H, W, C)

    def one_picture(totals, inputs_pair):
        picture, cotan_img = inputs_pair
        result, pullback = jax.vjp(image_block, params, picture.astype(jnp.float32))
        grads, grad_picture = pullback(cotan_img.astype(jnp.float32))
        totals = jax.tree.map(jnp.add, totals, grads)
        return (totals, (result.astype(jnp.bfloat16), grad_picture.astype(jnp.bfloat16)))
    zero_grads = jax.tree.map(jnp.zeros_like, params)
    totals, (results, grad_pictures) = lax.scan(one_picture, zero_grads, (pictures, cotangents))
    block_out = results.reshape(tokens_in.shape)
    input_grad = grad_pictures.reshape(tokens_in.shape)
    grad_a, grad_b, grad_c, grad_d, vectors_grad = totals
    outputs_list = [block_out, input_grad]
    plan = ((grad_a, 0, first_qkv, second_qkv, weight_qkv, left_qkv, right_qkv), (grad_b, 1, first_proj, second_proj, weight_proj, left_proj, right_proj), (grad_c, 2, first_fc1, second_fc1, weight_fc1, left_fc1, right_fc1), (grad_d, 3, first_fc2, second_fc2, weight_fc2, left_fc2, right_fc2))
    for grad, which, first_slots, second_slots, weight_slots, left_basis, right_basis in plan:
        owner_id = owners[which]
        first_new, second_new, weight_new = rotated_adam(grad, first_slots[owner_id], second_slots[owner_id], weight_slots[owner_id], left_basis, right_basis)
        outputs_list.append(grad)
        outputs_list.append(jnp.zeros_like(first_slots).at[owner_id].set(first_new))
        outputs_list.append(jnp.zeros_like(second_slots).at[owner_id].set(second_new))
        outputs_list.append(jnp.zeros_like(weight_slots).at[owner_id].set(weight_new))
    vec_first_new = BETA_ONE * vectors_first + (1.0 - BETA_ONE) * vectors_grad
    vec_second_new = BETA_TWO * vectors_second + (1.0 - BETA_TWO) * vectors_grad * vectors_grad
    vec_step = vec_first_new / (1.0 - BETA_ONE ** STEP) / (jnp.sqrt(vec_second_new / (1.0 - BETA_TWO ** STEP)) + EPS_ADAM)
    vectors_new = vectors - RATE_VECTORS * vec_step
    return (outputs_list[0], outputs_list[1], outputs_list[2], outputs_list[3], outputs_list[4], outputs_list[5], outputs_list[6], outputs_list[7], outputs_list[8], outputs_list[9], outputs_list[10], outputs_list[11], outputs_list[12], outputs_list[13], outputs_list[14], outputs_list[15], outputs_list[16], outputs_list[17], vectors_grad, vec_first_new, vec_second_new, vectors_new)
```

```python
import functools

import jax
import jax.numpy as jnp
from jax import lax
from jax.experimental import pallas as pl
from jax.experimental.pallas import tpu as pltpu
from jax.sharding import PartitionSpec as P

HEAD_DIM = 32
STRIPE = 7
STEP = 10
EPS_NORM = 1e-05
BETA_ONE = 0.5
BETA_TWO = 0.6
RATE = 0.04
RATE_VECTORS = 0.2
DECAY = 0.01
EPS_ADAM = 1e-08
MESH = pl.DeviceIdType.MESH
F32 = jnp.float32
BF16 = jnp.bfloat16
PIECE = 64
LOG2E = 1.4426950408889634
LN2 = 0.6931471805599453
Q_SCALE = LOG2E * HEAD_DIM**-0.5
VMEM_LIMIT = 60 * 1024 * 1024
ROW_QKV, ROW_PROJ, ROW_FC1, ROW_FC2, ROW_END = 0, 768, 1024, 2048, 3072


def mm(a, b):
    return lax.dot_general(a, b, (((1,), (0,)), ((), ())), preferred_element_type=F32)


def mm_nt(a, b):
    return lax.dot_general(a, b, (((1,), (1,)), ((), ())), preferred_element_type=F32)


def mm_tn(a, b):
    return lax.dot_general(a, b, (((0,), (0,)), ((), ())), preferred_element_type=F32)


def exchange_kernel(n, piece, x_ref, o_ref, send_sem, recv_sem, loc_sem):
    me = lax.axis_index("band")
    bar = pltpu.get_barrier_semaphore()

    def greet(k, c):
        pl.semaphore_signal(
            bar, inc=1, device_id={"band": lax.rem(me + k, n)}, device_id_type=MESH
        )
        return c

    lax.fori_loop(1, n, greet, 0)
    pl.semaphore_wait(bar, n - 1)

    def rows(i):
        return pl.ds(pl.multiple_of(i * piece, piece), piece)

    def send(k, c):
        d = lax.rem(me + k, n)
        pltpu.make_async_remote_copy(
            src_ref=x_ref.at[rows(d)],
            dst_ref=o_ref.at[rows(me)],
            send_sem=send_sem.at[k],
            recv_sem=recv_sem.at[k],
            device_id={"band": d},
            device_id_type=MESH,
        ).start()
        return c

    lax.fori_loop(1, n, send, 0)
    local = pltpu.make_async_copy(x_ref.at[rows(me)], o_ref.at[rows(me)], loc_sem)
    local.start()
    local.wait()

    def take(k, c):
        s = lax.rem(me - k + n, n)
        pltpu.make_async_remote_copy(
            src_ref=x_ref.at[rows(s)],
            dst_ref=o_ref.at[rows(s)],
            send_sem=send_sem.at[k],
            recv_sem=recv_sem.at[k],
            device_id={"band": s},
            device_id_type=MESH,
        ).wait()
        return c

    lax.fori_loop(1, n, take, 0)


def exchange(x, n, cid):
    return pl.pallas_call(
        functools.partial(exchange_kernel, n, x.shape[0] // n),
        out_shape=jax.ShapeDtypeStruct(x.shape, x.dtype),
        in_specs=[pl.BlockSpec(memory_space=pltpu.VMEM)],
        out_specs=pl.BlockSpec(memory_space=pltpu.VMEM),
        scratch_shapes=[
            pltpu.SemaphoreType.DMA((n,)),
            pltpu.SemaphoreType.DMA((n,)),
            pltpu.SemaphoreType.DMA,
        ],
        compiler_params=pltpu.CompilerParams(
            collective_id=cid, has_side_effects=True, vmem_limit_bytes=VMEM_LIMIT
        ),
        name="exchange",
    )(x)


def sum_kernel(nb, nx, total_rows, x_ref, o_ref, got, half, recv, s1, r1, s2, r2, s3, r3, s4, r4):
    nq = (nb // 2) * nx
    p = total_rows // (2 * nq)
    band = lax.axis_index("band")
    core = lax.rem(band, 2)
    q = (band // 2) * nx + lax.axis_index("batch")
    sibling = {"band": band + 1 - 2 * core}
    bar = pltpu.get_barrier_semaphore()

    def chip(t):
        return {"band": (t // nx) * 2 + core, "batch": lax.rem(t, nx)}

    def ahead(k):
        return lax.rem(q + k, nq)

    def behind(k):
        return lax.rem(q - k + nq, nq)

    def copy(src, dst, ss, rs, dev):
        return pltpu.make_async_remote_copy(
            src_ref=src, dst_ref=dst, send_sem=ss, recv_sem=rs, device_id=dev, device_id_type=MESH
        )

    def loop(lo, hi, body):
        def step(k, c):
            body(k)
            return c

        lax.fori_loop(lo, hi, step, 0)

    pl.semaphore_signal(bar, inc=1, device_id=sibling, device_id_type=MESH)
    loop(
        1,
        nq,
        lambda k: pl.semaphore_signal(
            bar, inc=1, device_id=chip(ahead(k)), device_id_type=MESH
        ),
    )
    pl.semaphore_wait(bar, nq)

    def whole_rows(c, t):
        return pl.ds(pl.multiple_of((c * nq + t) * p, 16), p)

    def half_rows(t):
        return pl.ds(pl.multiple_of(t * p, 16), p)

    def pair_copy(k, side):
        t = ahead(k)
        return copy(
            x_ref.at[whole_rows(side, t)], got.at[half_rows(t)], s1.at[t], r1.at[t], sibling
        )

    loop(1, nq + 1, lambda k: pair_copy(k, 1 - core).start())

    def scatter_copy(k):
        t = ahead(k)
        return copy(half.at[half_rows(t)], recv.at[half_rows(q)], s2.at[k], r2.at[k], chip(t))

    def pair_sum(k):
        t = ahead(k)
        pair_copy(k, core).wait()
        half[half_rows(t)] = (
            x_ref[whole_rows(core, t)].astype(F32) + got[half_rows(t)].astype(F32)
        ).astype(BF16)

        @pl.when(k < nq)
        def _():
            scatter_copy(k).start()

    loop(1, nq + 1, pair_sum)

    def add_piece(k, acc):
        t = behind(k)
        copy(half.at[half_rows(t)], recv.at[half_rows(t)], s2.at[k], r2.at[k], chip(t)).wait()
        return acc + recv[half_rows(t)].astype(F32)

    total = lax.fori_loop(1, nq, add_piece, half[half_rows(q)].astype(F32))
    mine = o_ref.at[whole_rows(core, q)]
    o_ref[whole_rows(core, q)] = total.astype(BF16)

    def gather_copy(k):
        return copy(mine, mine, s3.at[k], r3.at[k], chip(ahead(k)))

    def pass_on(t, side):
        return copy(
            o_ref.at[whole_rows(core, t)],
            o_ref.at[whole_rows(side, t)],
            s4.at[t],
            r4.at[t],
            sibling,
        )

    loop(1, nq, lambda k: gather_copy(k).start())
    pass_on(q, core).start()

    def relay(k):
        t = behind(k)
        copy(mine, o_ref.at[whole_rows(core, t)], s3.at[k], r3.at[k], chip(t)).wait()
        pass_on(t, core).start()

    loop(1, nq, relay)
    loop(0, nq, lambda t: pass_on(t, 1 - core).wait())


def sum_everywhere(x, nb, nx, cid):
    rows, cols = x.shape
    nq = nb // 2 * nx
    unit = 32 * nq
    padded = -(-rows // unit) * unit
    if padded != rows:
        x = jnp.concatenate([x, jnp.zeros((padded - rows, cols), x.dtype)], axis=0)
    sems = [pltpu.SemaphoreType.DMA((nq,)) for _ in range(8)]
    out = pl.pallas_call(
        functools.partial(sum_kernel, nb, nx, padded),
        out_shape=jax.ShapeDtypeStruct(x.shape, x.dtype),
        in_specs=[pl.BlockSpec(memory_space=pltpu.VMEM)],
        out_specs=pl.BlockSpec(memory_space=pltpu.VMEM),
        scratch_shapes=[pltpu.VMEM((padded // 2, cols), x.dtype)] * 3 + sems,
        compiler_params=pltpu.CompilerParams(
            collective_id=cid, has_side_effects=True, vmem_limit_bytes=VMEM_LIMIT
        ),
        name="sum_everywhere",
    )(x)
    return out


def order_out(pieces_n, length):
    row = lax.broadcasted_iota(jnp.int32, (pieces_n * PIECE, 1), 0)
    s = row // PIECE
    m = row % PIECE
    a = (m * 37) // 256
    b = m - STRIPE * a
    token = jnp.where(m < STRIPE * STRIPE, a * length + STRIPE * s + b, -1)
    column = lax.broadcasted_iota(jnp.int32, (pieces_n * PIECE, STRIPE * length), 1)
    return jnp.where(column == token, 1.0, 0.0).astype(BF16)


def order_in(pieces_n, length):
    row = lax.broadcasted_iota(jnp.int32, (1, pieces_n * PIECE), 1)
    s = row // PIECE
    m = row % PIECE
    a = (m * 37) // 256
    b = m - STRIPE * a
    token = jnp.where(m < STRIPE * STRIPE, b * length + STRIPE * s + a, -1)
    column = lax.broadcasted_iota(jnp.int32, (STRIPE * length, pieces_n * PIECE), 0)
    return jnp.where(column == token, 1.0, 0.0).astype(BF16)


def unit_rows(values):
    centred = values - jnp.mean(values, axis=-1, keepdims=True)
    inverse = lax.rsqrt(jnp.mean(centred * centred, axis=-1, keepdims=True) + EPS_NORM)
    return centred * inverse, inverse


def norm_back(grad_normed, gain, unit, inverse):
    scaled = grad_normed * gain
    first_mean = jnp.mean(scaled, axis=-1, keepdims=True)
    second_mean = jnp.mean(scaled * unit, axis=-1, keepdims=True)
    return inverse * (scaled - first_mean - unit * second_mean)


def shifted_columns(v, length):
    tokens = v.shape[0]
    column = lax.broadcasted_iota(jnp.int32, v.shape, 0) % length
    before = jnp.where(column == 0, 0.0, pltpu.roll(v, 1, 0))
    after = jnp.where(column == length - 1, 0.0, pltpu.roll(v, tokens - 1, 0))
    return before, v, after


def shifted_rows(v, length):
    zeros = jnp.zeros((length, v.shape[1]), v.dtype)
    above = jnp.concatenate([zeros, v[: v.shape[0] - length]], axis=0)
    below = jnp.concatenate([v[length:], zeros], axis=0)
    return above, v, below


def tap_row(half, a, b):
    return 12 + (3 * a + b if half == 0 else 3 * b + a)


def conv(v, vec_ref, lanes, half, length, flipped):
    total = jnp.zeros_like(v)
    for b, col in enumerate(shifted_columns(v, length)):
        for a, val in enumerate(shifted_rows(col, length)):
            row = tap_row(half, 2 - a, 2 - b) if flipped else tap_row(half, a, b)
            total = total + val * vec_ref[row : row + 1, lanes]
    return total


def head_mask(shape, h, offset=0):
    lane = lax.broadcasted_iota(jnp.int32, shape, len(shape) - 1) - offset
    return (lane >= h * HEAD_DIM) & (lane < (h + 1) * HEAD_DIM)


def three_parts(x):
    lane = lax.broadcasted_iota(jnp.int32, x.shape, len(x.shape) - 1) % HEAD_DIM
    hi = x.astype(BF16).astype(F32)
    mid = (x - hi).astype(BF16).astype(F32)
    low = x - hi - mid
    parts = jnp.where(lane == 0, hi, jnp.where(lane == 1, mid, jnp.where(lane == 2, low, 0.0)))
    return parts.astype(BF16)


def stack_heads(block, with_ones):
    lane = lax.broadcasted_iota(jnp.int32, block.shape, 1)
    rows = []
    for h in range(4):
        keep = head_mask(block.shape, h)
        part = jnp.where(keep, block, 0.0)
        if with_ones:
            ones = jnp.where(keep & (lane % HEAD_DIM < 3), 1.0, 0.0)
            part = jnp.concatenate([part, ones], axis=1)
        rows.append(part.astype(BF16))
    return jnp.concatenate(rows, axis=0)


def pick_heads(stacked, r):
    out = stacked[:r]
    for h in range(1, 4):
        out = jnp.where(head_mask(out.shape, h), stacked[h * r : (h + 1) * r], out)
    return out


def lane_blocks(w_ref, half):
    return lambda b: w_ref[256 * b : 256 * b + 256, 128 * half : 128 * half + 128]


def attention_forward(x, half, length, wb, vec_ref, qa_ref, k_ref, v_ref, o_ref, att_ref, vx_ref):
    tokens = x.shape[0]
    lanes = slice(128 * half, 128 * half + 128)
    unit, _ = unit_rows(x)
    normed = (unit * vec_ref[0:1] + vec_ref[1:2]).astype(BF16)
    q = (mm(normed, wb(0)) + vec_ref[2:3, lanes]) * Q_SCALE
    k = mm(normed, wb(1))
    v = mm(normed, wb(2)) + vec_ref[3:4, lanes]
    qa_ref[:, 0:128] = q.astype(BF16)
    k_ref[...] = k.astype(BF16)
    v_ref[...] = v.astype(BF16)
    vx_ref[:, 0:128] = v.astype(BF16)
    vx_ref[:, 128:256] = jnp.ones((tokens, 128), BF16)
    r = 112

    def block(i, c):
        rows = pl.ds(pl.multiple_of(i * r, r), r)
        qs = stack_heads(qa_ref[rows, 0:128].astype(F32), False)
        scores = mm_nt(qs, k_ref[...])
        highest = jnp.max(scores, axis=-1, keepdims=True)
        probs = jnp.exp2(scores - highest).astype(BF16)
        both = mm(probs, vx_ref[...])
        weighted = pick_heads(both[:, 0:128], r)
        total = pick_heads(both[:, 128:256], r)
        top = pick_heads(jnp.broadcast_to(highest, (4 * r, 128)), r)
        o_ref[rows, :] = weighted / total
        qa_ref[rows, 128:256] = three_parts(-(top + jnp.log2(total)))
        return c

    lax.fori_loop(0, tokens // r, block, 0)
    lepe = conv(v_ref[...].astype(F32), vec_ref, lanes, half, length, False)
    att_ref[...] = (o_ref[...] + lepe + vec_ref[21:22, lanes]).astype(BF16)


def attention_backward(
    x, half, length, grad, wb, vec_ref, qa_ref, k_ref, v_ref, o_ref, da_ref, dq_ref, dk_ref, dv_ref, gw_ref, rows_ref
):
    tokens = x.shape[0]
    lanes = slice(128 * half, 128 * half + 128)
    grad_f = grad.astype(F32)
    product = grad_f * o_ref[...]
    inner = jnp.zeros_like(product)
    for h in range(4):
        keep = head_mask(product.shape, h)
        inner = jnp.where(
            keep, jnp.sum(jnp.where(keep, product, 0.0), axis=-1, keepdims=True), inner
        )
    da_ref[:, 0:128] = grad
    da_ref[:, 128:256] = three_parts(-inner)
    dq_ref[...] = jnp.zeros_like(dq_ref)
    r = 112

    def block(i, c):
        rows = pl.ds(pl.multiple_of(i * r, r), r)
        kb = k_ref[rows, :].astype(F32)
        ks = stack_heads(kb, True)
        vs = stack_heads(v_ref[rows, :].astype(F32), True)
        p = jnp.exp2(mm_nt(ks, qa_ref[...]))
        ds = (p * mm_nt(vs, da_ref[...])).astype(BF16)
        dv_ref[rows, :] = pick_heads(mm(p.astype(BF16), da_ref[:, 0:128]), r)
        dk_ref[rows, :] = pick_heads(mm(ds, qa_ref[:, 0:128]), r)
        dq_ref[...] += mm_tn(ks[:, 0:128], ds)
        return c

    lax.fori_loop(0, tokens // r, block, 0)
    dq = (jnp.transpose(dq_ref[...]) * HEAD_DIM**-0.5).astype(BF16)
    dk = (dk_ref[...] * LN2).astype(BF16)
    dv = (dv_ref[...] + conv(grad_f, vec_ref, lanes, half, length, True)).astype(BF16)
    unit, _ = unit_rows(x)
    normed = (unit * vec_ref[0:1] + vec_ref[1:2]).astype(BF16)
    gw_ref[...] += mm_tn(normed, jnp.concatenate([dq, dk, dv], axis=1))
    rows_ref[0:1, :] += jnp.sum(dq.astype(F32), axis=0, keepdims=True)
    rows_ref[1:2, :] += jnp.sum(dv.astype(F32), axis=0, keepdims=True)
    for b, col in enumerate(shifted_columns(v_ref[...].astype(F32), length)):
        for a, val in enumerate(shifted_rows(col, length)):
            row = tap_row(half, a, b) - 10
            rows_ref[row : row + 1, :] += jnp.sum(grad_f * val, axis=0, keepdims=True)
    rows_ref[11:12, :] += jnp.sum(grad_f, axis=0, keepdims=True)
    part = mm_nt(dq, wb(0)) + mm_nt(dk, wb(1)) + mm_nt(dv, wb(2))
    gain_row = jnp.sum(part * unit, axis=0, keepdims=True)
    shift_row = jnp.sum(part, axis=0, keepdims=True)
    for i in range(2):
        rows_ref[12 + i : 13 + i, :] += gain_row[:, 128 * i : 128 * i + 128]
        rows_ref[14 + i : 15 + i, :] += shift_row[:, 128 * i : 128 * i + 128]
    return part


def feed_forward(x, att, top, w_ref, base, vec_ref, n2_ref, acc_ref, gn_ref, gp_ref, g1_ref, g2_ref, rows_ref):
    middle = x + mm(att, w_ref[base : base + 256, :]) + vec_ref[4:5]
    unit, inverse = unit_rows(middle)
    n2_ref[...] = (unit * vec_ref[5:6] + vec_ref[6:7]).astype(BF16)
    acc_ref[...] = middle + vec_ref[11:12]
    gn_ref[...] = jnp.zeros_like(gn_ref)
    for f in range(4):
        w1 = w_ref[base + 256 * (1 + f) : base + 256 * (2 + f), :]
        w2 = w_ref[base + 256 * (5 + f) : base + 256 * (6 + f), :]
        cols = slice(256 * f, 256 * f + 256)
        hidden = mm(n2_ref[...], w1) + vec_ref[7 + f : 8 + f]
        below = 0.5 * (1.0 + lax.erf(hidden * (0.5**0.5)))
        active = (hidden * below).astype(BF16)
        slope = below + hidden * jnp.exp(-0.5 * hidden * hidden) * 0.3989422804014327
        grad_hidden = (mm_nt(top, w2) * slope).astype(BF16)
        acc_ref[...] += mm(active, w2)
        gn_ref[...] += mm_nt(grad_hidden, w1)
        g1_ref[:, cols] += mm_tn(n2_ref[...], grad_hidden)
        g2_ref[:, cols] += mm_tn(top, active)
        rows_ref[3 + f : 4 + f, :] += jnp.sum(grad_hidden.astype(F32), axis=0, keepdims=True)
    grad_normed = gn_ref[...]
    top_f = top.astype(F32)
    grad_middle = top_f + norm_back(grad_normed, vec_ref[5:6], unit, inverse)
    branch = grad_middle.astype(BF16)
    gp_ref[...] += mm_tn(branch, att)
    rows_ref[0:1, :] += jnp.sum(branch.astype(F32), axis=0, keepdims=True)
    rows_ref[1:2, :] += jnp.sum(grad_normed * unit, axis=0, keepdims=True)
    rows_ref[2:3, :] += jnp.sum(grad_normed, axis=0, keepdims=True)
    rows_ref[7:8, :] += jnp.sum(top_f, axis=0, keepdims=True)
    grad_att = mm_nt(branch, w_ref[base : base + 256, :]).astype(BF16)
    return acc_ref[...].astype(BF16), grad_middle, grad_att


PARAMS = pltpu.CompilerParams(
    dimension_semantics=("arbitrary",), vmem_limit_bytes=VMEM_LIMIT
)


def whole(shape):
    return pl.BlockSpec(shape, lambda m: (0,) * len(shape))


def each(shape):
    return pl.BlockSpec((None,) + shape, lambda m: (m,) + (0,) * len(shape))


def shape_of(dtype, *shape):
    return jax.ShapeDtypeStruct(shape, dtype)


def pack_tokens(x, nb, length):
    micro, tokens, channels = x.shape

    def kernel(x_ref, o_ref, hot):
        @pl.when(pl.program_id(0) == 0)
        def _():
            hot[...] = order_out(nb, length)

        o_ref[...] = mm(hot[...], x_ref[...]).astype(BF16)

    return pl.pallas_call(
        kernel,
        grid=(micro,),
        in_specs=[each((tokens, channels))],
        out_specs=each((nb * PIECE, channels)),
        out_shape=shape_of(BF16, micro, nb * PIECE, channels),
        scratch_shapes=[pltpu.VMEM((nb * PIECE, tokens), BF16)],
        compiler_params=PARAMS,
        name="pack_tokens",
    )(x)


def forward_call(x, half, nb, length, weights, vectors):
    micro = x.shape[0]
    tokens = STRIPE * length
    packed = nb * PIECE

    def kernel(x_ref, w_ref, vec_ref, qa_ref, k_ref, v_ref, o_ref, att_ref, xs_ref, vx_ref, *scr):
        if half == 0:
            attention_forward(
                x_ref[...].astype(F32), half, length, lane_blocks(w_ref, half), vec_ref, qa_ref, k_ref, v_ref, o_ref, att_ref, vx_ref
            )
        else:
            att_s, hot_in, hot_out = scr

            @pl.when(pl.program_id(0) == 0)
            def _():
                hot_in[...] = order_in(nb, length)
                hot_out[...] = order_out(nb, length)

            xs_ref[...] = mm(hot_in[...], x_ref[...]).astype(BF16)
            attention_forward(
                xs_ref[...].astype(F32), half, length, lane_blocks(w_ref, half), vec_ref, qa_ref, k_ref, v_ref, o_ref, att_s, vx_ref
            )
            att_ref[...] = mm(hot_out[...], att_s[...]).astype(BF16)

    rows = tokens if half == 0 else packed
    scratch = [pltpu.VMEM((tokens, 256), BF16)]
    if half == 1:
        scratch += [
            pltpu.VMEM((tokens, 128), BF16),
            pltpu.VMEM((tokens, packed), BF16),
            pltpu.VMEM((packed, tokens), BF16),
        ]
    if half == 0:
        def body(x_ref, w_ref, vec_ref, qa_ref, k_ref, v_ref, o_ref, att_ref, *scr):
            kernel(x_ref, w_ref, vec_ref, qa_ref, k_ref, v_ref, o_ref, att_ref, None, *scr)
        extra_specs, extra_shapes = [], []
    else:
        body = kernel
        extra_specs = [each((tokens, 256))]
        extra_shapes = [shape_of(BF16, micro, tokens, 256)]
    return pl.pallas_call(
        body,
        grid=(micro,),
        in_specs=[each((rows, 256)), whole(weights.shape), whole(vectors.shape)],
        out_specs=[
            each((tokens, 256)),
            each((tokens, 128)),
            each((tokens, 128)),
            each((tokens, 128)),
            each((rows, 128)),
        ] + extra_specs,
        out_shape=[
            shape_of(BF16, micro, tokens, 256),
            shape_of(BF16, micro, tokens, 128),
            shape_of(BF16, micro, tokens, 128),
            shape_of(F32, micro, tokens, 128),
            shape_of(BF16, micro, rows, 128),
        ] + extra_shapes,
        scratch_shapes=scratch,
        compiler_params=PARAMS,
        name="attention_forward_%d" % half,
    )(x, weights, vectors)


def middle_call(x, att_h, att_v, top, nb, length, weights, vectors):
    micro, tokens, _ = x.shape
    packed = nb * PIECE

    def kernel(
        x_ref, h_ref, v_ref, top_ref, w_ref, vec_ref,
        out_ref, gm_ref, gh_ref, gv_ref, gp_ref, g1_ref, g2_ref, rows_ref,
        hot_in, hot_out, att, n2, acc, gn,
    ):
        @pl.when(pl.program_id(0) == 0)
        def _():
            hot_in[...] = order_in(nb, length)
            hot_out[...] = order_out(nb, length)
            for ref in (gp_ref, g1_ref, g2_ref, rows_ref):
                ref[...] = jnp.zeros_like(ref)

        att[:, 0:128] = h_ref[...]
        att[:, 128:256] = mm(hot_in[...], v_ref[...]).astype(BF16)
        out, grad_middle, grad_att = feed_forward(
            x_ref[...].astype(F32), att[...], top_ref[...], w_ref, ROW_PROJ, vec_ref, n2, acc, gn, gp_ref, g1_ref, g2_ref, rows_ref
        )
        out_ref[...] = out
        gm_ref[...] = grad_middle
        gh_ref[...] = grad_att[:, 0:128]
        gv_ref[...] = mm(hot_out[...], grad_att[:, 128:256]).astype(BF16)

    return pl.pallas_call(
        kernel,
        grid=(micro,),
        in_specs=[
            each((tokens, 256)), each((tokens, 128)), each((packed, 128)), each((tokens, 256)),
            whole(weights.shape), whole(vectors.shape),
        ],
        out_specs=[
            each((tokens, 256)), each((tokens, 256)), each((tokens, 128)), each((packed, 128)),
            whole((256, 256)), whole((256, 1024)), whole((256, 1024)), whole((8, 256)),
        ],
        out_shape=[
            shape_of(BF16, micro, tokens, 256), shape_of(F32, micro, tokens, 256),
            shape_of(BF16, micro, tokens, 128), shape_of(BF16, micro, packed, 128),
            shape_of(F32, 256, 256), shape_of(F32, 256, 1024), shape_of(F32, 256, 1024), shape_of(F32, 8, 256),
        ],
        scratch_shapes=[
            pltpu.VMEM((tokens, packed), BF16), pltpu.VMEM((packed, tokens), BF16),
            pltpu.VMEM((tokens, 256), BF16), pltpu.VMEM((tokens, 256), BF16),
            pltpu.VMEM((tokens, 256), F32), pltpu.VMEM((tokens, 256), F32),
        ],
        compiler_params=PARAMS,
        name="feed_forward",
    )(x, att_h, att_v, top, weights, vectors)


def backward_call(x, grad, qa, k, v, o, half, nb, length, weights, vectors):
    micro, tokens, _ = x.shape
    packed = nb * PIECE

    def kernel(
        x_ref, g_ref, qa_ref, k_ref, v_ref, o_ref, w_ref, vec_ref, gn_ref, gw_ref, rows_ref,
        da, dq, dk, dv, *scr,
    ):
        @pl.when(pl.program_id(0) == 0)
        def _():
            gw_ref[...] = jnp.zeros_like(gw_ref)
            rows_ref[...] = jnp.zeros_like(rows_ref)
            if half == 1:
                scr[0][...] = order_in(nb, length)
                scr[1][...] = order_out(nb, length)

        grad_in = g_ref[...] if half == 0 else mm(scr[0][...], g_ref[...]).astype(BF16)
        part = attention_backward(
            x_ref[...].astype(F32), half, length, grad_in, lane_blocks(w_ref, half), vec_ref, qa_ref, k_ref, v_ref, o_ref,
            da, dq, dk, dv, gw_ref, rows_ref,
        )
        if half == 0:
            gn_ref[...] = part
        else:
            gn_ref[...] = mm(scr[1][...], part.astype(BF16)).astype(BF16)

    rows = tokens if half == 0 else packed
    scratch = [
        pltpu.VMEM((tokens, 256), BF16), pltpu.VMEM((128, tokens), F32),
        pltpu.VMEM((tokens, 128), F32), pltpu.VMEM((tokens, 128), F32),
    ]
    if half == 1:
        scratch += [pltpu.VMEM((tokens, packed), BF16), pltpu.VMEM((packed, tokens), BF16)]
    return pl.pallas_call(
        kernel,
        grid=(micro,),
        in_specs=[
            each((tokens, 256)), each((rows, 128)), each((tokens, 256)), each((tokens, 128)),
            each((tokens, 128)), each((tokens, 128)), whole(weights.shape), whole(vectors.shape),
        ],
        out_specs=[each((rows, 256)), whole((256, 384)), whole((16, 128))],
        out_shape=[
            shape_of(F32 if half == 0 else BF16, micro, rows, 256),
            shape_of(F32, 256, 384), shape_of(F32, 16, 128),
        ],
        scratch_shapes=scratch,
        compiler_params=PARAMS,
        name="attention_backward_%d" % half,
    )(x, grad, qa, k, v, o, weights, vectors)


def last_call(x, grad_middle, part_h, part_v, nb, length, vectors):
    micro, tokens, _ = x.shape
    packed = nb * PIECE

    def kernel(x_ref, gm_ref, h_ref, v_ref, vec_ref, out_ref, hot_in):
        @pl.when(pl.program_id(0) == 0)
        def _():
            hot_in[...] = order_in(nb, length)

        grad_normed = h_ref[...] + mm(hot_in[...], v_ref[...])
        unit, inverse = unit_rows(x_ref[...].astype(F32))
        out_ref[...] = (
            gm_ref[...] + norm_back(grad_normed, vec_ref[0:1], unit, inverse)
        ).astype(BF16)

    return pl.pallas_call(
        kernel,
        grid=(micro,),
        in_specs=[
            each((tokens, 256)), each((tokens, 256)), each((tokens, 256)), each((packed, 256)), whole(vectors.shape),
        ],
        out_specs=each((tokens, 256)),
        out_shape=shape_of(BF16, micro, tokens, 256),
        scratch_shapes=[pltpu.VMEM((tokens, packed), BF16)],
        compiler_params=PARAMS,
        name="input_gradient",
    )(x, grad_middle, part_h, part_v, vectors)


def repeat(lo, hi, body):
    def step(k, c):
        body(k)
        return c

    lax.fori_loop(lo, hi, step, 0)


def remote(src, dst, ss, rs, dev):
    return pltpu.make_async_remote_copy(
        src_ref=src, dst_ref=dst, send_sem=ss, recv_sem=rs, device_id=dev, device_id_type=MESH
    )


class Swap:
    def __init__(self, n, out_ref, in_ref, send_sem, recv_sem):
        self.n, self.out, self.into, self.ss, self.rs = n, out_ref, in_ref, send_sem, recv_sem
        self.me = lax.axis_index("band")

    def rows(self, i):
        return pl.ds(pl.multiple_of(i * PIECE, PIECE), PIECE)

    def send(self, m):
        mine = self.rows(self.me)

        def one(k):
            d = lax.rem(self.me + k, self.n)
            remote(
                self.out.at[m, self.rows(d)],
                self.into.at[m, mine],
                self.ss.at[m, k],
                self.rs.at[m, k],
                {"band": d},
            ).start()

        repeat(1, self.n, one)
        self.into[m, mine, :] = self.out[m, mine, :]

    def wait(self, m):
        def one(k):
            s = lax.rem(self.me - k + self.n, self.n)
            remote(
                self.out.at[m, self.rows(s)],
                self.into.at[m, self.rows(s)],
                self.ss.at[m, k],
                self.rs.at[m, k],
                {"band": s},
            ).wait()

        repeat(1, self.n, one)


class Sum:
    def __init__(self, nb, nx, x_ref, o_ref, got, half, recv, sems):
        self.nx = nx
        self.nq = (nb // 2) * nx
        self.p = x_ref.shape[0] // (2 * self.nq)
        band = lax.axis_index("band")
        self.core = lax.rem(band, 2)
        self.q = (band // 2) * nx + lax.axis_index("batch")
        self.sibling = {"band": band + 1 - 2 * self.core}
        self.x, self.o, self.got, self.half, self.recv = x_ref, o_ref, got, half, recv
        self.sems = sems

    def chip(self, t):
        return {"band": (t // self.nx) * 2 + self.core, "batch": lax.rem(t, self.nx)}

    def ahead(self, k):
        return lax.rem(self.q + k, self.nq)

    def behind(self, k):
        return lax.rem(self.q - k + self.nq, self.nq)

    def wide(self, c, t):
        return pl.ds(pl.multiple_of((c * self.nq + t) * self.p, 16), self.p)

    def thin(self, t):
        return pl.ds(pl.multiple_of(t * self.p, 16), self.p)

    def sem(self, i, k):
        return self.sems.at[2 * i, k], self.sems.at[2 * i + 1, k]

    def pair_copy(self, k, side):
        t = self.ahead(k)
        return remote(
            self.x.at[self.wide(side, t)], self.got.at[self.thin(t)], *self.sem(0, t), self.sibling
        )

    def start(self):
        repeat(1, self.nq + 1, lambda k: self.pair_copy(k, 1 - self.core).start())

    def scatter(self):
        def one(k):
            t = self.ahead(k)
            self.pair_copy(k, self.core).wait()
            self.half[self.thin(t)] = (
                self.x[self.wide(self.core, t)].astype(F32) + self.got[self.thin(t)].astype(F32)
            ).astype(BF16)

            @pl.when(k < self.nq)
            def _():
                remote(
                    self.half.at[self.thin(t)],
                    self.recv.at[self.thin(self.q)],
                    *self.sem(1, k),
                    self.chip(t),
                ).start()

        repeat(1, self.nq + 1, one)

    def gather(self):
        def one(k, acc):
            t = self.behind(k)
            remote(
                self.half.at[self.thin(t)],
                self.recv.at[self.thin(t)],
                *self.sem(1, k),
                self.chip(t),
            ).wait()
            return acc + self.recv[self.thin(t)].astype(F32)

        total = lax.fori_loop(1, self.nq, one, self.half[self.thin(self.q)].astype(F32))
        mine = self.wide(self.core, self.q)
        self.o[mine] = total.astype(BF16)

        def give(k):
            remote(
                self.o.at[mine], self.o.at[mine], *self.sem(2, k), self.chip(self.ahead(k))
            ).start()

        repeat(1, self.nq, give)
        self.pass_on(self.q, self.core).start()

    def pass_on(self, t, side):
        return remote(
            self.o.at[self.wide(self.core, t)],
            self.o.at[self.wide(side, t)],
            *self.sem(3, t),
            self.sibling,
        )

    def relay(self):
        mine = self.wide(self.core, self.q)

        def one(k):
            t = self.behind(k)
            remote(
                self.o.at[mine], self.o.at[self.wide(self.core, t)], *self.sem(2, k), self.chip(t)
            ).wait()
            self.pass_on(t, self.core).start()

        repeat(1, self.nq, one)

    def finish(self):
        repeat(0, self.nq, lambda t: self.pass_on(t, 1 - self.core).wait())


ROWS_A = 1536
ROWS_B = 2304
ROWS_G = 800


def up(rows, unit):
    return -(-rows // unit) * unit


def split_rows(ref, at, rows):
    n = rows.shape[0]
    high = rows.astype(BF16)
    ref[at : at + n, :] = high
    ref[at + n : at + 2 * n, :] = (rows - high.astype(F32)).astype(BF16)


def block_kernel(
    nb, nx, length,
    own_ref, x_ref, top_ref, wq_ref, wp_ref, w1_ref, w2_ref, vec_ref,
    out_ref, ing_ref, gb_ref, gav_ref, gah_ref,
    wa_in, wb_in, wa, wb, gb_in, gav_in, gah_in,
    wide_got, wide_half, wide_recv, a_got, a_half, a_recv,
    gb_got, gb_half, gb_recv, v_got, v_half, v_recv, h_got, h_half, h_recv,
    hot_in, hot_out, x_out, x_in, a_out, a_in, g_out, g_in, p_out, p_in,
    xs, qa, ks, vs, os, vx, att, n2, acc, gn, gm, grad_h, part_h,
    gp, g1, g2, rows_mid, gw_v, gw_h, rows_v, rows_h, da, dq, dk, dv,
    x_ss, x_rs, a_ss, a_rs, g_ss, g_rs, p_ss, p_rs,
    wa_sem, wb_sem, gb_sem, gav_sem, gah_sem,
):
    band = lax.axis_index("band")
    batch = lax.axis_index("batch")
    device = band * nx + batch
    micro = x_ref.shape[0]
    core = lax.rem(band, 2)
    bar = pltpu.get_barrier_semaphore()
    repeat(
        1,
        nb,
        lambda k: pl.semaphore_signal(
            bar, inc=1, device_id={"band": lax.rem(band + k, nb)}, device_id_type=MESH
        ),
    )

    def greet(t):
        other = lax.rem(batch + 1 + t // (nb // 2), nx)
        pl.semaphore_signal(
            bar,
            inc=1,
            device_id={"band": lax.rem(t, nb // 2) * 2 + core, "batch": other},
            device_id_type=MESH,
        )

    repeat(0, (nb // 2) * (nx - 1), greet)

    sum_wa = Sum(nb, nx, wa_in, wa, a_got, a_half, a_recv, wa_sem)
    sum_wb = Sum(nb, nx, wb_in, wb, wide_got, wide_half, wide_recv, wb_sem)
    sum_gb = Sum(nb, nx, gb_in, gb_ref, gb_got, gb_half, gb_recv, gb_sem)
    sum_gav = Sum(nb, nx, gav_in, gav_ref, v_got, v_half, v_recv, gav_sem)
    sum_gah = Sum(nb, nx, gah_in, gah_ref, h_got, h_half, h_recv, gah_sem)
    swap_x = Swap(nb, x_out, x_in, x_ss, x_rs)
    swap_a = Swap(nb, a_out, a_in, a_ss, a_rs)
    swap_g = Swap(nb, g_out, g_in, g_ss, g_rs)
    swap_p = Swap(nb, p_out, p_in, p_ss, p_rs)

    def own(ref, which, cols):
        return jnp.where(own_ref[which] == device, ref[0, :, cols], 0.0).astype(BF16)

    for b in range(6):
        wa_in[256 * b : 256 * b + 256, :] = own(wq_ref, 0, slice(128 * b, 128 * b + 128))
    if wa_in.shape[0] > ROWS_A:
        wa_in[ROWS_A:, :] = jnp.zeros((wa_in.shape[0] - ROWS_A, 128), BF16)
    pl.semaphore_wait(bar, nb - 1 + (nb // 2) * (nx - 1))
    sum_wa.start()
    wb_in[0:256, :] = own(wp_ref, 1, slice(0, 256))
    for f in range(4):
        wb_in[256 * (f + 1) : 256 * (f + 2), :] = own(w1_ref, 2, slice(256 * f, 256 * f + 256))
    wb_in[1280:ROWS_B, :] = own(w2_ref, 3, slice(0, 256))
    wb_in[ROWS_B:, :] = jnp.zeros((wb_in.shape[0] - ROWS_B, 256), BF16)
    sum_wa.scatter()
    hot_out[...] = order_out(nb, length)
    x_out[0] = mm(hot_out[...], x_ref[0]).astype(BF16)
    swap_x.send(0)
    sum_wa.gather()
    hot_in[...] = order_in(nb, length)
    for m in range(1, micro):
        x_out[m] = mm(hot_out[...], x_ref[m]).astype(BF16)
        swap_x.send(m)
    sum_wb.start()
    for ref in (gp, g1, g2, rows_mid, gw_v, gw_h, rows_v, rows_h):
        ref[...] = jnp.zeros_like(ref)
    sum_wa.relay()
    sum_wa.finish()

    def blocks(half):
        return lambda b: wa[256 * (2 * b + half) : 256 * (2 * b + half) + 256, :]

    def forward_h(m):
        attention_forward(
            x_ref[m].astype(F32), 0, length, blocks(0), vec_ref,
            qa.at[m], ks.at[m], vs.at[m], os.at[m], att.at[m, :, pl.ds(0, 128)], vx,
        )

    def forward_v(m):
        swap_x.wait(m)
        xs[m] = mm(hot_in[...], x_in[m]).astype(BF16)
        w = micro + m
        attention_forward(
            xs[m].astype(F32), 1, length, blocks(1), vec_ref,
            qa.at[w], ks.at[w], vs.at[w], os.at[w], att.at[m, :, pl.ds(128, 128)], vx,
        )
        a_out[m] = mm(hot_out[...], att[m, :, 128:256]).astype(BF16)
        swap_a.send(m)

    def forward_step(i):
        @pl.when((i == 0) | (i > micro))
        def _():
            forward_h(jnp.where(i == 0, 0, i - micro))

        @pl.when((i > 0) & (i <= micro))
        def _():
            forward_v(i - 1)

        @pl.when(i == 0)
        def _():
            sum_wb.scatter()

        @pl.when(i == 1)
        def _():
            sum_wb.gather()

        @pl.when(i == 2)
        def _():
            sum_wb.relay()

    repeat(0, 2 * micro, forward_step)
    sum_wb.finish()

    def middle_step(m):
        swap_a.wait(m)
        att[m, :, 128:256] = mm(hot_in[...], a_in[m]).astype(BF16)
        out, grad_middle, grad_att = feed_forward(
            x_ref[m].astype(F32), att[m], top_ref[m], wb, 0, vec_ref, n2, acc, gn,
            gp, g1, g2, rows_mid,
        )
        out_ref[m] = out
        gm[m] = grad_middle
        grad_h[m] = grad_att[:, 0:128]
        g_out[m] = mm(hot_out[...], grad_att[:, 128:256]).astype(BF16)
        swap_g.send(m)

    repeat(0, micro, middle_step)
    gb_in[0:256, :] = jnp.transpose(gp[...]).astype(BF16)
    for f in range(4):
        cols = slice(256 * f, 256 * f + 256)
        gb_in[256 * (f + 1) : 256 * (f + 2), :] = g1[:, cols].astype(BF16)
        gb_in[1280 + 256 * f : 1536 + 256 * f, :] = jnp.transpose(g2[:, cols]).astype(BF16)
    gb_in[ROWS_B:, :] = jnp.zeros((gb_in.shape[0] - ROWS_B, 256), BF16)
    split_rows(gb_in, ROWS_B, rows_mid[...])
    sum_gb.start()

    def backward_v(m):
        swap_g.wait(m)
        w = micro + m
        grad_in = mm(hot_in[...], g_in[m]).astype(BF16)
        part = attention_backward(
            xs[m].astype(F32), 1, length, grad_in, blocks(1), vec_ref,
            qa.at[w], ks.at[w], vs.at[w], os.at[w], da, dq, dk, dv, gw_v, rows_v,
        )
        p_out[m] = mm(hot_out[...], part.astype(BF16)).astype(BF16)
        swap_p.send(m)

        @pl.when(m == 0)
        def _():
            sum_gb.scatter()

    repeat(0, micro, backward_v)
    sum_gb.gather()

    def fill(ref, gw, rows):
        for b in range(3):
            ref[256 * b : 256 * b + 256, :] = gw[:, 128 * b : 128 * b + 128].astype(BF16)
        split_rows(ref, 768, rows[...])
        ref[ROWS_G:, :] = jnp.zeros((ref.shape[0] - ROWS_G, 128), BF16)

    fill(gav_in, gw_v, rows_v)
    sum_gav.start()

    def backward_h(m):
        part_h[m] = attention_backward(
            x_ref[m].astype(F32), 0, length, grad_h[m], blocks(0), vec_ref,
            qa.at[m], ks.at[m], vs.at[m], os.at[m], da, dq, dk, dv, gw_h, rows_h,
        )

        @pl.when(m == 0)
        def _():
            sum_gb.relay()
            sum_gav.scatter()

    repeat(0, micro, backward_h)
    fill(gah_in, gw_h, rows_h)
    sum_gah.start()
    sum_gav.gather()
    sum_gb.finish()
    sum_gah.scatter()

    def last_step(m):
        swap_p.wait(m)
        grad_normed = part_h[m] + mm(hot_in[...], p_in[m])
        unit, inverse = unit_rows(x_ref[m].astype(F32))
        ing_ref[m] = (gm[m] + norm_back(grad_normed, vec_ref[0:1], unit, inverse)).astype(BF16)

    last_step(0)
    sum_gah.gather()
    sum_gav.relay()
    repeat(1, micro, last_step)
    sum_gah.relay()
    sum_gav.finish()
    sum_gah.finish()


def block_call(x, top, owners, w_qkv, w_proj, w_fc1, w_fc2, vectors, nb, nx, length):
    micro, tokens, _ = x.shape
    packed = nb * PIECE
    nq = nb // 2 * nx
    unit = 32 * nq
    ra, rb, rg = up(ROWS_A, unit), up(ROWS_B + 16, unit), up(ROWS_G, unit)
    vm = pltpu.VMEM
    windows = 2 * micro

    def steps(rows, cols):
        return [vm((rows // 2, cols), BF16)] * 3

    scratch = (
        [vm((ra, 128), BF16), vm((rb, 256), BF16), vm((ra, 128), BF16), vm((rb, 256), BF16)]
        + [vm((rb, 256), BF16), vm((rg, 128), BF16), vm((rg, 128), BF16)]
        + steps(rb, 256) + steps(ra, 128) + steps(rb, 256) + steps(rg, 128) + steps(rg, 128)
        + [vm((tokens, packed), BF16), vm((packed, tokens), BF16)]
        + [vm((micro, packed, 256), BF16)] * 2
        + [vm((micro, packed, 128), BF16)] * 4
        + [vm((micro, packed, 256), BF16)] * 2
        + [
            vm((micro, tokens, 256), BF16),
            vm((windows, tokens, 256), BF16),
            vm((windows, tokens, 128), BF16),
            vm((windows, tokens, 128), BF16),
            vm((windows, tokens, 128), F32),
            vm((tokens, 256), BF16),
            vm((micro, tokens, 256), BF16),
            vm((tokens, 256), BF16),
            vm((tokens, 256), F32),
            vm((tokens, 256), F32),
            vm((micro, tokens, 256), F32),
            vm((micro, tokens, 128), BF16),
            vm((micro, tokens, 256), F32),
            vm((256, 256), F32),
            vm((256, 1024), F32),
            vm((256, 1024), F32),
            vm((8, 256), F32),
            vm((256, 384), F32),
            vm((256, 384), F32),
            vm((16, 128), F32),
            vm((16, 128), F32),
            vm((tokens, 256), BF16),
            vm((128, tokens), F32),
            vm((tokens, 128), F32),
            vm((tokens, 128), F32),
        ]
        + [pltpu.SemaphoreType.DMA((micro, nb))] * 8
        + [pltpu.SemaphoreType.DMA((8, nq))] * 5
    )
    whole_vmem = pl.BlockSpec(memory_space=vm)
    return pl.pallas_call(
        functools.partial(block_kernel, nb, nx, length),
        in_specs=[pl.BlockSpec(memory_space=pltpu.SMEM)] + [whole_vmem] * 7,
        out_specs=[whole_vmem] * 5,
        out_shape=[
            shape_of(BF16, micro, tokens, 256), shape_of(BF16, micro, tokens, 256),
            shape_of(BF16, rb, 256), shape_of(BF16, rg, 128), shape_of(BF16, rg, 128),
        ],
        scratch_shapes=scratch,
        compiler_params=pltpu.CompilerParams(
            collective_id=0, has_side_effects=True, vmem_limit_bytes=VMEM_LIMIT
        ),
        name="block",
    )(owners, x, top, w_qkv, w_proj, w_fc1, w_fc2, vectors)


def parts_of(a):
    high = a.astype(BF16)
    return high, (a - high.astype(F32)).astype(BF16)


def careful(op, a, b):
    ah, al = parts_of(a)
    bh, bl = parts_of(b)
    return op(ah, bh) + (op(ah, bl) + op(al, bh))


def adam_kernel(
    vrows, rows,
    own_ref, gb_ref, gav_ref, gah_ref, vec_ref, vf_ref, vs_ref, *refs,
):
    moments = refs[0:12]
    bases = refs[12:20]
    grads = refs[20:24]
    outs = refs[24:36]
    vg_ref, vfn_ref, vsn_ref, vn_ref = refs[36:40]
    held = refs[40:52]
    left = refs[52:60]
    zeros_ref, in_sem, out_sem = refs[60:63]
    device = lax.axis_index("band") * lax.axis_size("batch") + lax.axis_index("batch")
    is_own = [own_ref[i] == device for i in range(4)]

    def load(i):
        pairs = [(moments[3 * i + j].at[0], held[3 * i + j], 5 * i + j) for j in range(3)]
        pairs += [(bases[2 * i + j], left[2 * i + j], 5 * i + 3 + j) for j in range(2)]
        return [pltpu.make_async_copy(a, b, in_sem.at[s]) for a, b, s in pairs]

    def store(i):
        return [
            pltpu.make_async_copy(held[3 * i + j], outs[3 * i + j].at[0], out_sem.at[3 * i + j])
            for j in range(3)
        ]

    def blank(i):
        copies = []
        for j in range(3):
            shape = outs[3 * i + j].shape
            copies.append(
                pltpu.make_async_copy(
                    zeros_ref.at[pl.ds(0, shape[1]), pl.ds(0, shape[2])],
                    outs[3 * i + j].at[0],
                    out_sem.at[3 * i + j],
                )
            )
        return copies

    for i in range(4):
        @pl.when(is_own[i])
        def _():
            for c in load(i):
                c.start()

    zeros_ref[...] = jnp.zeros_like(zeros_ref)
    for i in range(4):
        @pl.when(jnp.logical_not(is_own[i]))
        def _():
            for c in blank(i):
                c.start()

    for b in range(3):
        for half, ref in ((0, gah_ref), (1, gav_ref)):
            at = 256 * b + 128 * half
            grads[0][:, at : at + 128] = ref[256 * b : 256 * b + 256, :].astype(F32)
    grads[1][...] = gb_ref[0:256, :].astype(F32)
    for f in range(4):
        grads[2][:, 256 * f : 256 * f + 256] = gb_ref[256 * (f + 1) : 256 * (f + 2), :].astype(F32)
    grads[3][...] = gb_ref[1280:ROWS_B, :].astype(F32)

    mid = gb_ref[ROWS_B : ROWS_B + 8, :].astype(F32) + gb_ref[ROWS_B + 8 : ROWS_B + 16, :].astype(F32)
    side = [r[768:784, :].astype(F32) + r[784:800, :].astype(F32) for r in (gah_ref, gav_ref)]
    both = side[0] + side[1]
    for i in range(2):
        vg_ref[0:1, 128 * i : 128 * i + 128] = both[12 + i : 13 + i]
        vg_ref[1:2, 128 * i : 128 * i + 128] = both[14 + i : 15 + i]
        vg_ref[2:4, 128 * i : 128 * i + 128] = side[i][0:2]
        vg_ref[12:22, 128 * i : 128 * i + 128] = side[i][2:12]
    vg_ref[4:12, :] = mid
    grad = vg_ref[...]
    first_new = BETA_ONE * vf_ref[...] + (1.0 - BETA_ONE) * grad
    second_new = BETA_TWO * vs_ref[...] + (1.0 - BETA_TWO) * grad * grad
    vfn_ref[...] = first_new
    vsn_ref[...] = second_new
    vn_ref[...] = vec_ref[...] - RATE_VECTORS * (first_new / (1.0 - BETA_ONE**STEP)) / (
        jnp.sqrt(second_new / (1.0 - BETA_TWO**STEP)) + EPS_ADAM
    )

    for i in range(4):
        @pl.when(is_own[i])
        def _():
            for c in load(i):
                c.wait()
            first, second, weight = held[3 * i], held[3 * i + 1], held[3 * i + 2]
            lb, rb = left[2 * i], left[2 * i + 1]
            g = grads[i][...].astype(BF16)
            lh, ll = parts_of(lb[...])
            if i == 3:
                once = jnp.transpose(mm_tn(g, lh) + mm_tn(g, ll))
            else:
                once = mm_tn(lh, g) + mm_tn(ll, g)
            turned = careful(mm, once, rb[...])
            first_new = BETA_ONE * first[...] + (1.0 - BETA_ONE) * turned
            second_new = BETA_TWO * second[...] + (1.0 - BETA_TWO) * turned * turned
            first[...] = first_new
            second[...] = second_new
            step = (first_new / (1.0 - BETA_ONE**STEP)) / (
                jnp.sqrt(second_new / (1.0 - BETA_TWO**STEP)) + EPS_ADAM
            )
            back = mm_nt(mm(lh, step.astype(BF16)).astype(BF16), rb[...].astype(BF16))
            weight[...] = weight[...] - RATE * back - RATE * DECAY * weight[...]
            for c in store(i):
                c.start()

    for i in range(4):
        for c in store(i):
            c.wait()


def adam_call(owners, gb, gav, gah, vectors, vectors_first, vectors_second, slots, bases):
    vm = pltpu.VMEM
    any_space = pl.BlockSpec(memory_space=pl.ANY)
    vspec = pl.BlockSpec(memory_space=vm)
    sizes = [(s.shape[1], s.shape[2]) for s in slots[::3]]
    vshape = shape_of(F32, *vectors.shape)
    tallest = max(a for a, _ in sizes)
    widest = max(b for _, b in sizes)
    return pl.pallas_call(
        functools.partial(adam_kernel, vectors.shape[0], None),
        in_specs=[pl.BlockSpec(memory_space=pltpu.SMEM)] + [vspec] * 6 + [any_space] * 20,
        out_specs=[vspec] * 4 + [any_space] * 12 + [vspec] * 4,
        out_shape=[shape_of(F32, *s) for s in sizes]
        + [shape_of(F32, *s.shape) for s in slots]
        + [vshape] * 4,
        scratch_shapes=[vm((s.shape[1], s.shape[2]), F32) for s in slots]
        + [vm(b.shape, F32) for b in bases]
        + [vm((tallest, widest), F32), pltpu.SemaphoreType.DMA((20,)), pltpu.SemaphoreType.DMA((12,))],
        compiler_params=pltpu.CompilerParams(vmem_limit_bytes=VMEM_LIMIT),
        name="adam",
    )(owners, gb, gav, gah, vectors, vectors_first, vectors_second, *slots, *bases)


def wide_to_stack(w):
    n = w.shape[1] // 256
    return w.reshape(256, n, 256).transpose(1, 0, 2).reshape(256 * n, 256)


def by_steps(x, top, owners, slots, vectors, nb, nx, length):
    device_index = lax.axis_index(("band", "batch"))

    def own(slot, which):
        return jnp.where(device_index == owners[which], slot[0], 0.0).astype(BF16)

    stacked = jnp.concatenate(
        [
            wide_to_stack(own(slots[0], 0)),
            own(slots[1], 1),
            wide_to_stack(own(slots[2], 2)),
            own(slots[3], 3),
        ],
        axis=0,
    )
    weights = sum_everywhere(stacked, nb, nx, 0)[:ROW_END]

    def swap(packed, cid):
        m, rows, ch = packed.shape
        swapped = packed.reshape(m, nb, PIECE, ch).transpose(1, 0, 2, 3).reshape(m * rows, ch)
        got = exchange(swapped, nb, cid)
        return got.reshape(nb, m, PIECE, ch).transpose(1, 0, 2, 3).reshape(m, rows, ch)

    columns = swap(pack_tokens(x, nb, length), 1)
    qa_v, k_v, v_v, o_v, att_v, x_v = forward_call(columns, 1, nb, length, weights, vectors)
    qa_h, k_h, v_h, o_h, att_h = forward_call(x, 0, nb, length, weights, vectors)
    att_v = swap(att_v, 2)
    block_out, grad_middle, grad_h, grad_v, gp_t, g1, g2_t, rows_mid = middle_call(
        x, att_h, att_v, top, nb, length, weights, vectors
    )
    grad_v = swap(grad_v, 3)
    part_v, gw_v, rows_v = backward_call(
        x_v, grad_v, qa_v, k_v, v_v, o_v, 1, nb, length, weights, vectors
    )
    part_h, gw_h, rows_h = backward_call(
        x, grad_h, qa_h, k_h, v_h, o_h, 0, nb, length, weights, vectors
    )
    part_v = swap(part_v, 4)
    input_grad = last_call(x, grad_middle, part_h, part_v, nb, length, vectors)

    def two(rows):
        high = rows.astype(BF16)
        return [high, (rows - high.astype(F32)).astype(BF16)]

    gb = jnp.concatenate(
        [gp_t.T.astype(BF16), wide_to_stack(g1.astype(BF16)), g2_t.T.astype(BF16)] + two(rows_mid),
        axis=0,
    )

    def side(gw, rows):
        return jnp.concatenate(
            [gw[:, 128 * b : 128 * b + 128].astype(BF16) for b in range(3)] + two(rows), axis=0
        )

    gb = sum_everywhere(gb, nb, nx, 5)
    gav = sum_everywhere(side(gw_v, rows_v), nb, nx, 6)
    gah = sum_everywhere(side(gw_h, rows_h), nb, nx, 7)
    return block_out, input_grad, gb, gav, gah


def per_device(
    tokens_in, cotangent, owners,
    weight_qkv, weight_proj, weight_fc1, weight_fc2,
    first_qkv, second_qkv, first_proj, second_proj, first_fc1, second_fc1, first_fc2, second_fc2,
    left_qkv, right_qkv, left_proj, right_proj, left_fc1, right_fc1, left_fc2, right_fc2,
    vectors, vectors_first, vectors_second,
    *, nb, nx,
):
    micro, images, band_rows, length, channels = tokens_in.shape
    tokens = band_rows * length
    x = tokens_in.reshape(micro * images, tokens, channels)
    top = cotangent.reshape(micro * images, tokens, channels)
    weights = (weight_qkv, weight_proj, weight_fc1, weight_fc2)
    if tokens <= 1024:
        block_out, input_grad, gb, gav, gah = block_call(
            x, top, owners, *weights, vectors, nb, nx, length
        )
    else:
        block_out, input_grad, gb, gav, gah = by_steps(
            x, top, owners, weights, vectors, nb, nx, length
        )
    slots = (
        first_qkv, second_qkv, weight_qkv, first_proj, second_proj, weight_proj,
        first_fc1, second_fc1, weight_fc1, first_fc2, second_fc2, weight_fc2,
    )
    bases = (left_qkv, right_qkv, left_proj, right_proj, left_fc1, right_fc1, left_fc2, right_fc2)
    done = adam_call(
        owners, gb, gav, gah, vectors, vectors_first, vectors_second, slots, bases
    )
    results = [block_out.reshape(tokens_in.shape), input_grad.reshape(tokens_in.shape)]
    for i in range(4):
        results.append(done[i])
        results += list(done[4 + 3 * i : 7 + 3 * i])
    return tuple(results) + tuple(done[16:20])


def solution(mesh):
    tokens_spec = P(None, "batch", "band", None, None)
    slot_spec = P(("band", "batch"), None, None)
    return jax.shard_map(
        functools.partial(per_device, nb=mesh.shape["band"], nx=mesh.shape["batch"]),
        mesh=mesh,
        in_specs=(tokens_spec, tokens_spec, P()) + (slot_spec,) * 12 + (P(),) * 11,
        out_specs=(tokens_spec, tokens_spec)
        + (P(), slot_spec, slot_spec, slot_spec) * 4
        + (P(),) * 4,
        check_vma=False,
    )
```

```python
import functools

import jax
import jax.numpy as jnp
from jax import lax
from jax.experimental import pallas as pl
from jax.experimental.pallas import tpu as pltpu
from jax.sharding import PartitionSpec as P

HEAD_DIM = 32
STRIPE = 7
STEP = 10
EPS_NORM = 1e-05
BETA_ONE = 0.5
BETA_TWO = 0.6
RATE = 0.04
RATE_VECTORS = 0.2
DECAY = 0.01
EPS_ADAM = 1e-08
MESH = pl.DeviceIdType.MESH
F32 = jnp.float32
BF16 = jnp.bfloat16
PIECE = 64
LOG2E = 1.4426950408889634
LN2 = 0.6931471805599453
Q_SCALE = LOG2E * HEAD_DIM**-0.5
LONGEST = 1024
VMEM_LIMIT = 60 * 1024 * 1024
ROW_QKV, ROW_PROJ, ROW_FC1, ROW_FC2, ROW_END = 0, 768, 1024, 2048, 3072


def mm(a, b):
    return lax.dot_general(a, b, (((1,), (0,)), ((), ())), preferred_element_type=F32)


def mm_nt(a, b):
    return lax.dot_general(a, b, (((1,), (1,)), ((), ())), preferred_element_type=F32)


def mm_tn(a, b):
    return lax.dot_general(a, b, (((0,), (0,)), ((), ())), preferred_element_type=F32)


def exchange_kernel(n, piece, x_ref, o_ref, send_sem, recv_sem, loc_sem):
    me = lax.axis_index("band")
    bar = pltpu.get_barrier_semaphore()

    def greet(k, c):
        pl.semaphore_signal(
            bar, inc=1, device_id={"band": lax.rem(me + k, n)}, device_id_type=MESH
        )
        return c

    lax.fori_loop(1, n, greet, 0)
    pl.semaphore_wait(bar, n - 1)

    def rows(i):
        return pl.ds(pl.multiple_of(i * piece, piece), piece)

    def send(k, c):
        d = lax.rem(me + k, n)
        pltpu.make_async_remote_copy(
            src_ref=x_ref.at[rows(d)],
            dst_ref=o_ref.at[rows(me)],
            send_sem=send_sem.at[k],
            recv_sem=recv_sem.at[k],
            device_id={"band": d},
            device_id_type=MESH,
        ).start()
        return c

    lax.fori_loop(1, n, send, 0)
    local = pltpu.make_async_copy(x_ref.at[rows(me)], o_ref.at[rows(me)], loc_sem)
    local.start()
    local.wait()

    def take(k, c):
        s = lax.rem(me - k + n, n)
        pltpu.make_async_remote_copy(
            src_ref=x_ref.at[rows(s)],
            dst_ref=o_ref.at[rows(s)],
            send_sem=send_sem.at[k],
            recv_sem=recv_sem.at[k],
            device_id={"band": s},
            device_id_type=MESH,
        ).wait()
        return c

    lax.fori_loop(1, n, take, 0)


def exchange(x, n, cid):
    return pl.pallas_call(
        functools.partial(exchange_kernel, n, x.shape[0] // n),
        out_shape=jax.ShapeDtypeStruct(x.shape, x.dtype),
        in_specs=[pl.BlockSpec(memory_space=pltpu.VMEM)],
        out_specs=pl.BlockSpec(memory_space=pltpu.VMEM),
        scratch_shapes=[
            pltpu.SemaphoreType.DMA((n,)),
            pltpu.SemaphoreType.DMA((n,)),
            pltpu.SemaphoreType.DMA,
        ],
        compiler_params=pltpu.CompilerParams(
            collective_id=cid, has_side_effects=True, vmem_limit_bytes=VMEM_LIMIT
        ),
        name="exchange",
    )(x)


def sum_kernel(nb, nx, total_rows, x_ref, o_ref, got, half, recv, s1, r1, s2, r2, s3, r3, s4, r4):
    nq = (nb // 2) * nx
    p = total_rows // (2 * nq)
    band = lax.axis_index("band")
    core = lax.rem(band, 2)
    q = (band // 2) * nx + lax.axis_index("batch")
    sibling = {"band": band + 1 - 2 * core}
    bar = pltpu.get_barrier_semaphore()

    def chip(t):
        return {"band": (t // nx) * 2 + core, "batch": lax.rem(t, nx)}

    def ahead(k):
        return lax.rem(q + k, nq)

    def behind(k):
        return lax.rem(q - k + nq, nq)

    def copy(src, dst, ss, rs, dev):
        return pltpu.make_async_remote_copy(
            src_ref=src, dst_ref=dst, send_sem=ss, recv_sem=rs, device_id=dev, device_id_type=MESH
        )

    def loop(lo, hi, body):
        def step(k, c):
            body(k)
            return c

        lax.fori_loop(lo, hi, step, 0)

    pl.semaphore_signal(bar, inc=1, device_id=sibling, device_id_type=MESH)
    loop(
        1,
        nq,
        lambda k: pl.semaphore_signal(
            bar, inc=1, device_id=chip(ahead(k)), device_id_type=MESH
        ),
    )
    pl.semaphore_wait(bar, nq)

    def whole_rows(c, t):
        return pl.ds(pl.multiple_of((c * nq + t) * p, 16), p)

    def half_rows(t):
        return pl.ds(pl.multiple_of(t * p, 16), p)

    def pair_copy(k, side):
        t = ahead(k)
        return copy(
            x_ref.at[whole_rows(side, t)], got.at[half_rows(t)], s1.at[t], r1.at[t], sibling
        )

    loop(1, nq + 1, lambda k: pair_copy(k, 1 - core).start())

    def scatter_copy(k):
        t = ahead(k)
        return copy(half.at[half_rows(t)], recv.at[half_rows(q)], s2.at[k], r2.at[k], chip(t))

    def pair_sum(k):
        t = ahead(k)
        pair_copy(k, core).wait()
        half[half_rows(t)] = (
            x_ref[whole_rows(core, t)].astype(F32) + got[half_rows(t)].astype(F32)
        ).astype(BF16)

        @pl.when(k < nq)
        def _():
            scatter_copy(k).start()

    loop(1, nq + 1, pair_sum)

    def add_piece(k, acc):
        t = behind(k)
        copy(half.at[half_rows(t)], recv.at[half_rows(t)], s2.at[k], r2.at[k], chip(t)).wait()
        return acc + recv[half_rows(t)].astype(F32)

    total = lax.fori_loop(1, nq, add_piece, half[half_rows(q)].astype(F32))
    mine = o_ref.at[whole_rows(core, q)]
    o_ref[whole_rows(core, q)] = total.astype(BF16)

    def gather_copy(k):
        return copy(mine, mine, s3.at[k], r3.at[k], chip(ahead(k)))

    def pass_on(t, side):
        return copy(
            o_ref.at[whole_rows(core, t)],
            o_ref.at[whole_rows(side, t)],
            s4.at[t],
            r4.at[t],
            sibling,
        )

    loop(1, nq, lambda k: gather_copy(k).start())
    pass_on(q, core).start()

    def relay(k):
        t = behind(k)
        copy(mine, o_ref.at[whole_rows(core, t)], s3.at[k], r3.at[k], chip(t)).wait()
        pass_on(t, core).start()

    loop(1, nq, relay)
    loop(0, nq, lambda t: pass_on(t, 1 - core).wait())


def sum_everywhere(x, nb, nx, cid):
    rows, cols = x.shape
    nq = nb // 2 * nx
    unit = 32 * nq
    padded = -(-rows // unit) * unit
    if padded != rows:
        x = jnp.concatenate([x, jnp.zeros((padded - rows, cols), x.dtype)], axis=0)
    sems = [pltpu.SemaphoreType.DMA((nq,)) for _ in range(8)]
    out = pl.pallas_call(
        functools.partial(sum_kernel, nb, nx, padded),
        out_shape=jax.ShapeDtypeStruct(x.shape, x.dtype),
        in_specs=[pl.BlockSpec(memory_space=pltpu.VMEM)],
        out_specs=pl.BlockSpec(memory_space=pltpu.VMEM),
        scratch_shapes=[pltpu.VMEM((padded // 2, cols), x.dtype)] * 3 + sems,
        compiler_params=pltpu.CompilerParams(
            collective_id=cid, has_side_effects=True, vmem_limit_bytes=VMEM_LIMIT
        ),
        name="sum_everywhere",
    )(x)
    return out


def order_out(pieces_n, length):
    row = lax.broadcasted_iota(jnp.int32, (pieces_n * PIECE, 1), 0)
    s = row // PIECE
    m = row % PIECE
    a = (m * 37) // 256
    b = m - STRIPE * a
    token = jnp.where(m < STRIPE * STRIPE, a * length + STRIPE * s + b, -1)
    column = lax.broadcasted_iota(jnp.int32, (pieces_n * PIECE, STRIPE * length), 1)
    return jnp.where(column == token, 1.0, 0.0).astype(BF16)


def order_in(pieces_n, length):
    row = lax.broadcasted_iota(jnp.int32, (1, pieces_n * PIECE), 1)
    s = row // PIECE
    m = row % PIECE
    a = (m * 37) // 256
    b = m - STRIPE * a
    token = jnp.where(m < STRIPE * STRIPE, b * length + STRIPE * s + a, -1)
    column = lax.broadcasted_iota(jnp.int32, (STRIPE * length, pieces_n * PIECE), 0)
    return jnp.where(column == token, 1.0, 0.0).astype(BF16)


def unit_rows(values):
    centred = values - jnp.mean(values, axis=-1, keepdims=True)
    inverse = lax.rsqrt(jnp.mean(centred * centred, axis=-1, keepdims=True) + EPS_NORM)
    return centred * inverse, inverse


def norm_back(grad_normed, gain, unit, inverse):
    scaled = grad_normed * gain
    first_mean = jnp.mean(scaled, axis=-1, keepdims=True)
    second_mean = jnp.mean(scaled * unit, axis=-1, keepdims=True)
    return inverse * (scaled - first_mean - unit * second_mean)


def shifted_columns(v, length):
    tokens = v.shape[0]
    column = lax.broadcasted_iota(jnp.int32, v.shape, 0) % length
    before = jnp.where(column == 0, 0.0, pltpu.roll(v, 1, 0))
    after = jnp.where(column == length - 1, 0.0, pltpu.roll(v, tokens - 1, 0))
    return before, v, after


def shifted_rows(v, length):
    zeros = jnp.zeros((length, v.shape[1]), v.dtype)
    above = jnp.concatenate([zeros, v[: v.shape[0] - length]], axis=0)
    below = jnp.concatenate([v[length:], zeros], axis=0)
    return above, v, below


def tap_row(half, a, b):
    return 12 + (3 * a + b if half == 0 else 3 * b + a)


def conv(v, vec_ref, lanes, half, length, flipped):
    total = jnp.zeros_like(v)
    for b, col in enumerate(shifted_columns(v, length)):
        for a, val in enumerate(shifted_rows(col, length)):
            row = tap_row(half, 2 - a, 2 - b) if flipped else tap_row(half, a, b)
            total = total + val * vec_ref[row : row + 1, lanes]
    return total


def head_mask(shape, h, offset=0):
    lane = lax.broadcasted_iota(jnp.int32, shape, len(shape) - 1) - offset
    return (lane >= h * HEAD_DIM) & (lane < (h + 1) * HEAD_DIM)


def three_parts(x):
    lane = lax.broadcasted_iota(jnp.int32, x.shape, len(x.shape) - 1) % HEAD_DIM
    hi = x.astype(BF16).astype(F32)
    mid = (x - hi).astype(BF16).astype(F32)
    low = x - hi - mid
    parts = jnp.where(lane == 0, hi, jnp.where(lane == 1, mid, jnp.where(lane == 2, low, 0.0)))
    return parts.astype(BF16)


def head_lanes(h, width):
    lane = lax.broadcasted_iota(jnp.int32, (1, width), 1) % 128
    keep = (lane >= h * HEAD_DIM) & (lane < (h + 1) * HEAD_DIM)
    return jnp.where(keep, 1.0, 0.0).astype(BF16)


def beside_parts(block):
    lane = lax.broadcasted_iota(jnp.int32, block.shape, 1) % HEAD_DIM
    return jnp.concatenate([block, jnp.where(lane < 3, 1.0, 0.0).astype(BF16)], axis=1)


def turned(block):
    return jnp.transpose(block.astype(F32)).astype(BF16)


def lane_blocks(w_ref, half):
    return lambda b: w_ref[256 * b : 256 * b + 256, 128 * half : 128 * half + 128]


def attention_forward(x, half, length, wb, vec_ref, qa_ref, k_ref, v_ref, o_ref, att_ref):
    tokens = x.shape[0]
    lanes = slice(128 * half, 128 * half + 128)
    unit, _ = unit_rows(x)
    normed = (unit * vec_ref[0:1] + vec_ref[1:2]).astype(BF16)
    q = (mm(normed, wb(0)) + vec_ref[2:3, lanes]) * Q_SCALE
    qa_ref[:, 0:128] = q.astype(BF16)
    k_ref[...] = mm(normed, wb(1)).astype(BF16)
    v = (mm(normed, wb(2)) + vec_ref[3:4, lanes]).astype(BF16)
    v_ref[...] = v
    v_turned = turned(v)
    ones = jnp.ones((HEAD_DIM, tokens), BF16)

    def head_scores(h):
        return mm_nt(k_ref[...] * head_lanes(h, 128), qa_ref[:, 0:128])

    following = head_scores(0)
    weighted, totals, tops = [], [], []
    for h in range(4):
        scores = following
        if h < 3:
            following = head_scores(h + 1)
        highest = jnp.max(scores, axis=0, keepdims=True)
        probs = jnp.exp2(scores - highest).astype(BF16)
        rows = slice(HEAD_DIM * h, HEAD_DIM * h + HEAD_DIM)
        both = mm(jnp.concatenate([v_turned[rows], ones], axis=0), probs)
        weighted.append(both[:HEAD_DIM])
        totals.append(both[HEAD_DIM:])
        tops.append(jnp.broadcast_to(highest, (HEAD_DIM, tokens)))
    total = jnp.concatenate(totals, axis=0)
    attended = jnp.transpose(jnp.concatenate(weighted, axis=0) / total)
    o_ref[...] = attended
    log_total = jnp.concatenate(tops, axis=0) + jnp.log2(total)
    qa_ref[:, 128:256] = three_parts(-jnp.transpose(log_total))
    lepe = conv(v_ref[...].astype(F32), vec_ref, lanes, half, length, False)
    att_ref[...] = (attended + lepe + vec_ref[21:22, lanes]).astype(BF16)


def attention_backward(
    x, half, length, grad, wb, vec_ref, qa_ref, k_ref, v_ref, o_ref, da_ref, gw_ref, rows_ref
):
    lanes = slice(128 * half, 128 * half + 128)
    grad_f = grad.astype(F32)
    product = grad_f * o_ref[...]
    inner = jnp.zeros_like(product)
    for h in range(4):
        keep = head_mask(product.shape, h)
        inner = jnp.where(
            keep, jnp.sum(jnp.where(keep, product, 0.0), axis=-1, keepdims=True), inner
        )
    da_ref[:, 0:128] = grad
    da_ref[:, 128:256] = three_parts(-inner)
    k_turned = turned(k_ref[...])
    q_turned = turned(qa_ref[:, 0:128])
    grad_turned = turned(grad)
    k_wide = beside_parts(k_ref[...])
    v_wide = beside_parts(v_ref[...])

    def head_products(h):
        mask = head_lanes(h, 256)
        return mm_nt(qa_ref[...] * mask, k_wide), mm_nt(da_ref[...] * mask, v_wide)

    early = grad.shape[0] <= LONGEST
    following = head_products(0) if early else None
    dqs, dks, dvs = [], [], []
    for h in range(4):
        scores, grad_probs = following if early else head_products(h)
        if early and h < 3:
            following = head_products(h + 1)
        probs = jnp.exp2(scores)
        grad_scores = (probs * grad_probs).astype(BF16)
        rows = slice(HEAD_DIM * h, HEAD_DIM * h + HEAD_DIM)
        dvs.append(mm(grad_turned[rows], probs.astype(BF16)))
        dks.append(mm(q_turned[rows], grad_scores))
        dqs.append(mm_nt(k_turned[rows], grad_scores))
    dq = (jnp.transpose(jnp.concatenate(dqs, axis=0)) * HEAD_DIM**-0.5).astype(BF16)
    dk = (jnp.transpose(jnp.concatenate(dks, axis=0)) * LN2).astype(BF16)
    dv = jnp.transpose(jnp.concatenate(dvs, axis=0))
    dv = (dv + conv(grad_f, vec_ref, lanes, half, length, True)).astype(BF16)
    unit, _ = unit_rows(x)
    normed = (unit * vec_ref[0:1] + vec_ref[1:2]).astype(BF16)
    gw_ref[...] += mm_tn(normed, jnp.concatenate([dq, dk, dv], axis=1))
    rows_ref[0:1, :] += jnp.sum(dq.astype(F32), axis=0, keepdims=True)
    rows_ref[1:2, :] += jnp.sum(dv.astype(F32), axis=0, keepdims=True)
    for b, col in enumerate(shifted_columns(v_ref[...].astype(F32), length)):
        for a, val in enumerate(shifted_rows(col, length)):
            row = tap_row(half, a, b) - 10
            rows_ref[row : row + 1, :] += jnp.sum(grad_f * val, axis=0, keepdims=True)
    rows_ref[11:12, :] += jnp.sum(grad_f, axis=0, keepdims=True)
    part = mm_nt(dq, wb(0)) + mm_nt(dk, wb(1)) + mm_nt(dv, wb(2))
    gain_row = jnp.sum(part * unit, axis=0, keepdims=True)
    shift_row = jnp.sum(part, axis=0, keepdims=True)
    for i in range(2):
        rows_ref[12 + i : 13 + i, :] += gain_row[:, 128 * i : 128 * i + 128]
        rows_ref[14 + i : 15 + i, :] += shift_row[:, 128 * i : 128 * i + 128]
    return part


def feed_forward(x, att, top, w_ref, base, vec_ref, n2_ref, acc_ref, gn_ref, gp_ref, g1_ref, g2_ref, rows_ref):
    middle = x + mm(att, w_ref[base : base + 256, :]) + vec_ref[4:5]
    unit, inverse = unit_rows(middle)
    n2_ref[...] = (unit * vec_ref[5:6] + vec_ref[6:7]).astype(BF16)
    acc_ref[...] = middle + vec_ref[11:12]
    gn_ref[...] = jnp.zeros_like(gn_ref)
    for f in range(4):
        w1 = w_ref[base + 256 * (1 + f) : base + 256 * (2 + f), :]
        w2 = w_ref[base + 256 * (5 + f) : base + 256 * (6 + f), :]
        cols = slice(256 * f, 256 * f + 256)
        hidden = mm(n2_ref[...], w1) + vec_ref[7 + f : 8 + f]
        below = 0.5 * (1.0 + lax.erf(hidden * (0.5**0.5)))
        active = (hidden * below).astype(BF16)
        slope = below + hidden * jnp.exp(-0.5 * hidden * hidden) * 0.3989422804014327
        grad_hidden = (mm_nt(top, w2) * slope).astype(BF16)
        acc_ref[...] += mm(active, w2)
        gn_ref[...] += mm_nt(grad_hidden, w1)
        g1_ref[:, cols] += mm_tn(n2_ref[...], grad_hidden)
        g2_ref[:, cols] += mm_tn(top, active)
        rows_ref[3 + f : 4 + f, :] += jnp.sum(grad_hidden.astype(F32), axis=0, keepdims=True)
    grad_normed = gn_ref[...]
    top_f = top.astype(F32)
    grad_middle = top_f + norm_back(grad_normed, vec_ref[5:6], unit, inverse)
    branch = grad_middle.astype(BF16)
    gp_ref[...] += mm_tn(branch, att)
    rows_ref[0:1, :] += jnp.sum(branch.astype(F32), axis=0, keepdims=True)
    rows_ref[1:2, :] += jnp.sum(grad_normed * unit, axis=0, keepdims=True)
    rows_ref[2:3, :] += jnp.sum(grad_normed, axis=0, keepdims=True)
    rows_ref[7:8, :] += jnp.sum(top_f, axis=0, keepdims=True)
    grad_att = mm_nt(branch, w_ref[base : base + 256, :]).astype(BF16)
    return acc_ref[...].astype(BF16), grad_middle, grad_att


PARAMS = pltpu.CompilerParams(
    dimension_semantics=("arbitrary",), vmem_limit_bytes=VMEM_LIMIT
)


def whole(shape):
    return pl.BlockSpec(shape, lambda m: (0,) * len(shape))


def each(shape):
    return pl.BlockSpec((None,) + shape, lambda m: (m,) + (0,) * len(shape))


def shape_of(dtype, *shape):
    return jax.ShapeDtypeStruct(shape, dtype)


def pack_tokens(x, nb, length):
    micro, tokens, channels = x.shape

    def kernel(x_ref, o_ref, hot):
        @pl.when(pl.program_id(0) == 0)
        def _():
            hot[...] = order_out(nb, length)

        o_ref[...] = mm(hot[...], x_ref[...]).astype(BF16)

    return pl.pallas_call(
        kernel,
        grid=(micro,),
        in_specs=[each((tokens, channels))],
        out_specs=each((nb * PIECE, channels)),
        out_shape=shape_of(BF16, micro, nb * PIECE, channels),
        scratch_shapes=[pltpu.VMEM((nb * PIECE, tokens), BF16)],
        compiler_params=PARAMS,
        name="pack_tokens",
    )(x)


def forward_call(x, half, nb, length, weights, vectors):
    micro = x.shape[0]
    tokens = STRIPE * length
    packed = nb * PIECE

    def kernel(x_ref, w_ref, vec_ref, qa_ref, k_ref, v_ref, o_ref, att_ref, xs_ref, *scr):
        if half == 0:
            attention_forward(
                x_ref[...].astype(F32), half, length, lane_blocks(w_ref, half), vec_ref, qa_ref, k_ref, v_ref, o_ref, att_ref
            )
        else:
            att_s, hot_in, hot_out = scr

            @pl.when(pl.program_id(0) == 0)
            def _():
                hot_in[...] = order_in(nb, length)
                hot_out[...] = order_out(nb, length)

            xs_ref[...] = mm(hot_in[...], x_ref[...]).astype(BF16)
            attention_forward(
                xs_ref[...].astype(F32), half, length, lane_blocks(w_ref, half), vec_ref, qa_ref, k_ref, v_ref, o_ref, att_s
            )
            att_ref[...] = mm(hot_out[...], att_s[...]).astype(BF16)

    rows = tokens if half == 0 else packed
    scratch = []
    if half == 1:
        scratch += [
            pltpu.VMEM((tokens, 128), BF16),
            pltpu.VMEM((tokens, packed), BF16),
            pltpu.VMEM((packed, tokens), BF16),
        ]
    if half == 0:
        def body(x_ref, w_ref, vec_ref, qa_ref, k_ref, v_ref, o_ref, att_ref, *scr):
            kernel(x_ref, w_ref, vec_ref, qa_ref, k_ref, v_ref, o_ref, att_ref, None, *scr)
        extra_specs, extra_shapes = [], []
    else:
        body = kernel
        extra_specs = [each((tokens, 256))]
        extra_shapes = [shape_of(BF16, micro, tokens, 256)]
    return pl.pallas_call(
        body,
        grid=(micro,),
        in_specs=[each((rows, 256)), whole(weights.shape), whole(vectors.shape)],
        out_specs=[
            each((tokens, 256)),
            each((tokens, 128)),
            each((tokens, 128)),
            each((tokens, 128)),
            each((rows, 128)),
        ] + extra_specs,
        out_shape=[
            shape_of(BF16, micro, tokens, 256),
            shape_of(BF16, micro, tokens, 128),
            shape_of(BF16, micro, tokens, 128),
            shape_of(F32, micro, tokens, 128),
            shape_of(BF16, micro, rows, 128),
        ] + extra_shapes,
        scratch_shapes=scratch,
        compiler_params=PARAMS,
        name="attention_forward_%d" % half,
    )(x, weights, vectors)


def middle_call(x, att_h, att_v, top, nb, length, weights, vectors):
    micro, tokens, _ = x.shape
    packed = nb * PIECE

    def kernel(
        x_ref, h_ref, v_ref, top_ref, w_ref, vec_ref,
        out_ref, gm_ref, gh_ref, gv_ref, gp_ref, g1_ref, g2_ref, rows_ref,
        hot_in, hot_out, att, n2, acc, gn,
    ):
        @pl.when(pl.program_id(0) == 0)
        def _():
            hot_in[...] = order_in(nb, length)
            hot_out[...] = order_out(nb, length)
            for ref in (gp_ref, g1_ref, g2_ref, rows_ref):
                ref[...] = jnp.zeros_like(ref)

        att[:, 0:128] = h_ref[...]
        att[:, 128:256] = mm(hot_in[...], v_ref[...]).astype(BF16)
        out, grad_middle, grad_att = feed_forward(
            x_ref[...].astype(F32), att[...], top_ref[...], w_ref, ROW_PROJ, vec_ref, n2, acc, gn, gp_ref, g1_ref, g2_ref, rows_ref
        )
        out_ref[...] = out
        gm_ref[...] = grad_middle
        gh_ref[...] = grad_att[:, 0:128]
        gv_ref[...] = mm(hot_out[...], grad_att[:, 128:256]).astype(BF16)

    return pl.pallas_call(
        kernel,
        grid=(micro,),
        in_specs=[
            each((tokens, 256)), each((tokens, 128)), each((packed, 128)), each((tokens, 256)),
            whole(weights.shape), whole(vectors.shape),
        ],
        out_specs=[
            each((tokens, 256)), each((tokens, 256)), each((tokens, 128)), each((packed, 128)),
            whole((256, 256)), whole((256, 1024)), whole((256, 1024)), whole((8, 256)),
        ],
        out_shape=[
            shape_of(BF16, micro, tokens, 256), shape_of(F32, micro, tokens, 256),
            shape_of(BF16, micro, tokens, 128), shape_of(BF16, micro, packed, 128),
            shape_of(F32, 256, 256), shape_of(F32, 256, 1024), shape_of(F32, 256, 1024), shape_of(F32, 8, 256),
        ],
        scratch_shapes=[
            pltpu.VMEM((tokens, packed), BF16), pltpu.VMEM((packed, tokens), BF16),
            pltpu.VMEM((tokens, 256), BF16), pltpu.VMEM((tokens, 256), BF16),
            pltpu.VMEM((tokens, 256), F32), pltpu.VMEM((tokens, 256), F32),
        ],
        compiler_params=PARAMS,
        name="feed_forward",
    )(x, att_h, att_v, top, weights, vectors)


def backward_call(x, grad, qa, k, v, o, half, nb, length, weights, vectors):
    micro, tokens, _ = x.shape
    packed = nb * PIECE

    def kernel(
        x_ref, g_ref, qa_ref, k_ref, v_ref, o_ref, w_ref, vec_ref, gn_ref, gw_ref, rows_ref,
        da, *scr,
    ):
        @pl.when(pl.program_id(0) == 0)
        def _():
            gw_ref[...] = jnp.zeros_like(gw_ref)
            rows_ref[...] = jnp.zeros_like(rows_ref)
            if half == 1:
                scr[0][...] = order_in(nb, length)
                scr[1][...] = order_out(nb, length)

        grad_in = g_ref[...] if half == 0 else mm(scr[0][...], g_ref[...]).astype(BF16)
        part = attention_backward(
            x_ref[...].astype(F32), half, length, grad_in, lane_blocks(w_ref, half), vec_ref, qa_ref, k_ref, v_ref, o_ref,
            da, gw_ref, rows_ref,
        )
        if half == 0:
            gn_ref[...] = part
        else:
            gn_ref[...] = mm(scr[1][...], part.astype(BF16)).astype(BF16)

    rows = tokens if half == 0 else packed
    scratch = [pltpu.VMEM((tokens, 256), BF16)]
    if half == 1:
        scratch += [pltpu.VMEM((tokens, packed), BF16), pltpu.VMEM((packed, tokens), BF16)]
    return pl.pallas_call(
        kernel,
        grid=(micro,),
        in_specs=[
            each((tokens, 256)), each((rows, 128)), each((tokens, 256)), each((tokens, 128)),
            each((tokens, 128)), each((tokens, 128)), whole(weights.shape), whole(vectors.shape),
        ],
        out_specs=[each((rows, 256)), whole((256, 384)), whole((16, 128))],
        out_shape=[
            shape_of(F32 if half == 0 else BF16, micro, rows, 256),
            shape_of(F32, 256, 384), shape_of(F32, 16, 128),
        ],
        scratch_shapes=scratch,
        compiler_params=PARAMS,
        name="attention_backward_%d" % half,
    )(x, grad, qa, k, v, o, weights, vectors)


def last_call(x, grad_middle, part_h, part_v, nb, length, vectors):
    micro, tokens, _ = x.shape
    packed = nb * PIECE

    def kernel(x_ref, gm_ref, h_ref, v_ref, vec_ref, out_ref, hot_in):
        @pl.when(pl.program_id(0) == 0)
        def _():
            hot_in[...] = order_in(nb, length)

        grad_normed = h_ref[...] + mm(hot_in[...], v_ref[...])
        unit, inverse = unit_rows(x_ref[...].astype(F32))
        out_ref[...] = (
            gm_ref[...] + norm_back(grad_normed, vec_ref[0:1], unit, inverse)
        ).astype(BF16)

    return pl.pallas_call(
        kernel,
        grid=(micro,),
        in_specs=[
            each((tokens, 256)), each((tokens, 256)), each((tokens, 256)), each((packed, 256)), whole(vectors.shape),
        ],
        out_specs=each((tokens, 256)),
        out_shape=shape_of(BF16, micro, tokens, 256),
        scratch_shapes=[pltpu.VMEM((tokens, packed), BF16)],
        compiler_params=PARAMS,
        name="input_gradient",
    )(x, grad_middle, part_h, part_v, vectors)


def repeat(lo, hi, body):
    def step(k, c):
        body(k)
        return c

    lax.fori_loop(lo, hi, step, 0)


def remote(src, dst, ss, rs, dev):
    return pltpu.make_async_remote_copy(
        src_ref=src, dst_ref=dst, send_sem=ss, recv_sem=rs, device_id=dev, device_id_type=MESH
    )


class Swap:
    def __init__(self, n, out_ref, in_ref, send_sem, recv_sem):
        self.n, self.out, self.into, self.ss, self.rs = n, out_ref, in_ref, send_sem, recv_sem
        self.me = lax.axis_index("band")

    def rows(self, i):
        return pl.ds(pl.multiple_of(i * PIECE, PIECE), PIECE)

    def send(self, m):
        mine = self.rows(self.me)

        def one(k):
            d = lax.rem(self.me + k, self.n)
            remote(
                self.out.at[m, self.rows(d)],
                self.into.at[m, mine],
                self.ss.at[m, k],
                self.rs.at[m, k],
                {"band": d},
            ).start()

        repeat(1, self.n, one)
        self.into[m, mine, :] = self.out[m, mine, :]

    def wait(self, m):
        def one(k):
            s = lax.rem(self.me - k + self.n, self.n)
            remote(
                self.out.at[m, self.rows(s)],
                self.into.at[m, self.rows(s)],
                self.ss.at[m, k],
                self.rs.at[m, k],
                {"band": s},
            ).wait()

        repeat(1, self.n, one)


class Sum:
    def __init__(self, nb, nx, x_ref, o_ref, got, half, recv, sems):
        self.nx = nx
        self.nq = (nb // 2) * nx
        self.p = x_ref.shape[0] // (2 * self.nq)
        band = lax.axis_index("band")
        self.core = lax.rem(band, 2)
        self.q = (band // 2) * nx + lax.axis_index("batch")
        self.sibling = {"band": band + 1 - 2 * self.core}
        self.x, self.o, self.got, self.half, self.recv = x_ref, o_ref, got, half, recv
        self.sems = sems

    def chip(self, t):
        return {"band": (t // self.nx) * 2 + self.core, "batch": lax.rem(t, self.nx)}

    def ahead(self, k):
        return lax.rem(self.q + k, self.nq)

    def behind(self, k):
        return lax.rem(self.q - k + self.nq, self.nq)

    def wide(self, c, t):
        return pl.ds(pl.multiple_of((c * self.nq + t) * self.p, 16), self.p)

    def thin(self, t):
        return pl.ds(pl.multiple_of(t * self.p, 16), self.p)

    def sem(self, i, k):
        return self.sems.at[2 * i, k], self.sems.at[2 * i + 1, k]

    def pair_copy(self, k, side):
        t = self.ahead(k)
        return remote(
            self.x.at[self.wide(side, t)], self.got.at[self.thin(t)], *self.sem(0, t), self.sibling
        )

    def start(self):
        repeat(1, self.nq + 1, lambda k: self.pair_copy(k, 1 - self.core).start())

    def scatter(self):
        def one(k):
            t = self.ahead(k)
            self.pair_copy(k, self.core).wait()
            self.half[self.thin(t)] = (
                self.x[self.wide(self.core, t)].astype(F32) + self.got[self.thin(t)].astype(F32)
            ).astype(BF16)

            @pl.when(k < self.nq)
            def _():
                remote(
                    self.half.at[self.thin(t)],
                    self.recv.at[self.thin(self.q)],
                    *self.sem(1, k),
                    self.chip(t),
                ).start()

        repeat(1, self.nq + 1, one)

    def gather(self):
        def one(k, acc):
            t = self.behind(k)
            remote(
                self.half.at[self.thin(t)],
                self.recv.at[self.thin(t)],
                *self.sem(1, k),
                self.chip(t),
            ).wait()
            return acc + self.recv[self.thin(t)].astype(F32)

        total = lax.fori_loop(1, self.nq, one, self.half[self.thin(self.q)].astype(F32))
        mine = self.wide(self.core, self.q)
        self.o[mine] = total.astype(BF16)

        def give(k):
            remote(
                self.o.at[mine], self.o.at[mine], *self.sem(2, k), self.chip(self.ahead(k))
            ).start()

        repeat(1, self.nq, give)
        self.pass_on(self.q, self.core).start()

    def pass_on(self, t, side):
        return remote(
            self.o.at[self.wide(self.core, t)],
            self.o.at[self.wide(side, t)],
            *self.sem(3, t),
            self.sibling,
        )

    def relay(self):
        mine = self.wide(self.core, self.q)

        def one(k):
            t = self.behind(k)
            remote(
                self.o.at[mine], self.o.at[self.wide(self.core, t)], *self.sem(2, k), self.chip(t)
            ).wait()
            self.pass_on(t, self.core).start()

        repeat(1, self.nq, one)

    def finish(self):
        repeat(0, self.nq, lambda t: self.pass_on(t, 1 - self.core).wait())


class DeepSum:
    def __init__(self, nb, nx, x_ref, o_ref, got, half, recv, deep, deep_recv, sems):
        self.nx = nx
        self.n1, self.n2 = 2 * nx, nb // 4
        self.p = x_ref.shape[0] // (2 * self.n1 * self.n2)
        band = lax.axis_index("band")
        self.core = lax.rem(band, 2)
        self.j1 = lax.rem(band // 2, 2) * nx + lax.axis_index("batch")
        self.j2 = band // 4
        self.sibling = {"band": band + 1 - 2 * self.core}
        self.x, self.o, self.got, self.half, self.recv = x_ref, o_ref, got, half, recv
        self.deep, self.deep_recv = deep, deep_recv
        self.sems = sems

    def near(self, t):
        return {
            "band": self.j2 * 4 + (t // self.nx) * 2 + self.core,
            "batch": lax.rem(t, self.nx),
        }

    def far(self, t):
        return {"band": t * 4 + lax.rem(lax.axis_index("band"), 4)}

    def near_at(self, k):
        return lax.rem(self.j1 + k, self.n1)

    def far_at(self, k):
        return lax.rem(self.j2 + k, self.n2)

    def block(self, c, t):
        rows = self.n2 * self.p
        return pl.ds(pl.multiple_of((c * self.n1 + t) * rows, 16), rows)

    def thin(self, t):
        rows = self.n2 * self.p
        return pl.ds(pl.multiple_of(t * rows, 16), rows)

    def piece(self, t):
        return pl.ds(pl.multiple_of(t * self.p, 16), self.p)

    def o_piece(self, t):
        at = (self.core * self.n1 + self.j1) * self.n2 + t
        return self.o.at[pl.ds(pl.multiple_of(at * self.p, 16), self.p)]

    def sem(self, i, k):
        return self.sems.at[2 * i, k], self.sems.at[2 * i + 1, k]

    def pair_copy(self, t, side):
        return remote(
            self.x.at[self.block(side, t)], self.got.at[self.thin(t)], *self.sem(0, t), self.sibling
        )

    def start(self):
        repeat(1, self.n1 + 1, lambda k: self.pair_copy(self.near_at(k), 1 - self.core).start())

    def scatter(self):
        def one(k):
            t = self.near_at(k)
            self.pair_copy(t, self.core).wait()
            self.half[self.thin(t)] = (
                self.x[self.block(self.core, t)].astype(F32) + self.got[self.thin(t)].astype(F32)
            ).astype(BF16)

            @pl.when(k < self.n1)
            def _():
                remote(
                    self.half.at[self.thin(t)],
                    self.recv.at[self.thin(self.j1)],
                    *self.sem(1, k),
                    self.near(t),
                ).start()

        repeat(1, self.n1 + 1, one)

    def scatter_far(self):
        def one(k):
            t = self.near_at(self.n1 - k)
            remote(
                self.half.at[self.thin(t)],
                self.recv.at[self.thin(t)],
                *self.sem(1, k),
                self.near(t),
            ).wait()

        repeat(1, self.n1, one)
        total = self.half[self.thin(self.j1)].astype(F32)
        for k in range(1, self.n1):
            total = total + self.recv[self.thin(self.near_at(k))].astype(F32)
        self.deep[...] = total.astype(BF16)

        def give(k):
            t = self.far_at(k)
            remote(
                self.deep.at[self.piece(t)],
                self.deep_recv.at[self.piece(self.j2)],
                *self.sem(2, k),
                self.far(t),
            ).start()

        repeat(1, self.n2, give)

    def gather(self):
        def one(k):
            t = self.far_at(self.n2 - k)
            remote(
                self.deep.at[self.piece(t)],
                self.deep_recv.at[self.piece(t)],
                *self.sem(2, k),
                self.far(t),
            ).wait()

        repeat(1, self.n2, one)
        total = self.deep[self.piece(self.j2)].astype(F32)
        for k in range(1, self.n2):
            total = total + self.deep_recv[self.piece(self.far_at(k))].astype(F32)
        at = (self.core * self.n1 + self.j1) * self.n2 + self.j2
        self.o[pl.ds(pl.multiple_of(at * self.p, 16), self.p)] = total.astype(BF16)
        mine = self.o_piece(self.j2)
        repeat(
            1,
            self.n2,
            lambda k: remote(mine, mine, *self.sem(3, k), self.far(self.far_at(k))).start(),
        )

    def gather_near(self):
        def one(k):
            t = self.far_at(self.n2 - k)
            remote(self.o_piece(self.j2), self.o_piece(t), *self.sem(3, k), self.far(t)).wait()

        repeat(1, self.n2, one)
        mine = self.o.at[self.block(self.core, self.j1)]
        repeat(
            1,
            self.n1,
            lambda k: remote(mine, mine, *self.sem(4, k), self.near(self.near_at(k))).start(),
        )
        self.pass_on(self.j1, self.core).start()

    def pass_on(self, t, side):
        return remote(
            self.o.at[self.block(self.core, t)],
            self.o.at[self.block(side, t)],
            *self.sem(5, t),
            self.sibling,
        )

    def relay(self):
        def one(k):
            t = self.near_at(self.n1 - k)
            remote(
                self.o.at[self.block(self.core, self.j1)],
                self.o.at[self.block(self.core, t)],
                *self.sem(4, k),
                self.near(t),
            ).wait()
            self.pass_on(t, self.core).start()

        repeat(1, self.n1, one)

    def finish(self):
        repeat(0, self.n1, lambda t: self.pass_on(t, 1 - self.core).wait())


ROWS_A = 1536
ROWS_B = 2304
ROWS_G = 800


def up(rows, unit):
    return -(-rows // unit) * unit


def split_rows(ref, at, rows):
    n = rows.shape[0]
    high = rows.astype(BF16)
    ref[at : at + n, :] = high
    ref[at + n : at + 2 * n, :] = (rows - high.astype(F32)).astype(BF16)


def block_kernel(
    nb, nx, length,
    own_ref, x_ref, top_ref, wq_ref, wp_ref, w1_ref, w2_ref, vec_ref,
    out_ref, ing_ref, gb_ref, gav_ref, gah_ref,
    wa_in, wb_in, wa, wb, gb_in, gav_in, gah_in,
    wide_got, wide_half, wide_recv, wide_deep, wide_deep_recv, a_got, a_half, a_recv,
    gb_got, gb_half, gb_recv, gb_deep, gb_deep_recv,
    v_got, v_half, v_recv, v_deep, v_deep_recv, h_got, h_half, h_recv,
    hot_in, hot_out, x_out, x_in, a_out, a_in, g_out, g_in, p_out, p_in,
    xs, qa, ks, vs, os, att, n2, acc, gn, gm, grad_h, part_h,
    gp, g1, g2, rows_mid, gw_v, gw_h, rows_v, rows_h, da,
    x_ss, x_rs, a_ss, a_rs, g_ss, g_rs, p_ss, p_rs,
    wa_sem, wb_sem, gb_sem, gav_sem, gah_sem,
):
    band = lax.axis_index("band")
    batch = lax.axis_index("batch")
    device = band * nx + batch
    micro = x_ref.shape[0]
    core = lax.rem(band, 2)
    bar = pltpu.get_barrier_semaphore()
    repeat(
        1,
        nb,
        lambda k: pl.semaphore_signal(
            bar, inc=1, device_id={"band": lax.rem(band + k, nb)}, device_id_type=MESH
        ),
    )

    def greet(t):
        other = lax.rem(batch + 1 + t // (nb // 2), nx)
        pl.semaphore_signal(
            bar,
            inc=1,
            device_id={"band": lax.rem(t, nb // 2) * 2 + core, "batch": other},
            device_id_type=MESH,
        )

    repeat(0, (nb // 2) * (nx - 1), greet)

    sum_wa = Sum(nb, nx, wa_in, wa, a_got, a_half, a_recv, wa_sem)
    sum_wb = DeepSum(
        nb, nx, wb_in, wb, wide_got, wide_half, wide_recv, wide_deep, wide_deep_recv, wb_sem
    )
    sum_gb = DeepSum(
        nb, nx, gb_in, gb_ref, gb_got, gb_half, gb_recv, gb_deep, gb_deep_recv, gb_sem
    )
    sum_gav = DeepSum(
        nb, nx, gav_in, gav_ref, v_got, v_half, v_recv, v_deep, v_deep_recv, gav_sem
    )
    sum_gah = Sum(nb, nx, gah_in, gah_ref, h_got, h_half, h_recv, gah_sem)
    swap_x = Swap(nb, x_out, x_in, x_ss, x_rs)
    swap_a = Swap(nb, a_out, a_in, a_ss, a_rs)
    swap_g = Swap(nb, g_out, g_in, g_ss, g_rs)
    swap_p = Swap(nb, p_out, p_in, p_ss, p_rs)

    def own(ref, which, cols):
        return jnp.where(own_ref[which] == device, ref[0, :, cols], 0.0).astype(BF16)

    for b in range(6):
        wa_in[256 * b : 256 * b + 256, :] = own(wq_ref, 0, slice(128 * b, 128 * b + 128))
    if wa_in.shape[0] > ROWS_A:
        wa_in[ROWS_A:, :] = jnp.zeros((wa_in.shape[0] - ROWS_A, 128), BF16)
    pl.semaphore_wait(bar, nb - 1 + (nb // 2) * (nx - 1))
    sum_wa.start()
    wb_in[0:256, :] = own(wp_ref, 1, slice(0, 256))
    for f in range(4):
        wb_in[256 * (f + 1) : 256 * (f + 2), :] = own(w1_ref, 2, slice(256 * f, 256 * f + 256))
    wb_in[1280:ROWS_B, :] = own(w2_ref, 3, slice(0, 256))
    wb_in[ROWS_B:, :] = jnp.zeros((wb_in.shape[0] - ROWS_B, 256), BF16)
    sum_wa.scatter()
    hot_out[...] = order_out(nb, length)
    x_out[0] = mm(hot_out[...], x_ref[0]).astype(BF16)
    sum_wa.gather()
    swap_x.send(0)
    sum_wb.start()
    hot_in[...] = order_in(nb, length)
    for ref in (gp, g1, g2, rows_mid, gw_v, gw_h, rows_v, rows_h):
        ref[...] = jnp.zeros_like(ref)
    for m in range(1, micro):
        x_out[m] = mm(hot_out[...], x_ref[m]).astype(BF16)
    sum_wa.relay()
    for m in range(1, micro):
        swap_x.send(m)
    sum_wb.scatter()
    sum_wa.finish()

    def blocks(half):
        return lambda b: wa[256 * (2 * b + half) : 256 * (2 * b + half) + 256, :]

    def forward_h(m):
        attention_forward(
            x_ref[m].astype(F32), 0, length, blocks(0), vec_ref,
            qa.at[m], ks.at[m], vs.at[m], os.at[m], att.at[m, :, pl.ds(0, 128)],
        )

    def forward_v(m):
        swap_x.wait(m)
        xs[m] = mm(hot_in[...], x_in[m]).astype(BF16)
        w = micro + m
        attention_forward(
            xs[m].astype(F32), 1, length, blocks(1), vec_ref,
            qa.at[w], ks.at[w], vs.at[w], os.at[w], att.at[m, :, pl.ds(128, 128)],
        )
        a_out[m] = mm(hot_out[...], att[m, :, 128:256]).astype(BF16)
        swap_a.send(m)

    def forward_step(i):
        @pl.when((i == 0) | (i > micro))
        def _():
            forward_h(jnp.where(i == 0, 0, i - micro))

        @pl.when((i > 0) & (i <= micro))
        def _():
            forward_v(i - 1)

        @pl.when(i == 0)
        def _():
            sum_wb.scatter_far()

        @pl.when(i == 1)
        def _():
            sum_wb.gather()
            sum_wb.gather_near()

        @pl.when(i == 2)
        def _():
            sum_wb.relay()

    repeat(0, 2 * micro, forward_step)
    sum_wb.finish()

    def middle_step(m):
        swap_a.wait(m)
        att[m, :, 128:256] = mm(hot_in[...], a_in[m]).astype(BF16)
        out, grad_middle, grad_att = feed_forward(
            x_ref[m].astype(F32), att[m], top_ref[m], wb, 0, vec_ref, n2, acc, gn,
            gp, g1, g2, rows_mid,
        )
        out_ref[m] = out
        gm[m] = grad_middle
        grad_h[m] = grad_att[:, 0:128]
        g_out[m] = mm(hot_out[...], grad_att[:, 128:256]).astype(BF16)
        swap_g.send(m)

    repeat(0, micro, middle_step)
    gb_in[0:256, :] = jnp.transpose(gp[...]).astype(BF16)
    for f in range(4):
        cols = slice(256 * f, 256 * f + 256)
        gb_in[256 * (f + 1) : 256 * (f + 2), :] = g1[:, cols].astype(BF16)
        gb_in[1280 + 256 * f : 1536 + 256 * f, :] = jnp.transpose(g2[:, cols]).astype(BF16)
    gb_in[ROWS_B:, :] = jnp.zeros((gb_in.shape[0] - ROWS_B, 256), BF16)
    split_rows(gb_in, ROWS_B, rows_mid[...])
    sum_gb.start()

    def backward_v(m):
        swap_g.wait(m)
        w = micro + m
        grad_in = mm(hot_in[...], g_in[m]).astype(BF16)
        part = attention_backward(
            xs[m].astype(F32), 1, length, grad_in, blocks(1), vec_ref,
            qa.at[w], ks.at[w], vs.at[w], os.at[w], da, gw_v, rows_v,
        )
        p_out[m] = mm(hot_out[...], part.astype(BF16)).astype(BF16)
        swap_p.send(m)

        @pl.when(m == 0)
        def _():
            sum_gb.scatter()

    repeat(0, micro, backward_v)
    sum_gb.scatter_far()

    def fill(ref, gw, rows):
        for b in range(3):
            ref[256 * b : 256 * b + 256, :] = gw[:, 128 * b : 128 * b + 128].astype(BF16)
        split_rows(ref, 768, rows[...])
        ref[ROWS_G:, :] = jnp.zeros((ref.shape[0] - ROWS_G, 128), BF16)

    fill(gav_in, gw_v, rows_v)
    sum_gav.start()

    def backward_h(m):
        part_h[m] = attention_backward(
            x_ref[m].astype(F32), 0, length, grad_h[m], blocks(0), vec_ref,
            qa.at[m], ks.at[m], vs.at[m], os.at[m], da, gw_h, rows_h,
        )

        @pl.when(m == 0)
        def _():
            sum_gb.gather()
            sum_gav.scatter()
            sum_gb.gather_near()
            sum_gav.scatter_far()

    repeat(0, micro, backward_h)
    fill(gah_in, gw_h, rows_h)
    sum_gah.start()
    sum_gav.gather()
    sum_gah.scatter()
    sum_gb.relay()
    sum_gav.gather_near()
    sum_gb.finish()

    def last_step(m):
        swap_p.wait(m)
        grad_normed = part_h[m] + mm(hot_in[...], p_in[m])
        unit, inverse = unit_rows(x_ref[m].astype(F32))
        ing_ref[m] = (gm[m] + norm_back(grad_normed, vec_ref[0:1], unit, inverse)).astype(BF16)

    last_step(0)
    sum_gah.gather()
    sum_gav.relay()
    repeat(1, micro, last_step)
    sum_gah.relay()
    sum_gav.finish()
    sum_gah.finish()


def block_call(x, top, owners, w_qkv, w_proj, w_fc1, w_fc2, vectors, nb, nx, length):
    micro, tokens, _ = x.shape
    packed = nb * PIECE
    nq = nb // 2 * nx
    unit = 32 * nq
    ra, rb, rg = up(ROWS_A, unit), up(ROWS_B + 16, unit), up(ROWS_G, unit)
    vm = pltpu.VMEM
    windows = 2 * micro

    def steps(rows, cols):
        return [vm((rows // 2, cols), BF16)] * 3

    def deep_steps(rows, cols):
        return steps(rows, cols) + [vm((rows // (4 * nx), cols), BF16)] * 2

    scratch = (
        [vm((ra, 128), BF16), vm((rb, 256), BF16), vm((ra, 128), BF16), vm((rb, 256), BF16)]
        + [vm((rb, 256), BF16), vm((rg, 128), BF16), vm((rg, 128), BF16)]
        + deep_steps(rb, 256) + steps(ra, 128) + deep_steps(rb, 256) + deep_steps(rg, 128)
        + steps(rg, 128)
        + [vm((tokens, packed), BF16), vm((packed, tokens), BF16)]
        + [vm((micro, packed, 256), BF16)] * 2
        + [vm((micro, packed, 128), BF16)] * 4
        + [vm((micro, packed, 256), BF16)] * 2
        + [
            vm((micro, tokens, 256), BF16),
            vm((windows, tokens, 256), BF16),
            vm((windows, tokens, 128), BF16),
            vm((windows, tokens, 128), BF16),
            vm((windows, tokens, 128), F32),
            vm((micro, tokens, 256), BF16),
            vm((tokens, 256), BF16),
            vm((tokens, 256), F32),
            vm((tokens, 256), F32),
            vm((micro, tokens, 256), F32),
            vm((micro, tokens, 128), BF16),
            vm((micro, tokens, 256), F32),
            vm((256, 256), F32),
            vm((256, 1024), F32),
            vm((256, 1024), F32),
            vm((8, 256), F32),
            vm((256, 384), F32),
            vm((256, 384), F32),
            vm((16, 128), F32),
            vm((16, 128), F32),
            vm((tokens, 256), BF16),
        ]
        + [pltpu.SemaphoreType.DMA((micro, nb))] * 8
        + [pltpu.SemaphoreType.DMA((12, nq))] * 5
    )
    whole_vmem = pl.BlockSpec(memory_space=vm)
    return pl.pallas_call(
        functools.partial(block_kernel, nb, nx, length),
        in_specs=[pl.BlockSpec(memory_space=pltpu.SMEM)] + [whole_vmem] * 7,
        out_specs=[whole_vmem] * 5,
        out_shape=[
            shape_of(BF16, micro, tokens, 256), shape_of(BF16, micro, tokens, 256),
            shape_of(BF16, rb, 256), shape_of(BF16, rg, 128), shape_of(BF16, rg, 128),
        ],
        scratch_shapes=scratch,
        compiler_params=pltpu.CompilerParams(
            collective_id=0, has_side_effects=True, vmem_limit_bytes=VMEM_LIMIT
        ),
        name="block",
    )(owners, x, top, w_qkv, w_proj, w_fc1, w_fc2, vectors)


def parts_of(a):
    high = a.astype(BF16)
    return high, (a - high.astype(F32)).astype(BF16)


def careful(op, a, b):
    ah, al = parts_of(a)
    bh, bl = parts_of(b)
    return op(ah, bh) + (op(ah, bl) + op(al, bh))


def adam_kernel(
    vrows, rows,
    own_ref, gb_ref, gav_ref, gah_ref, vec_ref, vf_ref, vs_ref, *refs,
):
    moments = refs[0:12]
    bases = refs[12:20]
    grads = refs[20:24]
    outs = refs[24:36]
    vg_ref, vfn_ref, vsn_ref, vn_ref = refs[36:40]
    held = refs[40:52]
    left = refs[52:60]
    zeros_ref, in_sem, out_sem = refs[60:63]
    device = lax.axis_index("band") * lax.axis_size("batch") + lax.axis_index("batch")
    is_own = [own_ref[i] == device for i in range(4)]

    def load(i):
        pairs = [(moments[3 * i + j].at[0], held[3 * i + j], 5 * i + j) for j in range(3)]
        pairs += [(bases[2 * i + j], left[2 * i + j], 5 * i + 3 + j) for j in range(2)]
        return [pltpu.make_async_copy(a, b, in_sem.at[s]) for a, b, s in pairs]

    def store(i):
        return [
            pltpu.make_async_copy(held[3 * i + j], outs[3 * i + j].at[0], out_sem.at[3 * i + j])
            for j in range(3)
        ]

    def blank(i):
        copies = []
        for j in range(3):
            shape = outs[3 * i + j].shape
            copies.append(
                pltpu.make_async_copy(
                    zeros_ref.at[pl.ds(0, shape[1]), pl.ds(0, shape[2])],
                    outs[3 * i + j].at[0],
                    out_sem.at[3 * i + j],
                )
            )
        return copies

    for i in range(4):
        @pl.when(is_own[i])
        def _():
            for c in load(i):
                c.start()

    zeros_ref[...] = jnp.zeros_like(zeros_ref)
    for i in range(4):
        @pl.when(jnp.logical_not(is_own[i]))
        def _():
            for c in blank(i):
                c.start()

    for b in range(3):
        for half, ref in ((0, gah_ref), (1, gav_ref)):
            at = 256 * b + 128 * half
            grads[0][:, at : at + 128] = ref[256 * b : 256 * b + 256, :].astype(F32)
    grads[1][...] = gb_ref[0:256, :].astype(F32)
    for f in range(4):
        grads[2][:, 256 * f : 256 * f + 256] = gb_ref[256 * (f + 1) : 256 * (f + 2), :].astype(F32)
    grads[3][...] = gb_ref[1280:ROWS_B, :].astype(F32)

    mid = gb_ref[ROWS_B : ROWS_B + 8, :].astype(F32) + gb_ref[ROWS_B + 8 : ROWS_B + 16, :].astype(F32)
    side = [r[768:784, :].astype(F32) + r[784:800, :].astype(F32) for r in (gah_ref, gav_ref)]
    both = side[0] + side[1]
    for i in range(2):
        vg_ref[0:1, 128 * i : 128 * i + 128] = both[12 + i : 13 + i]
        vg_ref[1:2, 128 * i : 128 * i + 128] = both[14 + i : 15 + i]
        vg_ref[2:4, 128 * i : 128 * i + 128] = side[i][0:2]
        vg_ref[12:22, 128 * i : 128 * i + 128] = side[i][2:12]
    vg_ref[4:12, :] = mid
    grad = vg_ref[...]
    first_new = BETA_ONE * vf_ref[...] + (1.0 - BETA_ONE) * grad
    second_new = BETA_TWO * vs_ref[...] + (1.0 - BETA_TWO) * grad * grad
    vfn_ref[...] = first_new
    vsn_ref[...] = second_new
    vn_ref[...] = vec_ref[...] - RATE_VECTORS * (first_new / (1.0 - BETA_ONE**STEP)) / (
        jnp.sqrt(second_new / (1.0 - BETA_TWO**STEP)) + EPS_ADAM
    )

    for i in range(4):
        @pl.when(is_own[i])
        def _():
            for c in load(i):
                c.wait()
            first, second, weight = held[3 * i], held[3 * i + 1], held[3 * i + 2]
            lb, rb = left[2 * i], left[2 * i + 1]
            g = grads[i][...].astype(BF16)
            lh, ll = parts_of(lb[...])
            if i == 3:
                once = jnp.transpose(mm_tn(g, lh) + mm_tn(g, ll))
            else:
                once = mm_tn(lh, g) + mm_tn(ll, g)
            turned = careful(mm, once, rb[...])
            first_new = BETA_ONE * first[...] + (1.0 - BETA_ONE) * turned
            second_new = BETA_TWO * second[...] + (1.0 - BETA_TWO) * turned * turned
            first[...] = first_new
            second[...] = second_new
            step = (first_new / (1.0 - BETA_ONE**STEP)) / (
                jnp.sqrt(second_new / (1.0 - BETA_TWO**STEP)) + EPS_ADAM
            )
            back = mm_nt(mm(lh, step.astype(BF16)).astype(BF16), rb[...].astype(BF16))
            weight[...] = weight[...] - RATE * back - RATE * DECAY * weight[...]
            for c in store(i):
                c.start()

    for i in range(4):
        for c in store(i):
            c.wait()


def adam_call(owners, gb, gav, gah, vectors, vectors_first, vectors_second, slots, bases):
    vm = pltpu.VMEM
    any_space = pl.BlockSpec(memory_space=pl.ANY)
    vspec = pl.BlockSpec(memory_space=vm)
    sizes = [(s.shape[1], s.shape[2]) for s in slots[::3]]
    vshape = shape_of(F32, *vectors.shape)
    tallest = max(a for a, _ in sizes)
    widest = max(b for _, b in sizes)
    return pl.pallas_call(
        functools.partial(adam_kernel, vectors.shape[0], None),
        in_specs=[pl.BlockSpec(memory_space=pltpu.SMEM)] + [vspec] * 6 + [any_space] * 20,
        out_specs=[vspec] * 4 + [any_space] * 12 + [vspec] * 4,
        out_shape=[shape_of(F32, *s) for s in sizes]
        + [shape_of(F32, *s.shape) for s in slots]
        + [vshape] * 4,
        scratch_shapes=[vm((s.shape[1], s.shape[2]), F32) for s in slots]
        + [vm(b.shape, F32) for b in bases]
        + [vm((tallest, widest), F32), pltpu.SemaphoreType.DMA((20,)), pltpu.SemaphoreType.DMA((12,))],
        compiler_params=pltpu.CompilerParams(vmem_limit_bytes=VMEM_LIMIT),
        name="adam",
    )(owners, gb, gav, gah, vectors, vectors_first, vectors_second, *slots, *bases)


def wide_to_stack(w):
    n = w.shape[1] // 256
    return w.reshape(256, n, 256).transpose(1, 0, 2).reshape(256 * n, 256)


def by_steps(x, top, owners, slots, vectors, nb, nx, length):
    device_index = lax.axis_index(("band", "batch"))

    def own(slot, which):
        return jnp.where(device_index == owners[which], slot[0], 0.0).astype(BF16)

    stacked = jnp.concatenate(
        [
            wide_to_stack(own(slots[0], 0)),
            own(slots[1], 1),
            wide_to_stack(own(slots[2], 2)),
            own(slots[3], 3),
        ],
        axis=0,
    )
    weights = sum_everywhere(stacked, nb, nx, 0)[:ROW_END]

    def swap(packed, cid):
        m, rows, ch = packed.shape
        swapped = packed.reshape(m, nb, PIECE, ch).transpose(1, 0, 2, 3).reshape(m * rows, ch)
        got = exchange(swapped, nb, cid)
        return got.reshape(nb, m, PIECE, ch).transpose(1, 0, 2, 3).reshape(m, rows, ch)

    columns = swap(pack_tokens(x, nb, length), 1)
    qa_v, k_v, v_v, o_v, att_v, x_v = forward_call(columns, 1, nb, length, weights, vectors)
    qa_h, k_h, v_h, o_h, att_h = forward_call(x, 0, nb, length, weights, vectors)
    att_v = swap(att_v, 2)
    block_out, grad_middle, grad_h, grad_v, gp_t, g1, g2_t, rows_mid = middle_call(
        x, att_h, att_v, top, nb, length, weights, vectors
    )
    grad_v = swap(grad_v, 3)
    part_v, gw_v, rows_v = backward_call(
        x_v, grad_v, qa_v, k_v, v_v, o_v, 1, nb, length, weights, vectors
    )
    part_h, gw_h, rows_h = backward_call(
        x, grad_h, qa_h, k_h, v_h, o_h, 0, nb, length, weights, vectors
    )
    part_v = swap(part_v, 4)
    input_grad = last_call(x, grad_middle, part_h, part_v, nb, length, vectors)

    def two(rows):
        high = rows.astype(BF16)
        return [high, (rows - high.astype(F32)).astype(BF16)]

    gb = jnp.concatenate(
        [gp_t.T.astype(BF16), wide_to_stack(g1.astype(BF16)), g2_t.T.astype(BF16)] + two(rows_mid),
        axis=0,
    )

    def side(gw, rows):
        return jnp.concatenate(
            [gw[:, 128 * b : 128 * b + 128].astype(BF16) for b in range(3)] + two(rows), axis=0
        )

    gb = sum_everywhere(gb, nb, nx, 5)
    gav = sum_everywhere(side(gw_v, rows_v), nb, nx, 6)
    gah = sum_everywhere(side(gw_h, rows_h), nb, nx, 7)
    return block_out, input_grad, gb, gav, gah


def per_device(
    tokens_in, cotangent, owners,
    weight_qkv, weight_proj, weight_fc1, weight_fc2,
    first_qkv, second_qkv, first_proj, second_proj, first_fc1, second_fc1, first_fc2, second_fc2,
    left_qkv, right_qkv, left_proj, right_proj, left_fc1, right_fc1, left_fc2, right_fc2,
    vectors, vectors_first, vectors_second,
    *, nb, nx,
):
    micro, images, band_rows, length, channels = tokens_in.shape
    tokens = band_rows * length
    x = tokens_in.reshape(micro * images, tokens, channels)
    top = cotangent.reshape(micro * images, tokens, channels)
    weights = (weight_qkv, weight_proj, weight_fc1, weight_fc2)
    if tokens <= LONGEST:
        block_out, input_grad, gb, gav, gah = block_call(
            x, top, owners, *weights, vectors, nb, nx, length
        )
    else:
        block_out, input_grad, gb, gav, gah = by_steps(
            x, top, owners, weights, vectors, nb, nx, length
        )
    slots = (
        first_qkv, second_qkv, weight_qkv, first_proj, second_proj, weight_proj,
        first_fc1, second_fc1, weight_fc1, first_fc2, second_fc2, weight_fc2,
    )
    bases = (left_qkv, right_qkv, left_proj, right_proj, left_fc1, right_fc1, left_fc2, right_fc2)
    done = adam_call(
        owners, gb, gav, gah, vectors, vectors_first, vectors_second, slots, bases
    )
    results = [block_out.reshape(tokens_in.shape), input_grad.reshape(tokens_in.shape)]
    for i in range(4):
        results.append(done[i])
        results += list(done[4 + 3 * i : 7 + 3 * i])
    return tuple(results) + tuple(done[16:20])


def solution(mesh):
    tokens_spec = P(None, "batch", "band", None, None)
    slot_spec = P(("band", "batch"), None, None)
    return jax.shard_map(
        functools.partial(per_device, nb=mesh.shape["band"], nx=mesh.shape["batch"]),
        mesh=mesh,
        in_specs=(tokens_spec, tokens_spec, P()) + (slot_spec,) * 12 + (P(),) * 11,
        out_specs=(tokens_spec, tokens_spec)
        + (P(), slot_spec, slot_spec, slot_spec) * 4
        + (P(),) * 4,
        check_vma=False,
    )
```

```python
import functools

import jax
import jax.numpy as jnp
from jax import lax
from jax.experimental import pallas as pl
from jax.experimental.pallas import tpu as pltpu
from jax.sharding import PartitionSpec as P

HEAD_DIM = 32
STRIPE = 7
STEP = 10
EPS_NORM = 1e-05
BETA_ONE = 0.5
BETA_TWO = 0.6
RATE = 0.04
RATE_VECTORS = 0.2
DECAY = 0.01
EPS_ADAM = 1e-08
MESH = pl.DeviceIdType.MESH
F32 = jnp.float32
BF16 = jnp.bfloat16
PIECE = 64
LOG2E = 1.4426950408889634
LN2 = 0.6931471805599453
Q_SCALE = LOG2E * HEAD_DIM**-0.5
LONGEST = 1024
VMEM_LIMIT = 60 * 1024 * 1024
ROW_QKV, ROW_PROJ, ROW_FC1, ROW_FC2, ROW_END = 0, 768, 1024, 2048, 3072


def mm(a, b):
    return lax.dot_general(a, b, (((1,), (0,)), ((), ())), preferred_element_type=F32)


def mm_nt(a, b):
    return lax.dot_general(a, b, (((1,), (1,)), ((), ())), preferred_element_type=F32)


def mm_tn(a, b):
    return lax.dot_general(a, b, (((0,), (0,)), ((), ())), preferred_element_type=F32)


def exchange_kernel(n, piece, x_ref, o_ref, send_sem, recv_sem, loc_sem):
    me = lax.axis_index("band")
    bar = pltpu.get_barrier_semaphore()

    def greet(k, c):
        pl.semaphore_signal(
            bar, inc=1, device_id={"band": lax.rem(me + k, n)}, device_id_type=MESH
        )
        return c

    lax.fori_loop(1, n, greet, 0)
    pl.semaphore_wait(bar, n - 1)

    def rows(i):
        return pl.ds(pl.multiple_of(i * piece, piece), piece)

    def send(k, c):
        d = lax.rem(me + k, n)
        pltpu.make_async_remote_copy(
            src_ref=x_ref.at[rows(d)],
            dst_ref=o_ref.at[rows(me)],
            send_sem=send_sem.at[k],
            recv_sem=recv_sem.at[k],
            device_id={"band": d},
            device_id_type=MESH,
        ).start()
        return c

    lax.fori_loop(1, n, send, 0)
    local = pltpu.make_async_copy(x_ref.at[rows(me)], o_ref.at[rows(me)], loc_sem)
    local.start()
    local.wait()

    def take(k, c):
        s = lax.rem(me - k + n, n)
        pltpu.make_async_remote_copy(
            src_ref=x_ref.at[rows(s)],
            dst_ref=o_ref.at[rows(s)],
            send_sem=send_sem.at[k],
            recv_sem=recv_sem.at[k],
            device_id={"band": s},
            device_id_type=MESH,
        ).wait()
        return c

    lax.fori_loop(1, n, take, 0)


def exchange(x, n, cid):
    return pl.pallas_call(
        functools.partial(exchange_kernel, n, x.shape[0] // n),
        out_shape=jax.ShapeDtypeStruct(x.shape, x.dtype),
        in_specs=[pl.BlockSpec(memory_space=pltpu.VMEM)],
        out_specs=pl.BlockSpec(memory_space=pltpu.VMEM),
        scratch_shapes=[
            pltpu.SemaphoreType.DMA((n,)),
            pltpu.SemaphoreType.DMA((n,)),
            pltpu.SemaphoreType.DMA,
        ],
        compiler_params=pltpu.CompilerParams(
            collective_id=cid, has_side_effects=True, vmem_limit_bytes=VMEM_LIMIT
        ),
        name="exchange",
    )(x)


def sum_kernel(nb, nx, total_rows, x_ref, o_ref, got, half, recv, s1, r1, s2, r2, s3, r3, s4, r4):
    nq = (nb // 2) * nx
    p = total_rows // (2 * nq)
    band = lax.axis_index("band")
    core = lax.rem(band, 2)
    q = (band // 2) * nx + lax.axis_index("batch")
    sibling = {"band": band + 1 - 2 * core}
    bar = pltpu.get_barrier_semaphore()

    def chip(t):
        return {"band": (t // nx) * 2 + core, "batch": lax.rem(t, nx)}

    def ahead(k):
        return lax.rem(q + k, nq)

    def behind(k):
        return lax.rem(q - k + nq, nq)

    def copy(src, dst, ss, rs, dev):
        return pltpu.make_async_remote_copy(
            src_ref=src, dst_ref=dst, send_sem=ss, recv_sem=rs, device_id=dev, device_id_type=MESH
        )

    def loop(lo, hi, body):
        def step(k, c):
            body(k)
            return c

        lax.fori_loop(lo, hi, step, 0)

    pl.semaphore_signal(bar, inc=1, device_id=sibling, device_id_type=MESH)
    loop(
        1,
        nq,
        lambda k: pl.semaphore_signal(
            bar, inc=1, device_id=chip(ahead(k)), device_id_type=MESH
        ),
    )
    pl.semaphore_wait(bar, nq)

    def whole_rows(c, t):
        return pl.ds(pl.multiple_of((c * nq + t) * p, 16), p)

    def half_rows(t):
        return pl.ds(pl.multiple_of(t * p, 16), p)

    def pair_copy(k, side):
        t = ahead(k)
        return copy(
            x_ref.at[whole_rows(side, t)], got.at[half_rows(t)], s1.at[t], r1.at[t], sibling
        )

    loop(1, nq + 1, lambda k: pair_copy(k, 1 - core).start())

    def scatter_copy(k):
        t = ahead(k)
        return copy(half.at[half_rows(t)], recv.at[half_rows(q)], s2.at[k], r2.at[k], chip(t))

    def pair_sum(k):
        t = ahead(k)
        pair_copy(k, core).wait()
        half[half_rows(t)] = (
            x_ref[whole_rows(core, t)].astype(F32) + got[half_rows(t)].astype(F32)
        ).astype(BF16)

        @pl.when(k < nq)
        def _():
            scatter_copy(k).start()

    loop(1, nq + 1, pair_sum)

    def add_piece(k, acc):
        t = behind(k)
        copy(half.at[half_rows(t)], recv.at[half_rows(t)], s2.at[k], r2.at[k], chip(t)).wait()
        return acc + recv[half_rows(t)].astype(F32)

    total = lax.fori_loop(1, nq, add_piece, half[half_rows(q)].astype(F32))
    mine = o_ref.at[whole_rows(core, q)]
    o_ref[whole_rows(core, q)] = total.astype(BF16)

    def gather_copy(k):
        return copy(mine, mine, s3.at[k], r3.at[k], chip(ahead(k)))

    def pass_on(t, side):
        return copy(
            o_ref.at[whole_rows(core, t)],
            o_ref.at[whole_rows(side, t)],
            s4.at[t],
            r4.at[t],
            sibling,
        )

    loop(1, nq, lambda k: gather_copy(k).start())
    pass_on(q, core).start()

    def relay(k):
        t = behind(k)
        copy(mine, o_ref.at[whole_rows(core, t)], s3.at[k], r3.at[k], chip(t)).wait()
        pass_on(t, core).start()

    loop(1, nq, relay)
    loop(0, nq, lambda t: pass_on(t, 1 - core).wait())


def sum_everywhere(x, nb, nx, cid):
    rows, cols = x.shape
    nq = nb // 2 * nx
    unit = 32 * nq
    padded = -(-rows // unit) * unit
    if padded != rows:
        x = jnp.concatenate([x, jnp.zeros((padded - rows, cols), x.dtype)], axis=0)
    sems = [pltpu.SemaphoreType.DMA((nq,)) for _ in range(8)]
    out = pl.pallas_call(
        functools.partial(sum_kernel, nb, nx, padded),
        out_shape=jax.ShapeDtypeStruct(x.shape, x.dtype),
        in_specs=[pl.BlockSpec(memory_space=pltpu.VMEM)],
        out_specs=pl.BlockSpec(memory_space=pltpu.VMEM),
        scratch_shapes=[pltpu.VMEM((padded // 2, cols), x.dtype)] * 3 + sems,
        compiler_params=pltpu.CompilerParams(
            collective_id=cid, has_side_effects=True, vmem_limit_bytes=VMEM_LIMIT
        ),
        name="sum_everywhere",
    )(x)
    return out


def order_out(pieces_n, length):
    row = lax.broadcasted_iota(jnp.int32, (pieces_n * PIECE, 1), 0)
    s = row // PIECE
    m = row % PIECE
    a = (m * 37) // 256
    b = m - STRIPE * a
    token = jnp.where(m < STRIPE * STRIPE, a * length + STRIPE * s + b, -1)
    column = lax.broadcasted_iota(jnp.int32, (pieces_n * PIECE, STRIPE * length), 1)
    return jnp.where(column == token, 1.0, 0.0).astype(BF16)


def order_in(pieces_n, length):
    row = lax.broadcasted_iota(jnp.int32, (1, pieces_n * PIECE), 1)
    s = row // PIECE
    m = row % PIECE
    a = (m * 37) // 256
    b = m - STRIPE * a
    token = jnp.where(m < STRIPE * STRIPE, b * length + STRIPE * s + a, -1)
    column = lax.broadcasted_iota(jnp.int32, (STRIPE * length, pieces_n * PIECE), 0)
    return jnp.where(column == token, 1.0, 0.0).astype(BF16)


def unit_rows(values):
    centred = values - jnp.mean(values, axis=-1, keepdims=True)
    inverse = lax.rsqrt(jnp.mean(centred * centred, axis=-1, keepdims=True) + EPS_NORM)
    return centred * inverse, inverse


def norm_back(grad_normed, gain, unit, inverse):
    scaled = grad_normed * gain
    first_mean = jnp.mean(scaled, axis=-1, keepdims=True)
    second_mean = jnp.mean(scaled * unit, axis=-1, keepdims=True)
    return inverse * (scaled - first_mean - unit * second_mean)


def shifted_columns(v, length):
    tokens = v.shape[0]
    column = lax.broadcasted_iota(jnp.int32, v.shape, 0) % length
    before = jnp.where(column == 0, 0.0, pltpu.roll(v, 1, 0))
    after = jnp.where(column == length - 1, 0.0, pltpu.roll(v, tokens - 1, 0))
    return before, v, after


def shifted_rows(v, length):
    zeros = jnp.zeros((length, v.shape[1]), v.dtype)
    above = jnp.concatenate([zeros, v[: v.shape[0] - length]], axis=0)
    below = jnp.concatenate([v[length:], zeros], axis=0)
    return above, v, below


def tap_row(half, a, b):
    return 12 + (3 * a + b if half == 0 else 3 * b + a)


def conv(v, vec_ref, lanes, half, length, flipped):
    total = jnp.zeros_like(v)
    for b, col in enumerate(shifted_columns(v, length)):
        for a, val in enumerate(shifted_rows(col, length)):
            row = tap_row(half, 2 - a, 2 - b) if flipped else tap_row(half, a, b)
            total = total + val * vec_ref[row : row + 1, lanes]
    return total


def head_mask(shape, h, offset=0):
    lane = lax.broadcasted_iota(jnp.int32, shape, len(shape) - 1) - offset
    return (lane >= h * HEAD_DIM) & (lane < (h + 1) * HEAD_DIM)


def three_parts(x):
    lane = lax.broadcasted_iota(jnp.int32, x.shape, len(x.shape) - 1) % HEAD_DIM
    hi = x.astype(BF16).astype(F32)
    mid = (x - hi).astype(BF16).astype(F32)
    low = x - hi - mid
    parts = jnp.where(lane == 0, hi, jnp.where(lane == 1, mid, jnp.where(lane == 2, low, 0.0)))
    return parts.astype(BF16)


def head_lanes(h, width):
    lane = lax.broadcasted_iota(jnp.int32, (1, width), 1) % 128
    keep = (lane >= h * HEAD_DIM) & (lane < (h + 1) * HEAD_DIM)
    return jnp.where(keep, 1.0, 0.0).astype(BF16)


def beside_parts(block):
    lane = lax.broadcasted_iota(jnp.int32, block.shape, 1) % HEAD_DIM
    return jnp.concatenate([block, jnp.where(lane < 3, 1.0, 0.0).astype(BF16)], axis=1)


def turned(block):
    return jnp.transpose(block.astype(F32)).astype(BF16)


def lane_blocks(w_ref, half):
    return lambda b: w_ref[256 * b : 256 * b + 256, 128 * half : 128 * half + 128]


def attention_forward(x, half, length, wb, vec_ref, qa_ref, k_ref, v_ref, o_ref, att_ref):
    tokens = x.shape[0]
    lanes = slice(128 * half, 128 * half + 128)
    unit, _ = unit_rows(x)
    normed = (unit * vec_ref[0:1] + vec_ref[1:2]).astype(BF16)
    q = (mm(normed, wb(0)) + vec_ref[2:3, lanes]) * Q_SCALE
    qa_ref[:, 0:128] = q.astype(BF16)
    k_ref[...] = mm(normed, wb(1)).astype(BF16)
    v = (mm(normed, wb(2)) + vec_ref[3:4, lanes]).astype(BF16)
    v_ref[...] = v
    v_turned = turned(v)
    ones = jnp.ones((HEAD_DIM, tokens), BF16)

    def head_scores(h):
        return mm_nt(k_ref[...] * head_lanes(h, 128), qa_ref[:, 0:128])

    following = head_scores(0)
    weighted, totals, tops = [], [], []
    for h in range(4):
        scores = following
        if h < 3:
            following = head_scores(h + 1)
        highest = jnp.max(scores, axis=0, keepdims=True)
        probs = jnp.exp2(scores - highest).astype(BF16)
        rows = slice(HEAD_DIM * h, HEAD_DIM * h + HEAD_DIM)
        both = mm(jnp.concatenate([v_turned[rows], ones], axis=0), probs)
        weighted.append(both[:HEAD_DIM])
        totals.append(both[HEAD_DIM:])
        tops.append(jnp.broadcast_to(highest, (HEAD_DIM, tokens)))
    total = jnp.concatenate(totals, axis=0)
    attended = jnp.transpose(jnp.concatenate(weighted, axis=0) / total)
    o_ref[...] = attended
    log_total = jnp.concatenate(tops, axis=0) + jnp.log2(total)
    qa_ref[:, 128:256] = three_parts(-jnp.transpose(log_total))
    lepe = conv(v_ref[...].astype(F32), vec_ref, lanes, half, length, False)
    att_ref[...] = (attended + lepe + vec_ref[21:22, lanes]).astype(BF16)


def attention_backward(
    x, half, length, grad, wb, vec_ref, qa_ref, k_ref, v_ref, o_ref, da_ref, gw_ref, rows_ref
):
    lanes = slice(128 * half, 128 * half + 128)
    grad_f = grad.astype(F32)
    product = grad_f * o_ref[...]
    inner = jnp.zeros_like(product)
    for h in range(4):
        keep = head_mask(product.shape, h)
        inner = jnp.where(
            keep, jnp.sum(jnp.where(keep, product, 0.0), axis=-1, keepdims=True), inner
        )
    da_ref[:, 0:128] = grad
    da_ref[:, 128:256] = three_parts(-inner)
    k_turned = turned(k_ref[...])
    q_turned = turned(qa_ref[:, 0:128])
    grad_turned = turned(grad)
    k_wide = beside_parts(k_ref[...])
    v_wide = beside_parts(v_ref[...])

    def head_products(h):
        mask = head_lanes(h, 256)
        return mm_nt(qa_ref[...] * mask, k_wide), mm_nt(da_ref[...] * mask, v_wide)

    early = grad.shape[0] <= LONGEST
    following = head_products(0) if early else None
    dqs, dks, dvs = [], [], []
    for h in range(4):
        scores, grad_probs = following if early else head_products(h)
        if early and h < 3:
            following = head_products(h + 1)
        probs = jnp.exp2(scores)
        grad_scores = (probs * grad_probs).astype(BF16)
        rows = slice(HEAD_DIM * h, HEAD_DIM * h + HEAD_DIM)
        dvs.append(mm(grad_turned[rows], probs.astype(BF16)))
        dks.append(mm(q_turned[rows], grad_scores))
        dqs.append(mm_nt(k_turned[rows], grad_scores))
    dq = (jnp.transpose(jnp.concatenate(dqs, axis=0)) * HEAD_DIM**-0.5).astype(BF16)
    dk = (jnp.transpose(jnp.concatenate(dks, axis=0)) * LN2).astype(BF16)
    dv = jnp.transpose(jnp.concatenate(dvs, axis=0))
    dv = (dv + conv(grad_f, vec_ref, lanes, half, length, True)).astype(BF16)
    unit, _ = unit_rows(x)
    normed = (unit * vec_ref[0:1] + vec_ref[1:2]).astype(BF16)
    gw_ref[...] += mm_tn(normed, jnp.concatenate([dq, dk, dv], axis=1))
    rows_ref[0:1, :] += jnp.sum(dq.astype(F32), axis=0, keepdims=True)
    rows_ref[1:2, :] += jnp.sum(dv.astype(F32), axis=0, keepdims=True)
    for b, col in enumerate(shifted_columns(v_ref[...].astype(F32), length)):
        for a, val in enumerate(shifted_rows(col, length)):
            row = tap_row(half, a, b) - 10
            rows_ref[row : row + 1, :] += jnp.sum(grad_f * val, axis=0, keepdims=True)
    rows_ref[11:12, :] += jnp.sum(grad_f, axis=0, keepdims=True)
    part = mm_nt(dq, wb(0)) + mm_nt(dk, wb(1)) + mm_nt(dv, wb(2))
    gain_row = jnp.sum(part * unit, axis=0, keepdims=True)
    shift_row = jnp.sum(part, axis=0, keepdims=True)
    for i in range(2):
        rows_ref[12 + i : 13 + i, :] += gain_row[:, 128 * i : 128 * i + 128]
        rows_ref[14 + i : 15 + i, :] += shift_row[:, 128 * i : 128 * i + 128]
    return part


def feed_forward(x, att, top, w_ref, base, vec_ref, n2_ref, acc_ref, gn_ref, gp_ref, g1_ref, g2_ref, rows_ref):
    middle = x + mm(att, w_ref[base : base + 256, :]) + vec_ref[4:5]
    unit, inverse = unit_rows(middle)
    n2_ref[...] = (unit * vec_ref[5:6] + vec_ref[6:7]).astype(BF16)
    acc_ref[...] = middle + vec_ref[11:12]
    gn_ref[...] = jnp.zeros_like(gn_ref)
    for f in range(4):
        w1 = w_ref[base + 256 * (1 + f) : base + 256 * (2 + f), :]
        w2 = w_ref[base + 256 * (5 + f) : base + 256 * (6 + f), :]
        cols = slice(256 * f, 256 * f + 256)
        hidden = mm(n2_ref[...], w1) + vec_ref[7 + f : 8 + f]
        below = 0.5 * (1.0 + lax.erf(hidden * (0.5**0.5)))
        active = (hidden * below).astype(BF16)
        slope = below + hidden * jnp.exp(-0.5 * hidden * hidden) * 0.3989422804014327
        grad_hidden = (mm_nt(top, w2) * slope).astype(BF16)
        acc_ref[...] += mm(active, w2)
        gn_ref[...] += mm_nt(grad_hidden, w1)
        g1_ref[:, cols] += mm_tn(n2_ref[...], grad_hidden)
        g2_ref[:, cols] += mm_tn(top, active)
        rows_ref[3 + f : 4 + f, :] += jnp.sum(grad_hidden.astype(F32), axis=0, keepdims=True)
    grad_normed = gn_ref[...]
    top_f = top.astype(F32)
    grad_middle = top_f + norm_back(grad_normed, vec_ref[5:6], unit, inverse)
    branch = grad_middle.astype(BF16)
    gp_ref[...] += mm_tn(branch, att)
    rows_ref[0:1, :] += jnp.sum(branch.astype(F32), axis=0, keepdims=True)
    rows_ref[1:2, :] += jnp.sum(grad_normed * unit, axis=0, keepdims=True)
    rows_ref[2:3, :] += jnp.sum(grad_normed, axis=0, keepdims=True)
    rows_ref[7:8, :] += jnp.sum(top_f, axis=0, keepdims=True)
    grad_att = mm_nt(branch, w_ref[base : base + 256, :]).astype(BF16)
    return acc_ref[...].astype(BF16), grad_middle, grad_att


PARAMS = pltpu.CompilerParams(
    dimension_semantics=("arbitrary",), vmem_limit_bytes=VMEM_LIMIT
)


def whole(shape):
    return pl.BlockSpec(shape, lambda m: (0,) * len(shape))


def each(shape):
    return pl.BlockSpec((None,) + shape, lambda m: (m,) + (0,) * len(shape))


def shape_of(dtype, *shape):
    return jax.ShapeDtypeStruct(shape, dtype)


def pack_tokens(x, nb, length):
    micro, tokens, channels = x.shape

    def kernel(x_ref, o_ref, hot):
        @pl.when(pl.program_id(0) == 0)
        def _():
            hot[...] = order_out(nb, length)

        o_ref[...] = mm(hot[...], x_ref[...]).astype(BF16)

    return pl.pallas_call(
        kernel,
        grid=(micro,),
        in_specs=[each((tokens, channels))],
        out_specs=each((nb * PIECE, channels)),
        out_shape=shape_of(BF16, micro, nb * PIECE, channels),
        scratch_shapes=[pltpu.VMEM((nb * PIECE, tokens), BF16)],
        compiler_params=PARAMS,
        name="pack_tokens",
    )(x)


def forward_call(x, half, nb, length, weights, vectors):
    micro = x.shape[0]
    tokens = STRIPE * length
    packed = nb * PIECE

    def kernel(x_ref, w_ref, vec_ref, qa_ref, k_ref, v_ref, o_ref, att_ref, xs_ref, *scr):
        if half == 0:
            attention_forward(
                x_ref[...].astype(F32), half, length, lane_blocks(w_ref, half), vec_ref, qa_ref, k_ref, v_ref, o_ref, att_ref
            )
        else:
            att_s, hot_in, hot_out = scr

            @pl.when(pl.program_id(0) == 0)
            def _():
                hot_in[...] = order_in(nb, length)
                hot_out[...] = order_out(nb, length)

            xs_ref[...] = mm(hot_in[...], x_ref[...]).astype(BF16)
            attention_forward(
                xs_ref[...].astype(F32), half, length, lane_blocks(w_ref, half), vec_ref, qa_ref, k_ref, v_ref, o_ref, att_s
            )
            att_ref[...] = mm(hot_out[...], att_s[...]).astype(BF16)

    rows = tokens if half == 0 else packed
    scratch = []
    if half == 1:
        scratch += [
            pltpu.VMEM((tokens, 128), BF16),
            pltpu.VMEM((tokens, packed), BF16),
            pltpu.VMEM((packed, tokens), BF16),
        ]
    if half == 0:
        def body(x_ref, w_ref, vec_ref, qa_ref, k_ref, v_ref, o_ref, att_ref, *scr):
            kernel(x_ref, w_ref, vec_ref, qa_ref, k_ref, v_ref, o_ref, att_ref, None, *scr)
        extra_specs, extra_shapes = [], []
    else:
        body = kernel
        extra_specs = [each((tokens, 256))]
        extra_shapes = [shape_of(BF16, micro, tokens, 256)]
    return pl.pallas_call(
        body,
        grid=(micro,),
        in_specs=[each((rows, 256)), whole(weights.shape), whole(vectors.shape)],
        out_specs=[
            each((tokens, 256)),
            each((tokens, 128)),
            each((tokens, 128)),
            each((tokens, 128)),
            each((rows, 128)),
        ] + extra_specs,
        out_shape=[
            shape_of(BF16, micro, tokens, 256),
            shape_of(BF16, micro, tokens, 128),
            shape_of(BF16, micro, tokens, 128),
            shape_of(F32, micro, tokens, 128),
            shape_of(BF16, micro, rows, 128),
        ] + extra_shapes,
        scratch_shapes=scratch,
        compiler_params=PARAMS,
        name="attention_forward_%d" % half,
    )(x, weights, vectors)


def middle_call(x, att_h, att_v, top, nb, length, weights, vectors):
    micro, tokens, _ = x.shape
    packed = nb * PIECE

    def kernel(
        x_ref, h_ref, v_ref, top_ref, w_ref, vec_ref,
        out_ref, gm_ref, gh_ref, gv_ref, gp_ref, g1_ref, g2_ref, rows_ref,
        hot_in, hot_out, att, n2, acc, gn,
    ):
        @pl.when(pl.program_id(0) == 0)
        def _():
            hot_in[...] = order_in(nb, length)
            hot_out[...] = order_out(nb, length)
            for ref in (gp_ref, g1_ref, g2_ref, rows_ref):
                ref[...] = jnp.zeros_like(ref)

        att[:, 0:128] = h_ref[...]
        att[:, 128:256] = mm(hot_in[...], v_ref[...]).astype(BF16)
        out, grad_middle, grad_att = feed_forward(
            x_ref[...].astype(F32), att[...], top_ref[...], w_ref, ROW_PROJ, vec_ref, n2, acc, gn, gp_ref, g1_ref, g2_ref, rows_ref
        )
        out_ref[...] = out
        gm_ref[...] = grad_middle
        gh_ref[...] = grad_att[:, 0:128]
        gv_ref[...] = mm(hot_out[...], grad_att[:, 128:256]).astype(BF16)

    return pl.pallas_call(
        kernel,
        grid=(micro,),
        in_specs=[
            each((tokens, 256)), each((tokens, 128)), each((packed, 128)), each((tokens, 256)),
            whole(weights.shape), whole(vectors.shape),
        ],
        out_specs=[
            each((tokens, 256)), each((tokens, 256)), each((tokens, 128)), each((packed, 128)),
            whole((256, 256)), whole((256, 1024)), whole((256, 1024)), whole((8, 256)),
        ],
        out_shape=[
            shape_of(BF16, micro, tokens, 256), shape_of(F32, micro, tokens, 256),
            shape_of(BF16, micro, tokens, 128), shape_of(BF16, micro, packed, 128),
            shape_of(F32, 256, 256), shape_of(F32, 256, 1024), shape_of(F32, 256, 1024), shape_of(F32, 8, 256),
        ],
        scratch_shapes=[
            pltpu.VMEM((tokens, packed), BF16), pltpu.VMEM((packed, tokens), BF16),
            pltpu.VMEM((tokens, 256), BF16), pltpu.VMEM((tokens, 256), BF16),
            pltpu.VMEM((tokens, 256), F32), pltpu.VMEM((tokens, 256), F32),
        ],
        compiler_params=PARAMS,
        name="feed_forward",
    )(x, att_h, att_v, top, weights, vectors)


def backward_call(x, grad, qa, k, v, o, half, nb, length, weights, vectors):
    micro, tokens, _ = x.shape
    packed = nb * PIECE

    def kernel(
        x_ref, g_ref, qa_ref, k_ref, v_ref, o_ref, w_ref, vec_ref, gn_ref, gw_ref, rows_ref,
        da, *scr,
    ):
        @pl.when(pl.program_id(0) == 0)
        def _():
            gw_ref[...] = jnp.zeros_like(gw_ref)
            rows_ref[...] = jnp.zeros_like(rows_ref)
            if half == 1:
                scr[0][...] = order_in(nb, length)
                scr[1][...] = order_out(nb, length)

        grad_in = g_ref[...] if half == 0 else mm(scr[0][...], g_ref[...]).astype(BF16)
        part = attention_backward(
            x_ref[...].astype(F32), half, length, grad_in, lane_blocks(w_ref, half), vec_ref, qa_ref, k_ref, v_ref, o_ref,
            da, gw_ref, rows_ref,
        )
        if half == 0:
            gn_ref[...] = part
        else:
            gn_ref[...] = mm(scr[1][...], part.astype(BF16)).astype(BF16)

    rows = tokens if half == 0 else packed
    scratch = [pltpu.VMEM((tokens, 256), BF16)]
    if half == 1:
        scratch += [pltpu.VMEM((tokens, packed), BF16), pltpu.VMEM((packed, tokens), BF16)]
    return pl.pallas_call(
        kernel,
        grid=(micro,),
        in_specs=[
            each((tokens, 256)), each((rows, 128)), each((tokens, 256)), each((tokens, 128)),
            each((tokens, 128)), each((tokens, 128)), whole(weights.shape), whole(vectors.shape),
        ],
        out_specs=[each((rows, 256)), whole((256, 384)), whole((16, 128))],
        out_shape=[
            shape_of(F32 if half == 0 else BF16, micro, rows, 256),
            shape_of(F32, 256, 384), shape_of(F32, 16, 128),
        ],
        scratch_shapes=scratch,
        compiler_params=PARAMS,
        name="attention_backward_%d" % half,
    )(x, grad, qa, k, v, o, weights, vectors)


def last_call(x, grad_middle, part_h, part_v, nb, length, vectors):
    micro, tokens, _ = x.shape
    packed = nb * PIECE

    def kernel(x_ref, gm_ref, h_ref, v_ref, vec_ref, out_ref, hot_in):
        @pl.when(pl.program_id(0) == 0)
        def _():
            hot_in[...] = order_in(nb, length)

        grad_normed = h_ref[...] + mm(hot_in[...], v_ref[...])
        unit, inverse = unit_rows(x_ref[...].astype(F32))
        out_ref[...] = (
            gm_ref[...] + norm_back(grad_normed, vec_ref[0:1], unit, inverse)
        ).astype(BF16)

    return pl.pallas_call(
        kernel,
        grid=(micro,),
        in_specs=[
            each((tokens, 256)), each((tokens, 256)), each((tokens, 256)), each((packed, 256)), whole(vectors.shape),
        ],
        out_specs=each((tokens, 256)),
        out_shape=shape_of(BF16, micro, tokens, 256),
        scratch_shapes=[pltpu.VMEM((tokens, packed), BF16)],
        compiler_params=PARAMS,
        name="input_gradient",
    )(x, grad_middle, part_h, part_v, vectors)


def repeat(lo, hi, body):
    def step(k, c):
        body(k)
        return c

    lax.fori_loop(lo, hi, step, 0)


def remote(src, dst, ss, rs, dev):
    return pltpu.make_async_remote_copy(
        src_ref=src, dst_ref=dst, send_sem=ss, recv_sem=rs, device_id=dev, device_id_type=MESH
    )


def await_bytes(ref, sem):
    pltpu.make_async_copy(ref, ref, sem).wait()


class Swap:
    def __init__(self, n, out_ref, in_ref, send_sem, recv_sem):
        self.n, self.out, self.into, self.ss, self.rs = n, out_ref, in_ref, send_sem, recv_sem
        self.me = lax.axis_index("band")

    def rows(self, i):
        return pl.ds(pl.multiple_of(i * PIECE, PIECE), PIECE)

    def send(self, m):
        mine = self.rows(self.me)

        def one(k):
            d = lax.rem(self.me + k, self.n)
            remote(
                self.out.at[m, self.rows(d)],
                self.into.at[m, mine],
                self.ss.at[m],
                self.rs.at[m],
                {"band": d},
            ).start()

        repeat(1, self.n, one)
        self.into[m, mine, :] = self.out[m, mine, :]

    def wait(self, m):
        others = pl.ds(0, (self.n - 1) * PIECE)
        await_bytes(self.out.at[m, others], self.ss.at[m])
        await_bytes(self.into.at[m, others], self.rs.at[m])


class Sum:
    def __init__(self, nb, nx, x_ref, o_ref, got, half, recv, sems):
        self.nx = nx
        self.nq = (nb // 2) * nx
        self.p = x_ref.shape[0] // (2 * self.nq)
        band = lax.axis_index("band")
        self.core = lax.rem(band, 2)
        self.q = (band // 2) * nx + lax.axis_index("batch")
        self.sibling = {"band": band + 1 - 2 * self.core}
        self.x, self.o, self.got, self.half, self.recv = x_ref, o_ref, got, half, recv
        self.sems = sems

    def chip(self, t):
        return {"band": (t // self.nx) * 2 + self.core, "batch": lax.rem(t, self.nx)}

    def ahead(self, k):
        return lax.rem(self.q + k, self.nq)

    def behind(self, k):
        return lax.rem(self.q - k + self.nq, self.nq)

    def side(self, c):
        rows = self.nq * self.p
        return pl.ds(pl.multiple_of(c * rows, 16), rows)

    def wide(self, c, t):
        return pl.ds(pl.multiple_of((c * self.nq + t) * self.p, 16), self.p)

    def thin(self, t):
        return pl.ds(pl.multiple_of(t * self.p, 16), self.p)

    def sem(self, i):
        return self.sems.at[2 * i], self.sems.at[2 * i + 1]

    def arrived(self, i, sent, came):
        await_bytes(sent, self.sems.at[2 * i])
        await_bytes(came, self.sems.at[2 * i + 1])

    def pair_copy(self, c):
        return remote(self.x.at[self.side(c)], self.got, *self.sem(0), self.sibling)

    def start(self):
        self.pair_copy(1 - self.core).start()

    def scatter(self):
        self.pair_copy(self.core).wait()
        self.half[...] = (
            self.x[self.side(self.core)].astype(F32) + self.got[...].astype(F32)
        ).astype(BF16)

        def one(k):
            t = self.ahead(k)
            remote(
                self.half.at[self.thin(t)],
                self.recv.at[self.thin(self.q)],
                *self.sem(1),
                self.chip(t),
            ).start()

        repeat(1, self.nq, one)
        self.recv[self.thin(self.q)] = self.half[self.thin(self.q)]

    def gather(self):
        others = pl.ds(0, (self.nq - 1) * self.p)
        self.arrived(1, self.half.at[others], self.recv.at[others])
        total = self.recv[0 : self.p].astype(F32)
        for t in range(1, self.nq):
            total = total + self.recv[t * self.p : (t + 1) * self.p].astype(F32)
        mine = self.wide(self.core, self.q)
        self.o[mine] = total.astype(BF16)

        def give(k):
            remote(
                self.o.at[mine], self.o.at[mine], *self.sem(2), self.chip(self.ahead(k))
            ).start()

        repeat(1, self.nq, give)

    def pass_on(self, c):
        return remote(
            self.o.at[self.side(self.core)], self.o.at[self.side(c)], *self.sem(3), self.sibling
        )

    def relay(self):
        others = pl.ds(0, (self.nq - 1) * self.p)
        self.arrived(2, self.o.at[others], self.o.at[others])
        self.pass_on(self.core).start()

    def finish(self):
        self.pass_on(1 - self.core).wait()


class DeepSum:
    def __init__(self, nb, nx, x_ref, o_ref, got, half, recv, deep, deep_recv, sems):
        self.nx = nx
        self.n1, self.n2 = 2 * nx, nb // 4
        self.p = x_ref.shape[0] // (2 * self.n1 * self.n2)
        band = lax.axis_index("band")
        self.core = lax.rem(band, 2)
        self.j1 = lax.rem(band // 2, 2) * nx + lax.axis_index("batch")
        self.j2 = band // 4
        self.sibling = {"band": band + 1 - 2 * self.core}
        self.x, self.o, self.got, self.half, self.recv = x_ref, o_ref, got, half, recv
        self.deep, self.deep_recv = deep, deep_recv
        self.sems = sems

    def near(self, t):
        return {
            "band": self.j2 * 4 + (t // self.nx) * 2 + self.core,
            "batch": lax.rem(t, self.nx),
        }

    def far(self, t):
        return {"band": t * 4 + lax.rem(lax.axis_index("band"), 4)}

    def near_at(self, k):
        return lax.rem(self.j1 + k, self.n1)

    def far_at(self, k):
        return lax.rem(self.j2 + k, self.n2)

    def block(self, c, t):
        rows = self.n2 * self.p
        return pl.ds(pl.multiple_of((c * self.n1 + t) * rows, 16), rows)

    def thin(self, t):
        rows = self.n2 * self.p
        return pl.ds(pl.multiple_of(t * rows, 16), rows)

    def piece(self, t):
        return pl.ds(pl.multiple_of(t * self.p, 16), self.p)

    def o_piece(self, t):
        at = (self.core * self.n1 + self.j1) * self.n2 + t
        return self.o.at[pl.ds(pl.multiple_of(at * self.p, 16), self.p)]

    def sem(self, i):
        return self.sems.at[2 * i], self.sems.at[2 * i + 1]

    def arrived(self, i, sent, came):
        await_bytes(sent, self.sems.at[2 * i])
        await_bytes(came, self.sems.at[2 * i + 1])

    def side(self, c):
        rows = self.n1 * self.n2 * self.p
        return pl.ds(pl.multiple_of(c * rows, 16), rows)

    def pair_copy(self, c):
        return remote(self.x.at[self.side(c)], self.got, *self.sem(0), self.sibling)

    def start(self):
        self.pair_copy(1 - self.core).start()

    def scatter(self):
        self.pair_copy(self.core).wait()
        self.half[...] = (
            self.x[self.side(self.core)].astype(F32) + self.got[...].astype(F32)
        ).astype(BF16)

        def one(k):
            t = self.near_at(k)
            remote(
                self.half.at[self.thin(t)],
                self.recv.at[self.thin(self.j1)],
                *self.sem(1),
                self.near(t),
            ).start()

        repeat(1, self.n1, one)

    def scatter_far(self):
        others = pl.ds(0, (self.n1 - 1) * self.n2 * self.p)
        self.arrived(1, self.half.at[others], self.recv.at[others])
        total = self.half[self.thin(self.j1)].astype(F32)
        for k in range(1, self.n1):
            total = total + self.recv[self.thin(self.near_at(k))].astype(F32)
        self.deep[...] = total.astype(BF16)

        def give(k):
            t = self.far_at(k)
            remote(
                self.deep.at[self.piece(t)],
                self.deep_recv.at[self.piece(self.j2)],
                *self.sem(2),
                self.far(t),
            ).start()

        repeat(1, self.n2, give)

    def gather(self):
        others = pl.ds(0, (self.n2 - 1) * self.p)
        self.arrived(2, self.deep.at[others], self.deep_recv.at[others])
        total = self.deep[self.piece(self.j2)].astype(F32)
        for k in range(1, self.n2):
            total = total + self.deep_recv[self.piece(self.far_at(k))].astype(F32)
        at = (self.core * self.n1 + self.j1) * self.n2 + self.j2
        self.o[pl.ds(pl.multiple_of(at * self.p, 16), self.p)] = total.astype(BF16)
        mine = self.o_piece(self.j2)
        repeat(
            1,
            self.n2,
            lambda k: remote(mine, mine, *self.sem(3), self.far(self.far_at(k))).start(),
        )

    def gather_near(self):
        others = pl.ds(0, (self.n2 - 1) * self.p)
        self.arrived(3, self.o.at[others], self.o.at[others])
        mine = self.o.at[self.block(self.core, self.j1)]
        repeat(
            1,
            self.n1,
            lambda k: remote(mine, mine, *self.sem(4), self.near(self.near_at(k))).start(),
        )

    def pass_on(self, c):
        return remote(
            self.o.at[self.side(self.core)], self.o.at[self.side(c)], *self.sem(5), self.sibling
        )

    def relay(self):
        others = pl.ds(0, (self.n1 - 1) * self.n2 * self.p)
        self.arrived(4, self.o.at[others], self.o.at[others])
        self.pass_on(self.core).start()

    def finish(self):
        self.pass_on(1 - self.core).wait()


ROWS_A = 1536
ROWS_B = 2304
ROWS_G = 800


def up(rows, unit):
    return -(-rows // unit) * unit


def split_rows(ref, at, rows):
    n = rows.shape[0]
    high = rows.astype(BF16)
    ref[at : at + n, :] = high
    ref[at + n : at + 2 * n, :] = (rows - high.astype(F32)).astype(BF16)


def block_kernel(
    nb, nx, length,
    own_ref, x_ref, wq_ref, vec_ref, top_hbm, wp_hbm, w1_hbm, w2_hbm,
    out_ref, ing_ref, gb_ref, gav_ref, gah_ref,
    wa_in, wb_in, wa, wb, gb_in, gav_in, gah_in,
    wide_got, wide_half, wide_recv, wide_deep, wide_deep_recv, a_got, a_half, a_recv,
    gb_got, gb_half, gb_recv, gb_deep, gb_deep_recv,
    v_got, v_half, v_recv, v_deep, v_deep_recv, h_got, h_half, h_recv,
    hot_in, hot_out, x_out, x_in, a_out, a_in, g_out, g_in, p_out, p_in,
    xs, qa, ks, vs, os, att, n2, acc, gn, gm, grad_h, part_h,
    gp, g1, g2, rows_mid, gw_v, gw_h, rows_v, rows_h, da,
    x_ss, x_rs, a_ss, a_rs, g_ss, g_rs, p_ss, p_rs,
    wa_sem, wb_sem, gb_sem, gav_sem, gah_sem,
    top_ref, wp_ref, w1_ref, w2_ref, fetch_sem,
):
    fetches = [
        pltpu.make_async_copy(src, dst, fetch_sem.at[i])
        for i, (src, dst) in enumerate(
            ((wp_hbm, wp_ref), (w1_hbm, w1_ref), (w2_hbm, w2_ref), (top_hbm, top_ref))
        )
    ]
    for c in fetches:
        c.start()
    band = lax.axis_index("band")
    batch = lax.axis_index("batch")
    device = band * nx + batch
    micro = x_ref.shape[0]
    core = lax.rem(band, 2)
    bar = pltpu.get_barrier_semaphore()
    repeat(
        1,
        nb,
        lambda k: pl.semaphore_signal(
            bar, inc=1, device_id={"band": lax.rem(band + k, nb)}, device_id_type=MESH
        ),
    )

    def greet(t):
        other = lax.rem(batch + 1 + t // (nb // 2), nx)
        pl.semaphore_signal(
            bar,
            inc=1,
            device_id={"band": lax.rem(t, nb // 2) * 2 + core, "batch": other},
            device_id_type=MESH,
        )

    repeat(0, (nb // 2) * (nx - 1), greet)

    sum_wa = Sum(nb, nx, wa_in, wa, a_got, a_half, a_recv, wa_sem)
    sum_wb = DeepSum(
        nb, nx, wb_in, wb, wide_got, wide_half, wide_recv, wide_deep, wide_deep_recv, wb_sem
    )
    sum_gb = DeepSum(
        nb, nx, gb_in, gb_ref, gb_got, gb_half, gb_recv, gb_deep, gb_deep_recv, gb_sem
    )
    sum_gav = DeepSum(
        nb, nx, gav_in, gav_ref, v_got, v_half, v_recv, v_deep, v_deep_recv, gav_sem
    )
    sum_gah = Sum(nb, nx, gah_in, gah_ref, h_got, h_half, h_recv, gah_sem)
    swap_x = Swap(nb, x_out, x_in, x_ss, x_rs)
    swap_a = Swap(nb, a_out, a_in, a_ss, a_rs)
    swap_g = Swap(nb, g_out, g_in, g_ss, g_rs)
    swap_p = Swap(nb, p_out, p_in, p_ss, p_rs)

    def own(ref, which, cols):
        return jnp.where(own_ref[which] == device, ref[0, :, cols], 0.0).astype(BF16)

    for b in range(6):
        wa_in[256 * b : 256 * b + 256, :] = own(wq_ref, 0, slice(128 * b, 128 * b + 128))
    if wa_in.shape[0] > ROWS_A:
        wa_in[ROWS_A:, :] = jnp.zeros((wa_in.shape[0] - ROWS_A, 128), BF16)
    pl.semaphore_wait(bar, nb - 1 + (nb // 2) * (nx - 1))
    sum_wa.start()
    sum_wa.scatter()
    hot_out[...] = order_out(nb, length)
    x_out[0] = mm(hot_out[...], x_ref[0]).astype(BF16)
    sum_wa.gather()
    swap_x.send(0)
    for c in fetches[:3]:
        c.wait()
    wb_in[0:256, :] = own(wp_ref, 1, slice(0, 256))
    for f in range(4):
        wb_in[256 * (f + 1) : 256 * (f + 2), :] = own(w1_ref, 2, slice(256 * f, 256 * f + 256))
    wb_in[1280:ROWS_B, :] = own(w2_ref, 3, slice(0, 256))
    wb_in[ROWS_B:, :] = jnp.zeros((wb_in.shape[0] - ROWS_B, 256), BF16)
    sum_wb.start()
    hot_in[...] = order_in(nb, length)
    for ref in (gp, g1, g2, rows_mid, gw_v, gw_h, rows_v, rows_h):
        ref[...] = jnp.zeros_like(ref)
    for m in range(1, micro):
        x_out[m] = mm(hot_out[...], x_ref[m]).astype(BF16)
    sum_wa.relay()
    for m in range(1, micro):
        swap_x.send(m)
    sum_wb.scatter()
    sum_wa.finish()

    def blocks(half):
        return lambda b: wa[256 * (2 * b + half) : 256 * (2 * b + half) + 256, :]

    def forward_h(m):
        attention_forward(
            x_ref[m].astype(F32), 0, length, blocks(0), vec_ref,
            qa.at[m], ks.at[m], vs.at[m], os.at[m], att.at[m, :, pl.ds(0, 128)],
        )

    def forward_v(m):
        swap_x.wait(m)
        xs[m] = mm(hot_in[...], x_in[m]).astype(BF16)
        w = micro + m
        attention_forward(
            xs[m].astype(F32), 1, length, blocks(1), vec_ref,
            qa.at[w], ks.at[w], vs.at[w], os.at[w], att.at[m, :, pl.ds(128, 128)],
        )
        a_out[m] = mm(hot_out[...], att[m, :, 128:256]).astype(BF16)
        swap_a.send(m)

    def forward_rows(m):
        forward_h(m)

        @pl.when(m == 0)
        def _():
            sum_wb.scatter_far()

    repeat(0, micro, forward_rows)
    sum_wb.gather()

    def forward_columns(m):
        forward_v(m)

        @pl.when(m == 0)
        def _():
            sum_wb.gather_near()

    repeat(0, micro, forward_columns)
    sum_wb.relay()
    sum_wb.finish()
    fetches[3].wait()

    def middle_step(m):
        swap_a.wait(m)
        att[m, :, 128:256] = mm(hot_in[...], a_in[m]).astype(BF16)
        out, grad_middle, grad_att = feed_forward(
            x_ref[m].astype(F32), att[m], top_ref[m], wb, 0, vec_ref, n2, acc, gn,
            gp, g1, g2, rows_mid,
        )
        out_ref[m] = out
        gm[m] = grad_middle
        grad_h[m] = grad_att[:, 0:128]
        g_out[m] = mm(hot_out[...], grad_att[:, 128:256]).astype(BF16)
        swap_g.send(m)

    repeat(0, micro, middle_step)
    gb_in[0:256, :] = jnp.transpose(gp[...]).astype(BF16)
    for f in range(4):
        cols = slice(256 * f, 256 * f + 256)
        gb_in[256 * (f + 1) : 256 * (f + 2), :] = g1[:, cols].astype(BF16)
        gb_in[1280 + 256 * f : 1536 + 256 * f, :] = jnp.transpose(g2[:, cols]).astype(BF16)
    gb_in[ROWS_B:, :] = jnp.zeros((gb_in.shape[0] - ROWS_B, 256), BF16)
    split_rows(gb_in, ROWS_B, rows_mid[...])
    sum_gb.start()

    def backward_v(m):
        swap_g.wait(m)
        w = micro + m
        grad_in = mm(hot_in[...], g_in[m]).astype(BF16)
        part = attention_backward(
            xs[m].astype(F32), 1, length, grad_in, blocks(1), vec_ref,
            qa.at[w], ks.at[w], vs.at[w], os.at[w], da, gw_v, rows_v,
        )
        p_out[m] = mm(hot_out[...], part.astype(BF16)).astype(BF16)
        swap_p.send(m)

        @pl.when(m == 0)
        def _():
            sum_gb.scatter()

    repeat(0, micro, backward_v)
    sum_gb.scatter_far()

    def fill(ref, gw, rows):
        for b in range(3):
            ref[256 * b : 256 * b + 256, :] = gw[:, 128 * b : 128 * b + 128].astype(BF16)
        split_rows(ref, 768, rows[...])
        ref[ROWS_G:, :] = jnp.zeros((ref.shape[0] - ROWS_G, 128), BF16)

    fill(gav_in, gw_v, rows_v)
    sum_gav.start()

    def backward_h(m):
        part_h[m] = attention_backward(
            x_ref[m].astype(F32), 0, length, grad_h[m], blocks(0), vec_ref,
            qa.at[m], ks.at[m], vs.at[m], os.at[m], da, gw_h, rows_h,
        )

        @pl.when(m == 0)
        def _():
            sum_gb.gather()
            sum_gav.scatter()
            sum_gb.gather_near()
            sum_gav.scatter_far()

    repeat(0, micro, backward_h)
    fill(gah_in, gw_h, rows_h)
    sum_gah.start()
    sum_gav.gather()
    sum_gah.scatter()
    sum_gb.relay()
    sum_gav.gather_near()
    sum_gb.finish()

    def last_step(m):
        swap_p.wait(m)
        grad_normed = part_h[m] + mm(hot_in[...], p_in[m])
        unit, inverse = unit_rows(x_ref[m].astype(F32))
        ing_ref[m] = (gm[m] + norm_back(grad_normed, vec_ref[0:1], unit, inverse)).astype(BF16)

    last_step(0)
    sum_gah.gather()
    sum_gav.relay()
    repeat(1, micro, last_step)
    sum_gah.relay()
    sum_gav.finish()
    sum_gah.finish()


def block_call(x, top, owners, w_qkv, w_proj, w_fc1, w_fc2, vectors, nb, nx, length):
    micro, tokens, _ = x.shape
    packed = nb * PIECE
    nq = nb // 2 * nx
    unit = 32 * nq
    ra, rb, rg = up(ROWS_A, unit), up(ROWS_B + 16, unit), up(ROWS_G, unit)
    vm = pltpu.VMEM
    windows = 2 * micro

    def steps(rows, cols):
        return [vm((rows // 2, cols), BF16)] * 3

    def deep_steps(rows, cols):
        return steps(rows, cols) + [vm((rows // (4 * nx), cols), BF16)] * 2

    scratch = (
        [vm((ra, 128), BF16), vm((rb, 256), BF16), vm((ra, 128), BF16), vm((rb, 256), BF16)]
        + [vm((rb, 256), BF16), vm((rg, 128), BF16), vm((rg, 128), BF16)]
        + deep_steps(rb, 256) + steps(ra, 128) + deep_steps(rb, 256) + deep_steps(rg, 128)
        + steps(rg, 128)
        + [vm((tokens, packed), BF16), vm((packed, tokens), BF16)]
        + [vm((micro, packed, 256), BF16)] * 2
        + [vm((micro, packed, 128), BF16)] * 4
        + [vm((micro, packed, 256), BF16)] * 2
        + [
            vm((micro, tokens, 256), BF16),
            vm((windows, tokens, 256), BF16),
            vm((windows, tokens, 128), BF16),
            vm((windows, tokens, 128), BF16),
            vm((windows, tokens, 128), F32),
            vm((micro, tokens, 256), BF16),
            vm((tokens, 256), BF16),
            vm((tokens, 256), F32),
            vm((tokens, 256), F32),
            vm((micro, tokens, 256), F32),
            vm((micro, tokens, 128), BF16),
            vm((micro, tokens, 256), F32),
            vm((256, 256), F32),
            vm((256, 1024), F32),
            vm((256, 1024), F32),
            vm((8, 256), F32),
            vm((256, 384), F32),
            vm((256, 384), F32),
            vm((16, 128), F32),
            vm((16, 128), F32),
            vm((tokens, 256), BF16),
        ]
        + [pltpu.SemaphoreType.DMA((micro,))] * 8
        + [pltpu.SemaphoreType.DMA((k,)) for k in (8, 12, 12, 12, 8)]
        + [vm(top.shape, BF16)]
        + [vm(w.shape, F32) for w in (w_proj, w_fc1, w_fc2)]
        + [pltpu.SemaphoreType.DMA((4,))]
    )
    whole_vmem = pl.BlockSpec(memory_space=vm)
    return pl.pallas_call(
        functools.partial(block_kernel, nb, nx, length),
        in_specs=[pl.BlockSpec(memory_space=pltpu.SMEM)]
        + [whole_vmem] * 3
        + [pl.BlockSpec(memory_space=pl.ANY)] * 4,
        out_specs=[whole_vmem] * 5,
        out_shape=[
            shape_of(BF16, micro, tokens, 256), shape_of(BF16, micro, tokens, 256),
            shape_of(BF16, rb, 256), shape_of(BF16, rg, 128), shape_of(BF16, rg, 128),
        ],
        scratch_shapes=scratch,
        compiler_params=pltpu.CompilerParams(
            collective_id=0, has_side_effects=True, vmem_limit_bytes=VMEM_LIMIT
        ),
        name="block",
    )(owners, x, w_qkv, vectors, top, w_proj, w_fc1, w_fc2)


def adam_kernel(
    vrows, rows,
    own_ref, gb_ref, gav_ref, gah_ref, vec_ref, vf_ref, vs_ref, *refs,
):
    moments = refs[0:12]
    bases = refs[12:20]
    grads = refs[20:24]
    outs = refs[24:36]
    vg_ref, vfn_ref, vsn_ref, vn_ref = refs[36:40]
    held = refs[40:52]
    left = refs[52:60]
    zeros_ref, in_sem, out_sem = refs[60:63]
    device = lax.axis_index("band") * lax.axis_size("batch") + lax.axis_index("batch")
    is_own = [own_ref[i] == device for i in range(4)]

    def load(i):
        pairs = [(moments[3 * i + j].at[0], held[3 * i + j], 5 * i + j) for j in range(3)]
        pairs += [(bases[2 * i + j], left[2 * i + j], 5 * i + 3 + j) for j in range(2)]
        return [pltpu.make_async_copy(a, b, in_sem.at[s]) for a, b, s in pairs]

    def store(i):
        return [
            pltpu.make_async_copy(held[3 * i + j], outs[3 * i + j].at[0], out_sem.at[3 * i + j])
            for j in range(3)
        ]

    def blank(i):
        copies = []
        for j in range(3):
            shape = outs[3 * i + j].shape
            copies.append(
                pltpu.make_async_copy(
                    zeros_ref.at[pl.ds(0, shape[1]), pl.ds(0, shape[2])],
                    outs[3 * i + j].at[0],
                    out_sem.at[3 * i + j],
                )
            )
        return copies

    for i in range(4):
        @pl.when(is_own[i])
        def _():
            for c in load(i):
                c.start()

    zeros_ref[...] = jnp.zeros_like(zeros_ref)
    for i in range(4):
        @pl.when(jnp.logical_not(is_own[i]))
        def _():
            for c in blank(i):
                c.start()

    for b in range(3):
        for half, ref in ((0, gah_ref), (1, gav_ref)):
            at = 256 * b + 128 * half
            grads[0][:, at : at + 128] = ref[256 * b : 256 * b + 256, :].astype(F32)
    grads[1][...] = gb_ref[0:256, :].astype(F32)
    for f in range(4):
        grads[2][:, 256 * f : 256 * f + 256] = gb_ref[256 * (f + 1) : 256 * (f + 2), :].astype(F32)
    grads[3][...] = gb_ref[1280:ROWS_B, :].astype(F32)

    mid = gb_ref[ROWS_B : ROWS_B + 8, :].astype(F32) + gb_ref[ROWS_B + 8 : ROWS_B + 16, :].astype(F32)
    side = [r[768:784, :].astype(F32) + r[784:800, :].astype(F32) for r in (gah_ref, gav_ref)]
    both = side[0] + side[1]
    for i in range(2):
        vg_ref[0:1, 128 * i : 128 * i + 128] = both[12 + i : 13 + i]
        vg_ref[1:2, 128 * i : 128 * i + 128] = both[14 + i : 15 + i]
        vg_ref[2:4, 128 * i : 128 * i + 128] = side[i][0:2]
        vg_ref[12:22, 128 * i : 128 * i + 128] = side[i][2:12]
    vg_ref[4:12, :] = mid
    grad = vg_ref[...]
    first_new = BETA_ONE * vf_ref[...] + (1.0 - BETA_ONE) * grad
    second_new = BETA_TWO * vs_ref[...] + (1.0 - BETA_TWO) * grad * grad
    vfn_ref[...] = first_new
    vsn_ref[...] = second_new
    vn_ref[...] = vec_ref[...] - RATE_VECTORS * (first_new / (1.0 - BETA_ONE**STEP)) / (
        jnp.sqrt(second_new / (1.0 - BETA_TWO**STEP)) + EPS_ADAM
    )

    for i in range(4):
        @pl.when(is_own[i])
        def _():
            for c in load(i):
                c.wait()
            first, second, weight = held[3 * i], held[3 * i + 1], held[3 * i + 2]
            lb, rb = left[2 * i], left[2 * i + 1]
            g = grads[i][...].astype(BF16)
            lh, rh = lb[...].astype(BF16), rb[...].astype(BF16)
            once = jnp.transpose(mm_tn(g, lh)) if i == 3 else mm_tn(lh, g)
            turned_grad = mm(once.astype(BF16), rh)
            first_new = BETA_ONE * first[...] + (1.0 - BETA_ONE) * turned_grad
            second_new = BETA_TWO * second[...] + (1.0 - BETA_TWO) * turned_grad * turned_grad
            first[...] = first_new
            second[...] = second_new
            step = (first_new / (1.0 - BETA_ONE**STEP)) / (
                jnp.sqrt(second_new / (1.0 - BETA_TWO**STEP)) + EPS_ADAM
            )
            back = mm_nt(mm(lh, step.astype(BF16)).astype(BF16), rh)
            weight[...] = weight[...] - RATE * back - RATE * DECAY * weight[...]
            for c in store(i):
                c.start()

    for i in range(4):
        for c in store(i):
            c.wait()


def adam_call(owners, gb, gav, gah, vectors, vectors_first, vectors_second, slots, bases):
    vm = pltpu.VMEM
    any_space = pl.BlockSpec(memory_space=pl.ANY)
    vspec = pl.BlockSpec(memory_space=vm)
    sizes = [(s.shape[1], s.shape[2]) for s in slots[::3]]
    vshape = shape_of(F32, *vectors.shape)
    tallest = max(a for a, _ in sizes)
    widest = max(b for _, b in sizes)
    return pl.pallas_call(
        functools.partial(adam_kernel, vectors.shape[0], None),
        in_specs=[pl.BlockSpec(memory_space=pltpu.SMEM)] + [vspec] * 6 + [any_space] * 20,
        out_specs=[vspec] * 4 + [any_space] * 12 + [vspec] * 4,
        out_shape=[shape_of(F32, *s) for s in sizes]
        + [shape_of(F32, *s.shape) for s in slots]
        + [vshape] * 4,
        scratch_shapes=[vm((s.shape[1], s.shape[2]), F32) for s in slots]
        + [vm(b.shape, F32) for b in bases]
        + [vm((tallest, widest), F32), pltpu.SemaphoreType.DMA((20,)), pltpu.SemaphoreType.DMA((12,))],
        compiler_params=pltpu.CompilerParams(vmem_limit_bytes=VMEM_LIMIT),
        name="adam",
    )(owners, gb, gav, gah, vectors, vectors_first, vectors_second, *slots, *bases)


def wide_to_stack(w):
    n = w.shape[1] // 256
    return w.reshape(256, n, 256).transpose(1, 0, 2).reshape(256 * n, 256)


def by_steps(x, top, owners, slots, vectors, nb, nx, length):
    device_index = lax.axis_index(("band", "batch"))

    def own(slot, which):
        return jnp.where(device_index == owners[which], slot[0], 0.0).astype(BF16)

    stacked = jnp.concatenate(
        [
            wide_to_stack(own(slots[0], 0)),
            own(slots[1], 1),
            wide_to_stack(own(slots[2], 2)),
            own(slots[3], 3),
        ],
        axis=0,
    )
    weights = sum_everywhere(stacked, nb, nx, 0)[:ROW_END]

    def swap(packed, cid):
        m, rows, ch = packed.shape
        swapped = packed.reshape(m, nb, PIECE, ch).transpose(1, 0, 2, 3).reshape(m * rows, ch)
        got = exchange(swapped, nb, cid)
        return got.reshape(nb, m, PIECE, ch).transpose(1, 0, 2, 3).reshape(m, rows, ch)

    columns = swap(pack_tokens(x, nb, length), 1)
    qa_v, k_v, v_v, o_v, att_v, x_v = forward_call(columns, 1, nb, length, weights, vectors)
    qa_h, k_h, v_h, o_h, att_h = forward_call(x, 0, nb, length, weights, vectors)
    att_v = swap(att_v, 2)
    block_out, grad_middle, grad_h, grad_v, gp_t, g1, g2_t, rows_mid = middle_call(
        x, att_h, att_v, top, nb, length, weights, vectors
    )
    grad_v = swap(grad_v, 3)
    part_v, gw_v, rows_v = backward_call(
        x_v, grad_v, qa_v, k_v, v_v, o_v, 1, nb, length, weights, vectors
    )
    part_h, gw_h, rows_h = backward_call(
        x, grad_h, qa_h, k_h, v_h, o_h, 0, nb, length, weights, vectors
    )
    part_v = swap(part_v, 4)
    input_grad = last_call(x, grad_middle, part_h, part_v, nb, length, vectors)

    def two(rows):
        high = rows.astype(BF16)
        return [high, (rows - high.astype(F32)).astype(BF16)]

    gb = jnp.concatenate(
        [gp_t.T.astype(BF16), wide_to_stack(g1.astype(BF16)), g2_t.T.astype(BF16)] + two(rows_mid),
        axis=0,
    )

    def side(gw, rows):
        return jnp.concatenate(
            [gw[:, 128 * b : 128 * b + 128].astype(BF16) for b in range(3)] + two(rows), axis=0
        )

    gb = sum_everywhere(gb, nb, nx, 5)
    gav = sum_everywhere(side(gw_v, rows_v), nb, nx, 6)
    gah = sum_everywhere(side(gw_h, rows_h), nb, nx, 7)
    return block_out, input_grad, gb, gav, gah


def per_device(
    tokens_in, cotangent, owners,
    weight_qkv, weight_proj, weight_fc1, weight_fc2,
    first_qkv, second_qkv, first_proj, second_proj, first_fc1, second_fc1, first_fc2, second_fc2,
    left_qkv, right_qkv, left_proj, right_proj, left_fc1, right_fc1, left_fc2, right_fc2,
    vectors, vectors_first, vectors_second,
    *, nb, nx,
):
    micro, images, band_rows, length, channels = tokens_in.shape
    tokens = band_rows * length
    x = tokens_in.reshape(micro * images, tokens, channels)
    top = cotangent.reshape(micro * images, tokens, channels)
    weights = (weight_qkv, weight_proj, weight_fc1, weight_fc2)
    if tokens <= LONGEST:
        block_out, input_grad, gb, gav, gah = block_call(
            x, top, owners, *weights, vectors, nb, nx, length
        )
    else:
        block_out, input_grad, gb, gav, gah = by_steps(
            x, top, owners, weights, vectors, nb, nx, length
        )
    slots = (
        first_qkv, second_qkv, weight_qkv, first_proj, second_proj, weight_proj,
        first_fc1, second_fc1, weight_fc1, first_fc2, second_fc2, weight_fc2,
    )
    bases = (left_qkv, right_qkv, left_proj, right_proj, left_fc1, right_fc1, left_fc2, right_fc2)
    done = adam_call(
        owners, gb, gav, gah, vectors, vectors_first, vectors_second, slots, bases
    )
    results = [block_out.reshape(tokens_in.shape), input_grad.reshape(tokens_in.shape)]
    for i in range(4):
        results.append(done[i])
        results += list(done[4 + 3 * i : 7 + 3 * i])
    return tuple(results) + tuple(done[16:20])


def solution(mesh):
    tokens_spec = P(None, "batch", "band", None, None)
    slot_spec = P(("band", "batch"), None, None)
    return jax.shard_map(
        functools.partial(per_device, nb=mesh.shape["band"], nx=mesh.shape["batch"]),
        mesh=mesh,
        in_specs=(tokens_spec, tokens_spec, P()) + (slot_spec,) * 12 + (P(),) * 11,
        out_specs=(tokens_spec, tokens_spec)
        + (P(), slot_spec, slot_spec, slot_spec) * 4
        + (P(),) * 4,
        check_vma=False,
    )
```

```python
import functools

import jax
import jax.numpy as jnp
from jax import lax
from jax.experimental import pallas as pl
from jax.experimental.pallas import tpu as pltpu
from jax.sharding import PartitionSpec as P

HEAD_DIM = 32
STRIPE = 7
STEP = 10
EPS_NORM = 1e-05
BETA_ONE = 0.5
BETA_TWO = 0.6
RATE = 0.04
RATE_VECTORS = 0.2
DECAY = 0.01
EPS_ADAM = 1e-08
MESH = pl.DeviceIdType.MESH
F32 = jnp.float32
BF16 = jnp.bfloat16
PIECE = 64
LOG2E = 1.4426950408889634
LN2 = 0.6931471805599453
Q_SCALE = LOG2E * HEAD_DIM**-0.5
LONGEST = 1024
VMEM_LIMIT = 60 * 1024 * 1024
ROW_QKV, ROW_PROJ, ROW_FC1, ROW_FC2, ROW_END = 0, 768, 1024, 2048, 3072


def mm(a, b):
    return lax.dot_general(a, b, (((1,), (0,)), ((), ())), preferred_element_type=F32)


def mm_nt(a, b):
    return lax.dot_general(a, b, (((1,), (1,)), ((), ())), preferred_element_type=F32)


def mm_tn(a, b):
    return lax.dot_general(a, b, (((0,), (0,)), ((), ())), preferred_element_type=F32)


def exchange_kernel(n, piece, x_ref, o_ref, send_sem, recv_sem, loc_sem):
    me = lax.axis_index("band")
    bar = pltpu.get_barrier_semaphore()

    def greet(k, c):
        pl.semaphore_signal(
            bar, inc=1, device_id={"band": lax.rem(me + k, n)}, device_id_type=MESH
        )
        return c

    lax.fori_loop(1, n, greet, 0)
    pl.semaphore_wait(bar, n - 1)

    def rows(i):
        return pl.ds(pl.multiple_of(i * piece, piece), piece)

    def send(k, c):
        d = lax.rem(me + k, n)
        pltpu.make_async_remote_copy(
            src_ref=x_ref.at[rows(d)],
            dst_ref=o_ref.at[rows(me)],
            send_sem=send_sem.at[k],
            recv_sem=recv_sem.at[k],
            device_id={"band": d},
            device_id_type=MESH,
        ).start()
        return c

    lax.fori_loop(1, n, send, 0)
    local = pltpu.make_async_copy(x_ref.at[rows(me)], o_ref.at[rows(me)], loc_sem)
    local.start()
    local.wait()

    def take(k, c):
        s = lax.rem(me - k + n, n)
        pltpu.make_async_remote_copy(
            src_ref=x_ref.at[rows(s)],
            dst_ref=o_ref.at[rows(s)],
            send_sem=send_sem.at[k],
            recv_sem=recv_sem.at[k],
            device_id={"band": s},
            device_id_type=MESH,
        ).wait()
        return c

    lax.fori_loop(1, n, take, 0)


def exchange(x, n, cid):
    return pl.pallas_call(
        functools.partial(exchange_kernel, n, x.shape[0] // n),
        out_shape=jax.ShapeDtypeStruct(x.shape, x.dtype),
        in_specs=[pl.BlockSpec(memory_space=pltpu.VMEM)],
        out_specs=pl.BlockSpec(memory_space=pltpu.VMEM),
        scratch_shapes=[
            pltpu.SemaphoreType.DMA((n,)),
            pltpu.SemaphoreType.DMA((n,)),
            pltpu.SemaphoreType.DMA,
        ],
        compiler_params=pltpu.CompilerParams(
            collective_id=cid, has_side_effects=True, vmem_limit_bytes=VMEM_LIMIT
        ),
        name="exchange",
    )(x)


def sum_kernel(nb, nx, total_rows, x_ref, o_ref, got, half, recv, s1, r1, s2, r2, s3, r3, s4, r4):
    nq = (nb // 2) * nx
    p = total_rows // (2 * nq)
    band = lax.axis_index("band")
    core = lax.rem(band, 2)
    q = (band // 2) * nx + lax.axis_index("batch")
    sibling = {"band": band + 1 - 2 * core}
    bar = pltpu.get_barrier_semaphore()

    def chip(t):
        return {"band": (t // nx) * 2 + core, "batch": lax.rem(t, nx)}

    def ahead(k):
        return lax.rem(q + k, nq)

    def behind(k):
        return lax.rem(q - k + nq, nq)

    def copy(src, dst, ss, rs, dev):
        return pltpu.make_async_remote_copy(
            src_ref=src, dst_ref=dst, send_sem=ss, recv_sem=rs, device_id=dev, device_id_type=MESH
        )

    def loop(lo, hi, body):
        def step(k, c):
            body(k)
            return c

        lax.fori_loop(lo, hi, step, 0)

    pl.semaphore_signal(bar, inc=1, device_id=sibling, device_id_type=MESH)
    loop(
        1,
        nq,
        lambda k: pl.semaphore_signal(
            bar, inc=1, device_id=chip(ahead(k)), device_id_type=MESH
        ),
    )
    pl.semaphore_wait(bar, nq)

    def whole_rows(c, t):
        return pl.ds(pl.multiple_of((c * nq + t) * p, 16), p)

    def half_rows(t):
        return pl.ds(pl.multiple_of(t * p, 16), p)

    def pair_copy(k, side):
        t = ahead(k)
        return copy(
            x_ref.at[whole_rows(side, t)], got.at[half_rows(t)], s1.at[t], r1.at[t], sibling
        )

    loop(1, nq + 1, lambda k: pair_copy(k, 1 - core).start())

    def scatter_copy(k):
        t = ahead(k)
        return copy(half.at[half_rows(t)], recv.at[half_rows(q)], s2.at[k], r2.at[k], chip(t))

    def pair_sum(k):
        t = ahead(k)
        pair_copy(k, core).wait()
        half[half_rows(t)] = (
            x_ref[whole_rows(core, t)].astype(F32) + got[half_rows(t)].astype(F32)
        ).astype(BF16)

        @pl.when(k < nq)
        def _():
            scatter_copy(k).start()

    loop(1, nq + 1, pair_sum)

    def add_piece(k, acc):
        t = behind(k)
        copy(half.at[half_rows(t)], recv.at[half_rows(t)], s2.at[k], r2.at[k], chip(t)).wait()
        return acc + recv[half_rows(t)].astype(F32)

    total = lax.fori_loop(1, nq, add_piece, half[half_rows(q)].astype(F32))
    mine = o_ref.at[whole_rows(core, q)]
    o_ref[whole_rows(core, q)] = total.astype(BF16)

    def gather_copy(k):
        return copy(mine, mine, s3.at[k], r3.at[k], chip(ahead(k)))

    def pass_on(t, side):
        return copy(
            o_ref.at[whole_rows(core, t)],
            o_ref.at[whole_rows(side, t)],
            s4.at[t],
            r4.at[t],
            sibling,
        )

    loop(1, nq, lambda k: gather_copy(k).start())
    pass_on(q, core).start()

    def relay(k):
        t = behind(k)
        copy(mine, o_ref.at[whole_rows(core, t)], s3.at[k], r3.at[k], chip(t)).wait()
        pass_on(t, core).start()

    loop(1, nq, relay)
    loop(0, nq, lambda t: pass_on(t, 1 - core).wait())


def sum_everywhere(x, nb, nx, cid):
    rows, cols = x.shape
    nq = nb // 2 * nx
    unit = 32 * nq
    padded = -(-rows // unit) * unit
    if padded != rows:
        x = jnp.concatenate([x, jnp.zeros((padded - rows, cols), x.dtype)], axis=0)
    sems = [pltpu.SemaphoreType.DMA((nq,)) for _ in range(8)]
    out = pl.pallas_call(
        functools.partial(sum_kernel, nb, nx, padded),
        out_shape=jax.ShapeDtypeStruct(x.shape, x.dtype),
        in_specs=[pl.BlockSpec(memory_space=pltpu.VMEM)],
        out_specs=pl.BlockSpec(memory_space=pltpu.VMEM),
        scratch_shapes=[pltpu.VMEM((padded // 2, cols), x.dtype)] * 3 + sems,
        compiler_params=pltpu.CompilerParams(
            collective_id=cid, has_side_effects=True, vmem_limit_bytes=VMEM_LIMIT
        ),
        name="sum_everywhere",
    )(x)
    return out


def order_out(pieces_n, length):
    row = lax.broadcasted_iota(jnp.int32, (pieces_n * PIECE, 1), 0)
    s = row // PIECE
    m = row % PIECE
    a = (m * 37) // 256
    b = m - STRIPE * a
    token = jnp.where(m < STRIPE * STRIPE, a * length + STRIPE * s + b, -1)
    column = lax.broadcasted_iota(jnp.int32, (pieces_n * PIECE, STRIPE * length), 1)
    return jnp.where(column == token, 1.0, 0.0).astype(BF16)


def order_in(pieces_n, length):
    row = lax.broadcasted_iota(jnp.int32, (1, pieces_n * PIECE), 1)
    s = row // PIECE
    m = row % PIECE
    a = (m * 37) // 256
    b = m - STRIPE * a
    token = jnp.where(m < STRIPE * STRIPE, b * length + STRIPE * s + a, -1)
    column = lax.broadcasted_iota(jnp.int32, (STRIPE * length, pieces_n * PIECE), 0)
    return jnp.where(column == token, 1.0, 0.0).astype(BF16)


def unit_rows(values):
    centred = values - jnp.mean(values, axis=-1, keepdims=True)
    inverse = lax.rsqrt(jnp.mean(centred * centred, axis=-1, keepdims=True) + EPS_NORM)
    return centred * inverse, inverse


def norm_back(grad_normed, gain, unit, inverse):
    scaled = grad_normed * gain
    first_mean = jnp.mean(scaled, axis=-1, keepdims=True)
    second_mean = jnp.mean(scaled * unit, axis=-1, keepdims=True)
    return inverse * (scaled - first_mean - unit * second_mean)


def shifted_columns(v, length):
    tokens = v.shape[0]
    column = lax.broadcasted_iota(jnp.int32, v.shape, 0) % length
    before = jnp.where(column == 0, 0.0, pltpu.roll(v, 1, 0))
    after = jnp.where(column == length - 1, 0.0, pltpu.roll(v, tokens - 1, 0))
    return before, v, after


def shifted_rows(v, length):
    zeros = jnp.zeros((length, v.shape[1]), v.dtype)
    above = jnp.concatenate([zeros, v[: v.shape[0] - length]], axis=0)
    below = jnp.concatenate([v[length:], zeros], axis=0)
    return above, v, below


def half_rows(vec_ref, half):
    def get(i):
        if 2 <= i < 11:
            a, b = divmod(i - 2, 3)
            row = 12 + (3 * a + b if half == 0 else 3 * b + a)
        else:
            row = {0: 2, 1: 3, 11: 21}[i]
        return vec_ref[row : row + 1, 128 * half : 128 * half + 128]

    return get


def conv(v, hv, length, flipped):
    total = jnp.zeros_like(v)
    for b, col in enumerate(shifted_columns(v, length)):
        for a, val in enumerate(shifted_rows(col, length)):
            total = total + val * hv(2 + (8 - 3 * a - b if flipped else 3 * a + b))
    return total


def head_mask(shape, h, offset=0):
    lane = lax.broadcasted_iota(jnp.int32, shape, len(shape) - 1) - offset
    return (lane >= h * HEAD_DIM) & (lane < (h + 1) * HEAD_DIM)


def three_parts(x):
    lane = lax.broadcasted_iota(jnp.int32, x.shape, len(x.shape) - 1) % HEAD_DIM
    hi = x.astype(BF16).astype(F32)
    mid = (x - hi).astype(BF16).astype(F32)
    low = x - hi - mid
    parts = jnp.where(lane == 0, hi, jnp.where(lane == 1, mid, jnp.where(lane == 2, low, 0.0)))
    return parts.astype(BF16)


def head_lanes(h, width):
    lane = lax.broadcasted_iota(jnp.int32, (1, width), 1) % 128
    keep = (lane >= h * HEAD_DIM) & (lane < (h + 1) * HEAD_DIM)
    return jnp.where(keep, 1.0, 0.0).astype(BF16)


def beside_parts(block):
    lane = lax.broadcasted_iota(jnp.int32, block.shape, 1) % HEAD_DIM
    return jnp.concatenate([block, jnp.where(lane < 3, 1.0, 0.0).astype(BF16)], axis=1)


def turned(block):
    return jnp.transpose(block.astype(F32)).astype(BF16)


def lane_blocks(w_ref, half):
    return lambda b: w_ref[256 * b : 256 * b + 256, 128 * half : 128 * half + 128]


def attention_forward(x, hv, length, wb, vec_ref, qa_ref, k_ref, v_ref, o_ref, att_ref):
    tokens = x.shape[0]
    unit, _ = unit_rows(x)
    normed = (unit * vec_ref[0:1] + vec_ref[1:2]).astype(BF16)
    qa_ref[:, 0:128] = ((mm(normed, wb(0)) + hv(0)) * Q_SCALE).astype(BF16)
    k_ref[...] = mm(normed, wb(1)).astype(BF16)
    v = (mm(normed, wb(2)) + hv(1)).astype(BF16)
    v_ref[...] = v

    def heads(v_turned, weighted, totals, tops):
        v_turned[...] = turned(v)

        def head_scores(h):
            return mm_nt(k_ref[...] * head_lanes(h, 128), qa_ref[:, 0:128])

        following = head_scores(0)
        ones = jnp.ones((HEAD_DIM, tokens), BF16)
        for h in range(4):
            scores = following
            if h < 3:
                following = head_scores(h + 1)
            highest = jnp.max(scores, axis=0, keepdims=True)
            probs = jnp.exp2(scores - highest).astype(BF16)
            rows = slice(HEAD_DIM * h, HEAD_DIM * h + HEAD_DIM)
            both = mm(jnp.concatenate([v_turned[rows, :], ones], axis=0), probs)
            weighted[rows, :] = both[:HEAD_DIM]
            totals[rows, :] = both[HEAD_DIM:]
            tops[rows, :] = jnp.broadcast_to(highest, (HEAD_DIM, tokens))

        o_ref[...] = jnp.transpose(weighted[...] / totals[...])
        log_total = tops[...] + jnp.log2(totals[...])
        qa_ref[:, 128:256] = three_parts(-jnp.transpose(log_total))

    pl.run_scoped(heads, pltpu.VMEM((128, tokens), BF16), *[pltpu.VMEM((128, tokens), F32)] * 3)
    lepe = conv(v_ref[...].astype(F32), hv, length, False)
    att_ref[...] = (o_ref[...] + lepe + hv(11)).astype(BF16)


def attention_backward(
    x, hv, length, grad, wb, vec_ref, qa_ref, k_ref, v_ref, o_ref, da_ref, gw_ref, rows_ref,
    between=None,
):
    tokens = x.shape[0]
    grad_f = grad.astype(F32)
    product = grad_f * o_ref[...]
    inner = jnp.zeros_like(product)
    for h in range(4):
        keep = head_mask(product.shape, h)
        inner = jnp.where(
            keep, jnp.sum(jnp.where(keep, product, 0.0), axis=-1, keepdims=True), inner
        )
    da_ref[:, 0:128] = grad
    da_ref[:, 128:256] = three_parts(-inner)

    def heads(k_turned, q_turned, grad_turned, k_wide, v_wide, dqs, dks, dvs):
        k_turned[...] = turned(k_ref[...])
        q_turned[...] = turned(qa_ref[:, 0:128])
        grad_turned[...] = turned(grad)
        k_wide[...] = beside_parts(k_ref[...])
        v_wide[...] = beside_parts(v_ref[...])

        def head_products(h):
            mask = head_lanes(h, 256)
            return mm_nt(qa_ref[...] * mask, k_wide[...]), mm_nt(da_ref[...] * mask, v_wide[...])

        early = tokens <= LONGEST
        following = head_products(0) if early else None
        for h in range(4):
            scores, grad_probs = following if early else head_products(h)
            if early and h < 3:
                following = head_products(h + 1)
            probs = jnp.exp2(scores)
            grad_scores = (probs * grad_probs).astype(BF16)
            rows = slice(HEAD_DIM * h, HEAD_DIM * h + HEAD_DIM)
            dvs[rows, :] = mm(grad_turned[rows, :], probs.astype(BF16))
            dks[rows, :] = mm(q_turned[rows, :], grad_scores)
            dqs[rows, :] = mm_nt(k_turned[rows, :], grad_scores)

        if between is not None:
            between()
        dq = (jnp.transpose(dqs[...]) * HEAD_DIM**-0.5).astype(BF16)
        dk = (jnp.transpose(dks[...]) * LN2).astype(BF16)
        dv = (jnp.transpose(dvs[...]) + conv(grad_f, hv, length, True)).astype(BF16)
        unit, _ = unit_rows(x)
        normed = (unit * vec_ref[0:1] + vec_ref[1:2]).astype(BF16)
        gw_ref[...] += mm_tn(normed, jnp.concatenate([dq, dk, dv], axis=1))
        rows_ref[0:1, :] += jnp.sum(dq.astype(F32), axis=0, keepdims=True)
        rows_ref[1:2, :] += jnp.sum(dv.astype(F32), axis=0, keepdims=True)
        for b, col in enumerate(shifted_columns(v_ref[...].astype(F32), length)):
            for a, val in enumerate(shifted_rows(col, length)):
                row = 2 + 3 * a + b
                rows_ref[row : row + 1, :] += jnp.sum(grad_f * val, axis=0, keepdims=True)
        rows_ref[11:12, :] += jnp.sum(grad_f, axis=0, keepdims=True)
        part = mm_nt(dq, wb(0)) + mm_nt(dk, wb(1)) + mm_nt(dv, wb(2))
        gain_row = jnp.sum(part * unit, axis=0, keepdims=True)
        shift_row = jnp.sum(part, axis=0, keepdims=True)
        for i in range(2):
            rows_ref[12 + i : 13 + i, :] += gain_row[:, 128 * i : 128 * i + 128]
            rows_ref[14 + i : 15 + i, :] += shift_row[:, 128 * i : 128 * i + 128]
        return part

    return pl.run_scoped(
        heads,
        *[pltpu.VMEM((128, tokens), BF16)] * 3,
        *[pltpu.VMEM((tokens, 256), BF16)] * 2,
        *[pltpu.VMEM((128, tokens), F32)] * 3,
    )


def feed_forward(x, att, top, w_ref, base, vec_ref, n2_ref, acc_ref, gn_ref, gp_ref, g1_ref, g2_ref, rows_ref):
    middle = x + mm(att, w_ref[base : base + 256, :]) + vec_ref[4:5]
    unit, inverse = unit_rows(middle)
    n2_ref[...] = (unit * vec_ref[5:6] + vec_ref[6:7]).astype(BF16)
    acc_ref[...] = middle + vec_ref[11:12]
    gn_ref[...] = jnp.zeros_like(gn_ref)
    for f in range(4):
        w1 = w_ref[base + 256 * (1 + f) : base + 256 * (2 + f), :]
        w2 = w_ref[base + 256 * (5 + f) : base + 256 * (6 + f), :]
        cols = slice(256 * f, 256 * f + 256)
        hidden = mm(n2_ref[...], w1) + vec_ref[7 + f : 8 + f]
        below = 0.5 * (1.0 + lax.erf(hidden * (0.5**0.5)))
        active = (hidden * below).astype(BF16)
        slope = below + hidden * jnp.exp(-0.5 * hidden * hidden) * 0.3989422804014327
        grad_hidden = (mm_nt(top, w2) * slope).astype(BF16)
        acc_ref[...] += mm(active, w2)
        gn_ref[...] += mm_nt(grad_hidden, w1)
        g1_ref[:, cols] += mm_tn(n2_ref[...], grad_hidden)
        g2_ref[:, cols] += mm_tn(top, active)
        rows_ref[3 + f : 4 + f, :] += jnp.sum(grad_hidden.astype(F32), axis=0, keepdims=True)
    grad_normed = gn_ref[...]
    top_f = top.astype(F32)
    grad_middle = top_f + norm_back(grad_normed, vec_ref[5:6], unit, inverse)
    branch = grad_middle.astype(BF16)
    gp_ref[...] += mm_tn(branch, att)
    rows_ref[0:1, :] += jnp.sum(branch.astype(F32), axis=0, keepdims=True)
    rows_ref[1:2, :] += jnp.sum(grad_normed * unit, axis=0, keepdims=True)
    rows_ref[2:3, :] += jnp.sum(grad_normed, axis=0, keepdims=True)
    rows_ref[7:8, :] += jnp.sum(top_f, axis=0, keepdims=True)
    grad_att = mm_nt(branch, w_ref[base : base + 256, :]).astype(BF16)
    return acc_ref[...].astype(BF16), grad_middle, grad_att


PARAMS = pltpu.CompilerParams(
    dimension_semantics=("arbitrary",), vmem_limit_bytes=VMEM_LIMIT
)


def whole(shape):
    return pl.BlockSpec(shape, lambda m: (0,) * len(shape))


def each(shape):
    return pl.BlockSpec((None,) + shape, lambda m: (m,) + (0,) * len(shape))


def shape_of(dtype, *shape):
    return jax.ShapeDtypeStruct(shape, dtype)


def pack_tokens(x, nb, length):
    micro, tokens, channels = x.shape

    def kernel(x_ref, o_ref, hot):
        @pl.when(pl.program_id(0) == 0)
        def _():
            hot[...] = order_out(nb, length)

        o_ref[...] = mm(hot[...], x_ref[...]).astype(BF16)

    return pl.pallas_call(
        kernel,
        grid=(micro,),
        in_specs=[each((tokens, channels))],
        out_specs=each((nb * PIECE, channels)),
        out_shape=shape_of(BF16, micro, nb * PIECE, channels),
        scratch_shapes=[pltpu.VMEM((nb * PIECE, tokens), BF16)],
        compiler_params=PARAMS,
        name="pack_tokens",
    )(x)


def forward_call(x, half, nb, length, weights, vectors):
    micro = x.shape[0]
    tokens = STRIPE * length
    packed = nb * PIECE

    def kernel(x_ref, w_ref, vec_ref, qa_ref, k_ref, v_ref, o_ref, att_ref, xs_ref, *scr):
        if half == 0:
            attention_forward(
                x_ref[...].astype(F32), half_rows(vec_ref, half), length, lane_blocks(w_ref, half), vec_ref, qa_ref, k_ref, v_ref, o_ref, att_ref
            )
        else:
            att_s, hot_in, hot_out = scr

            @pl.when(pl.program_id(0) == 0)
            def _():
                hot_in[...] = order_in(nb, length)
                hot_out[...] = order_out(nb, length)

            xs_ref[...] = mm(hot_in[...], x_ref[...]).astype(BF16)
            attention_forward(
                xs_ref[...].astype(F32), half_rows(vec_ref, half), length, lane_blocks(w_ref, half), vec_ref, qa_ref, k_ref, v_ref, o_ref, att_s
            )
            att_ref[...] = mm(hot_out[...], att_s[...]).astype(BF16)

    rows = tokens if half == 0 else packed
    scratch = []
    if half == 1:
        scratch += [
            pltpu.VMEM((tokens, 128), BF16),
            pltpu.VMEM((tokens, packed), BF16),
            pltpu.VMEM((packed, tokens), BF16),
        ]
    if half == 0:
        def body(x_ref, w_ref, vec_ref, qa_ref, k_ref, v_ref, o_ref, att_ref, *scr):
            kernel(x_ref, w_ref, vec_ref, qa_ref, k_ref, v_ref, o_ref, att_ref, None, *scr)
        extra_specs, extra_shapes = [], []
    else:
        body = kernel
        extra_specs = [each((tokens, 256))]
        extra_shapes = [shape_of(BF16, micro, tokens, 256)]
    return pl.pallas_call(
        body,
        grid=(micro,),
        in_specs=[each((rows, 256)), whole(weights.shape), whole(vectors.shape)],
        out_specs=[
            each((tokens, 256)),
            each((tokens, 128)),
            each((tokens, 128)),
            each((tokens, 128)),
            each((rows, 128)),
        ] + extra_specs,
        out_shape=[
            shape_of(BF16, micro, tokens, 256),
            shape_of(BF16, micro, tokens, 128),
            shape_of(BF16, micro, tokens, 128),
            shape_of(F32, micro, tokens, 128),
            shape_of(BF16, micro, rows, 128),
        ] + extra_shapes,
        scratch_shapes=scratch,
        compiler_params=PARAMS,
        name="attention_forward_%d" % half,
    )(x, weights, vectors)


def middle_call(x, att_h, att_v, top, nb, length, weights, vectors):
    micro, tokens, _ = x.shape
    packed = nb * PIECE

    def kernel(
        x_ref, h_ref, v_ref, top_ref, w_ref, vec_ref,
        out_ref, gm_ref, gh_ref, gv_ref, gp_ref, g1_ref, g2_ref, rows_ref,
        hot_in, hot_out, att, n2, acc, gn,
    ):
        @pl.when(pl.program_id(0) == 0)
        def _():
            hot_in[...] = order_in(nb, length)
            hot_out[...] = order_out(nb, length)
            for ref in (gp_ref, g1_ref, g2_ref, rows_ref):
                ref[...] = jnp.zeros_like(ref)

        att[:, 0:128] = h_ref[...]
        att[:, 128:256] = mm(hot_in[...], v_ref[...]).astype(BF16)
        out, grad_middle, grad_att = feed_forward(
            x_ref[...].astype(F32), att[...], top_ref[...], w_ref, ROW_PROJ, vec_ref, n2, acc, gn, gp_ref, g1_ref, g2_ref, rows_ref
        )
        out_ref[...] = out
        gm_ref[...] = grad_middle
        gh_ref[...] = grad_att[:, 0:128]
        gv_ref[...] = mm(hot_out[...], grad_att[:, 128:256]).astype(BF16)

    return pl.pallas_call(
        kernel,
        grid=(micro,),
        in_specs=[
            each((tokens, 256)), each((tokens, 128)), each((packed, 128)), each((tokens, 256)),
            whole(weights.shape), whole(vectors.shape),
        ],
        out_specs=[
            each((tokens, 256)), each((tokens, 256)), each((tokens, 128)), each((packed, 128)),
            whole((256, 256)), whole((256, 1024)), whole((256, 1024)), whole((8, 256)),
        ],
        out_shape=[
            shape_of(BF16, micro, tokens, 256), shape_of(F32, micro, tokens, 256),
            shape_of(BF16, micro, tokens, 128), shape_of(BF16, micro, packed, 128),
            shape_of(F32, 256, 256), shape_of(F32, 256, 1024), shape_of(F32, 256, 1024), shape_of(F32, 8, 256),
        ],
        scratch_shapes=[
            pltpu.VMEM((tokens, packed), BF16), pltpu.VMEM((packed, tokens), BF16),
            pltpu.VMEM((tokens, 256), BF16), pltpu.VMEM((tokens, 256), BF16),
            pltpu.VMEM((tokens, 256), F32), pltpu.VMEM((tokens, 256), F32),
        ],
        compiler_params=PARAMS,
        name="feed_forward",
    )(x, att_h, att_v, top, weights, vectors)


def backward_call(x, grad, qa, k, v, o, half, nb, length, weights, vectors):
    micro, tokens, _ = x.shape
    packed = nb * PIECE

    def kernel(
        x_ref, g_ref, qa_ref, k_ref, v_ref, o_ref, w_ref, vec_ref, gn_ref, gw_ref, rows_ref,
        da, *scr,
    ):
        @pl.when(pl.program_id(0) == 0)
        def _():
            gw_ref[...] = jnp.zeros_like(gw_ref)
            rows_ref[...] = jnp.zeros_like(rows_ref)
            if half == 1:
                scr[0][...] = order_in(nb, length)
                scr[1][...] = order_out(nb, length)

        grad_in = g_ref[...] if half == 0 else mm(scr[0][...], g_ref[...]).astype(BF16)
        part = attention_backward(
            x_ref[...].astype(F32), half_rows(vec_ref, half), length, grad_in, lane_blocks(w_ref, half), vec_ref, qa_ref, k_ref, v_ref, o_ref,
            da, gw_ref, rows_ref,
        )
        if half == 0:
            gn_ref[...] = part
        else:
            gn_ref[...] = mm(scr[1][...], part.astype(BF16)).astype(BF16)

    rows = tokens if half == 0 else packed
    scratch = [pltpu.VMEM((tokens, 256), BF16)]
    if half == 1:
        scratch += [pltpu.VMEM((tokens, packed), BF16), pltpu.VMEM((packed, tokens), BF16)]
    return pl.pallas_call(
        kernel,
        grid=(micro,),
        in_specs=[
            each((tokens, 256)), each((rows, 128)), each((tokens, 256)), each((tokens, 128)),
            each((tokens, 128)), each((tokens, 128)), whole(weights.shape), whole(vectors.shape),
        ],
        out_specs=[each((rows, 256)), whole((256, 384)), whole((16, 128))],
        out_shape=[
            shape_of(F32 if half == 0 else BF16, micro, rows, 256),
            shape_of(F32, 256, 384), shape_of(F32, 16, 128),
        ],
        scratch_shapes=scratch,
        compiler_params=PARAMS,
        name="attention_backward_%d" % half,
    )(x, grad, qa, k, v, o, weights, vectors)


def last_call(x, grad_middle, part_h, part_v, nb, length, vectors):
    micro, tokens, _ = x.shape
    packed = nb * PIECE

    def kernel(x_ref, gm_ref, h_ref, v_ref, vec_ref, out_ref, hot_in):
        @pl.when(pl.program_id(0) == 0)
        def _():
            hot_in[...] = order_in(nb, length)

        grad_normed = h_ref[...] + mm(hot_in[...], v_ref[...])
        unit, inverse = unit_rows(x_ref[...].astype(F32))
        out_ref[...] = (
            gm_ref[...] + norm_back(grad_normed, vec_ref[0:1], unit, inverse)
        ).astype(BF16)

    return pl.pallas_call(
        kernel,
        grid=(micro,),
        in_specs=[
            each((tokens, 256)), each((tokens, 256)), each((tokens, 256)), each((packed, 256)), whole(vectors.shape),
        ],
        out_specs=each((tokens, 256)),
        out_shape=shape_of(BF16, micro, tokens, 256),
        scratch_shapes=[pltpu.VMEM((tokens, packed), BF16)],
        compiler_params=PARAMS,
        name="input_gradient",
    )(x, grad_middle, part_h, part_v, vectors)


def repeat(lo, hi, body):
    def step(k, c):
        body(k)
        return c

    lax.fori_loop(lo, hi, step, 0)


def remote(src, dst, ss, rs, dev):
    return pltpu.make_async_remote_copy(
        src_ref=src, dst_ref=dst, send_sem=ss, recv_sem=rs, device_id=dev, device_id_type=MESH
    )


def await_bytes(ref, sem):
    pltpu.make_async_copy(ref, ref, sem).wait()


class Swap:
    def __init__(self, n, out_ref, in_ref, send_sem, recv_sem):
        self.n, self.out, self.into, self.ss, self.rs = n, out_ref, in_ref, send_sem, recv_sem
        self.me = lax.axis_index("band")

    def rows(self, i):
        return pl.ds(pl.multiple_of(i * PIECE, PIECE), PIECE)

    def send(self, m):
        mine = self.rows(self.me)

        def one(k):
            d = lax.rem(self.me + k, self.n)
            remote(
                self.out.at[m, self.rows(d)],
                self.into.at[m, mine],
                self.ss.at[m],
                self.rs.at[m],
                {"band": d},
            ).start()

        repeat(1, self.n, one)
        self.into[m, mine, :] = self.out[m, mine, :]

    def wait(self, m):
        others = pl.ds(0, (self.n - 1) * PIECE)
        await_bytes(self.out.at[m, others], self.ss.at[m])
        await_bytes(self.into.at[m, others], self.rs.at[m])


class Sum:
    def __init__(self, nb, nx, x_ref, o_ref, got, half, recv, sems):
        self.nx = nx
        self.nq = (nb // 2) * nx
        self.p = x_ref.shape[0] // (2 * self.nq)
        band = lax.axis_index("band")
        self.core = lax.rem(band, 2)
        self.q = (band // 2) * nx + lax.axis_index("batch")
        self.sibling = {"band": band + 1 - 2 * self.core}
        self.x, self.o, self.got, self.half, self.recv = x_ref, o_ref, got, half, recv
        self.sems = sems

    def chip(self, t):
        return {"band": (t // self.nx) * 2 + self.core, "batch": lax.rem(t, self.nx)}

    def ahead(self, k):
        return lax.rem(self.q + k, self.nq)

    def behind(self, k):
        return lax.rem(self.q - k + self.nq, self.nq)

    def side(self, c):
        rows = self.nq * self.p
        return pl.ds(pl.multiple_of(c * rows, 16), rows)

    def wide(self, c, t):
        return pl.ds(pl.multiple_of((c * self.nq + t) * self.p, 16), self.p)

    def thin(self, t):
        return pl.ds(pl.multiple_of(t * self.p, 16), self.p)

    def sem(self, i):
        return self.sems.at[2 * i], self.sems.at[2 * i + 1]

    def arrived(self, i, sent, came):
        await_bytes(sent, self.sems.at[2 * i])
        await_bytes(came, self.sems.at[2 * i + 1])

    def pair_copy(self, c):
        return remote(self.x.at[self.side(c)], self.got, *self.sem(0), self.sibling)

    def start(self):
        self.pair_copy(1 - self.core).start()

    def scatter(self):
        self.pair_copy(self.core).wait()
        self.half[...] = (
            self.x[self.side(self.core)].astype(F32) + self.got[...].astype(F32)
        ).astype(BF16)

        def one(k):
            t = self.ahead(k)
            remote(
                self.half.at[self.thin(t)],
                self.recv.at[self.thin(self.q)],
                *self.sem(1),
                self.chip(t),
            ).start()

        repeat(1, self.nq, one)
        self.recv[self.thin(self.q)] = self.half[self.thin(self.q)]

    def gather(self):
        others = pl.ds(0, (self.nq - 1) * self.p)
        self.arrived(1, self.half.at[others], self.recv.at[others])
        total = self.recv[0 : self.p].astype(F32)
        for t in range(1, self.nq):
            total = total + self.recv[t * self.p : (t + 1) * self.p].astype(F32)
        mine = self.wide(self.core, self.q)
        self.o[mine] = total.astype(BF16)

        def give(k):
            remote(
                self.o.at[mine], self.o.at[mine], *self.sem(2), self.chip(self.ahead(k))
            ).start()

        repeat(1, self.nq, give)

    def pass_on(self, c):
        return remote(
            self.o.at[self.side(self.core)], self.o.at[self.side(c)], *self.sem(3), self.sibling
        )

    def relay(self):
        others = pl.ds(0, (self.nq - 1) * self.p)
        self.arrived(2, self.o.at[others], self.o.at[others])
        self.pass_on(self.core).start()

    def finish(self):
        self.pass_on(1 - self.core).wait()


class DeepSum:
    def __init__(self, nb, nx, x_ref, o_ref, got, half, recv, deep, deep_recv, sems):
        self.nx = nx
        self.n1, self.n2 = 2 * nx, nb // 4
        self.p = x_ref.shape[0] // (2 * self.n1 * self.n2)
        band = lax.axis_index("band")
        self.core = lax.rem(band, 2)
        self.j1 = lax.rem(band // 2, 2) * nx + lax.axis_index("batch")
        self.j2 = band // 4
        self.sibling = {"band": band + 1 - 2 * self.core}
        self.x, self.o, self.got, self.half, self.recv = x_ref, o_ref, got, half, recv
        self.deep, self.deep_recv = deep, deep_recv
        self.sems = sems

    def near(self, t):
        return {
            "band": self.j2 * 4 + (t // self.nx) * 2 + self.core,
            "batch": lax.rem(t, self.nx),
        }

    def far(self, t):
        return {"band": t * 4 + lax.rem(lax.axis_index("band"), 4)}

    def near_at(self, k):
        return lax.rem(self.j1 + k, self.n1)

    def far_at(self, k):
        return lax.rem(self.j2 + k, self.n2)

    def block(self, c, t):
        rows = self.n2 * self.p
        return pl.ds(pl.multiple_of((c * self.n1 + t) * rows, 16), rows)

    def thin(self, t):
        rows = self.n2 * self.p
        return pl.ds(pl.multiple_of(t * rows, 16), rows)

    def piece(self, t):
        return pl.ds(pl.multiple_of(t * self.p, 16), self.p)

    def o_piece(self, t):
        at = (self.core * self.n1 + self.j1) * self.n2 + t
        return self.o.at[pl.ds(pl.multiple_of(at * self.p, 16), self.p)]

    def sem(self, i):
        return self.sems.at[2 * i], self.sems.at[2 * i + 1]

    def arrived(self, i, sent, came):
        await_bytes(sent, self.sems.at[2 * i])
        await_bytes(came, self.sems.at[2 * i + 1])

    def side(self, c):
        rows = self.n1 * self.n2 * self.p
        return pl.ds(pl.multiple_of(c * rows, 16), rows)

    def pair_copy(self, c):
        return remote(self.x.at[self.side(c)], self.got, *self.sem(0), self.sibling)

    def start(self):
        self.pair_copy(1 - self.core).start()

    def scatter(self):
        self.pair_copy(self.core).wait()
        self.half[...] = (
            self.x[self.side(self.core)].astype(F32) + self.got[...].astype(F32)
        ).astype(BF16)

        def one(k):
            t = self.near_at(k)
            remote(
                self.half.at[self.thin(t)],
                self.recv.at[self.thin(self.j1)],
                *self.sem(1),
                self.near(t),
            ).start()

        repeat(1, self.n1, one)

    def scatter_far(self):
        others = pl.ds(0, (self.n1 - 1) * self.n2 * self.p)
        self.arrived(1, self.half.at[others], self.recv.at[others])
        total = self.half[self.thin(self.j1)].astype(F32)
        for k in range(1, self.n1):
            total = total + self.recv[self.thin(self.near_at(k))].astype(F32)
        self.deep[...] = total.astype(BF16)

        def give(k):
            t = self.far_at(k)
            remote(
                self.deep.at[self.piece(t)],
                self.deep_recv.at[self.piece(self.j2)],
                *self.sem(2),
                self.far(t),
            ).start()

        repeat(1, self.n2, give)

    def gather(self):
        others = pl.ds(0, (self.n2 - 1) * self.p)
        self.arrived(2, self.deep.at[others], self.deep_recv.at[others])
        total = self.deep[self.piece(self.j2)].astype(F32)
        for k in range(1, self.n2):
            total = total + self.deep_recv[self.piece(self.far_at(k))].astype(F32)
        at = (self.core * self.n1 + self.j1) * self.n2 + self.j2
        self.o[pl.ds(pl.multiple_of(at * self.p, 16), self.p)] = total.astype(BF16)
        mine = self.o_piece(self.j2)
        repeat(
            1,
            self.n2,
            lambda k: remote(mine, mine, *self.sem(3), self.far(self.far_at(k))).start(),
        )

    def gather_near(self):
        others = pl.ds(0, (self.n2 - 1) * self.p)
        self.arrived(3, self.o.at[others], self.o.at[others])
        mine = self.o.at[self.block(self.core, self.j1)]
        repeat(
            1,
            self.n1,
            lambda k: remote(mine, mine, *self.sem(4), self.near(self.near_at(k))).start(),
        )

    def pass_on(self, c):
        return remote(
            self.o.at[self.side(self.core)], self.o.at[self.side(c)], *self.sem(5), self.sibling
        )

    def relay(self):
        others = pl.ds(0, (self.n1 - 1) * self.n2 * self.p)
        self.arrived(4, self.o.at[others], self.o.at[others])
        self.pass_on(self.core).start()

    def finish(self):
        self.pass_on(1 - self.core).wait()


ROWS_A = 1536
ROWS_B = 2304
ROWS_G = 800


def up(rows, unit):
    return -(-rows // unit) * unit


def split_rows(ref, at, rows):
    n = rows.shape[0]
    high = rows.astype(BF16)
    ref[at : at + n, :] = high
    ref[at + n : at + 2 * n, :] = (rows - high.astype(F32)).astype(BF16)


def block_kernel(
    nb, nx, length,
    own_ref, x_ref, wq_ref, vec_ref, top_hbm, wp_hbm, w1_hbm, w2_hbm,
    out_ref, ing_ref, gb_ref, gav_ref, gah_ref,
    wa_in, wb_in, wa, wb, gb_in, gav_in, gah_in,
    wide_got, wide_half, wide_recv, wide_deep, wide_deep_recv,
    a_got, a_half, a_recv, a_deep, a_deep_recv,
    gb_got, gb_half, gb_recv, gb_deep, gb_deep_recv,
    v_got, v_half, v_recv, v_deep, v_deep_recv, h_got, h_half, h_recv,
    hot_in, hot_out, x_out, x_in, a_out, a_in, g_in, p_in,
    xs, qa, ks, vs, os, att_w, att, n2, acc, gn, gm, grad_w, part_w, hv_ref,
    gp, g1, g2, rows_mid, gw, rows, da,
    x_ss, x_rs, a_ss, a_rs, g_ss, g_rs, p_ss, p_rs,
    wa_sem, wb_sem, gb_sem, gav_sem, gah_sem,
    top_ref, wp_ref, w1_ref, w2_ref, fetch_sem,
):
    fetches = [
        pltpu.make_async_copy(src, dst, fetch_sem.at[i])
        for i, (src, dst) in enumerate(
            ((wp_hbm, wp_ref), (w1_hbm, w1_ref), (w2_hbm, w2_ref), (top_hbm, top_ref))
        )
    ]
    for c in fetches:
        c.start()
    band = lax.axis_index("band")
    batch = lax.axis_index("batch")
    device = band * nx + batch
    micro = x_ref.shape[0]
    core = lax.rem(band, 2)
    bar = pltpu.get_barrier_semaphore()
    repeat(
        1,
        nb,
        lambda k: pl.semaphore_signal(
            bar, inc=1, device_id={"band": lax.rem(band + k, nb)}, device_id_type=MESH
        ),
    )

    def greet(t):
        other = lax.rem(batch + 1 + t // (nb // 2), nx)
        pl.semaphore_signal(
            bar,
            inc=1,
            device_id={"band": lax.rem(t, nb // 2) * 2 + core, "batch": other},
            device_id_type=MESH,
        )

    repeat(0, (nb // 2) * (nx - 1), greet)

    sum_wa = DeepSum(
        nb, nx, wa_in, wa, a_got, a_half, a_recv, a_deep, a_deep_recv, wa_sem
    )
    sum_wb = DeepSum(
        nb, nx, wb_in, wb, wide_got, wide_half, wide_recv, wide_deep, wide_deep_recv, wb_sem
    )
    sum_gb = DeepSum(
        nb, nx, gb_in, gb_ref, gb_got, gb_half, gb_recv, gb_deep, gb_deep_recv, gb_sem
    )
    sum_gav = DeepSum(
        nb, nx, gav_in, gav_ref, v_got, v_half, v_recv, v_deep, v_deep_recv, gav_sem
    )
    sum_gah = Sum(nb, nx, gah_in, gah_ref, h_got, h_half, h_recv, gah_sem)
    swap_x = Swap(nb, x_out, x_in, x_ss, x_rs)
    swap_a = Swap(nb, a_out, a_in, a_ss, a_rs)
    swap_g = Swap(nb, a_out, g_in, g_ss, g_rs)
    swap_p = Swap(nb, x_out, p_in, p_ss, p_rs)

    def own(ref, which, cols):
        return jnp.where(own_ref[which] == device, ref[0, :, cols], 0.0).astype(BF16)

    for b in range(6):
        wa_in[256 * b : 256 * b + 256, :] = own(wq_ref, 0, slice(128 * b, 128 * b + 128))
    if wa_in.shape[0] > ROWS_A:
        wa_in[ROWS_A:, :] = jnp.zeros((wa_in.shape[0] - ROWS_A, 128), BF16)
    pl.semaphore_wait(bar, nb - 1 + (nb // 2) * (nx - 1))
    sum_wa.start()
    sum_wa.scatter()
    for c in fetches[:3]:
        c.wait()
    wb_in[0:256, :] = own(wp_ref, 1, slice(0, 256))
    for f in range(4):
        wb_in[256 * (f + 1) : 256 * (f + 2), :] = own(w1_ref, 2, slice(256 * f, 256 * f + 256))
    wb_in[1280:ROWS_B, :] = own(w2_ref, 3, slice(0, 256))
    wb_in[ROWS_B:, :] = jnp.zeros((wb_in.shape[0] - ROWS_B, 256), BF16)
    sum_wb.start()
    hot_out[...] = order_out(nb, length)
    x_out[0] = mm(hot_out[...], x_ref[0]).astype(BF16)
    sum_wa.scatter_far()
    swap_x.send(0)
    sum_wb.scatter()
    sum_wa.gather()
    hot_in[...] = order_in(nb, length)
    for m in range(1, micro):
        x_out[m] = mm(hot_out[...], x_ref[m]).astype(BF16)
    sum_wa.gather_near()
    for m in range(1, micro):
        swap_x.send(m)
    sum_wa.relay()
    for ref in (gp, g1, g2, rows_mid, gw, rows):
        ref[...] = jnp.zeros_like(ref)
    for half in range(2):
        get = half_rows(vec_ref, half)
        for i in range(12):
            hv_ref[half, i : i + 1, :] = get(i)
    for m in range(micro):
        xs[m] = x_ref[m]
    sum_wa.finish()

    def blocks(half):
        return lambda b: wa[pl.ds(pl.multiple_of(256 * (2 * b + half), 256), 256), :]

    def vectors_of(half):
        return lambda i: hv_ref[half, i : i + 1, :]

    def forward_step(w):
        half, m = w // micro, lax.rem(w, micro)

        @pl.when(w >= micro)
        def _():
            swap_x.wait(m)
            xs[w] = mm(hot_in[...], x_in[m]).astype(BF16)

        attention_forward(
            xs[w].astype(F32), vectors_of(half), length, blocks(half), vec_ref,
            qa.at[w], ks.at[w], vs.at[w], os.at[w], att_w.at[w],
        )

        @pl.when(w >= micro)
        def _():
            a_out[m] = mm(hot_out[...], att_w[w]).astype(BF16)
            swap_a.send(m)

        pl.when(w == 0)(sum_wb.scatter_far)
        pl.when(w == micro - 1)(sum_wb.gather)
        pl.when(w == micro)(sum_wb.gather_near)

    repeat(0, 2 * micro, forward_step)
    sum_wb.relay()
    sum_wb.finish()
    fetches[3].wait()

    def middle_step(m):
        swap_a.wait(m)
        att[:, 0:128] = att_w[m]
        att[:, 128:256] = mm(hot_in[...], a_in[m]).astype(BF16)
        out, grad_middle, grad_att = feed_forward(
            x_ref[m].astype(F32), att[...], top_ref[m], wb, 0, vec_ref, n2, acc, gn,
            gp, g1, g2, rows_mid,
        )
        out_ref[m] = out
        gm[m] = grad_middle
        grad_w[m] = grad_att[:, 0:128]
        a_out[m] = mm(hot_out[...], grad_att[:, 128:256]).astype(BF16)
        swap_g.send(m)

    repeat(0, micro, middle_step)
    gb_in[0:256, :] = jnp.transpose(gp[...]).astype(BF16)
    for f in range(4):
        cols = slice(256 * f, 256 * f + 256)
        gb_in[256 * (f + 1) : 256 * (f + 2), :] = g1[:, cols].astype(BF16)
        gb_in[1280 + 256 * f : 1536 + 256 * f, :] = jnp.transpose(g2[:, cols]).astype(BF16)
    gb_in[ROWS_B:, :] = jnp.zeros((gb_in.shape[0] - ROWS_B, 256), BF16)
    split_rows(gb_in, ROWS_B, rows_mid[...])
    sum_gb.start()

    def fill(ref, half):
        for b in range(3):
            ref[256 * b : 256 * b + 256, :] = gw[half, :, 128 * b : 128 * b + 128].astype(BF16)
        split_rows(ref, 768, rows[half])
        ref[ROWS_G:, :] = jnp.zeros((ref.shape[0] - ROWS_G, 128), BF16)

    def backward_step(i):
        w = lax.rem(i + micro, 2 * micro)
        half, m = w // micro, lax.rem(w, micro)

        @pl.when(w >= micro)
        def _():
            swap_g.wait(m)
            grad_w[w] = mm(hot_in[...], g_in[m]).astype(BF16)

        def between():
            pl.when(i == 0)(sum_gb.scatter)
            pl.when(i == micro - 1)(sum_gb.scatter_far)

            @pl.when(i == micro)
            def _():
                sum_gb.gather()
                sum_gav.scatter()

            @pl.when(i == 2 * micro - 1)
            def _():
                sum_gb.gather_near()
                sum_gav.gather()

        into = jnp.where(w >= micro, micro, m)
        part_w[into] = attention_backward(
            xs[w].astype(F32), vectors_of(half), length, grad_w[w], blocks(half), vec_ref,
            qa.at[w], ks.at[w], vs.at[w], os.at[w], da, gw.at[half], rows.at[half],
            between,
        )

        @pl.when(w >= micro)
        def _():
            x_out[m] = mm(hot_out[...], part_w[micro].astype(BF16)).astype(BF16)
            swap_p.send(m)

        @pl.when(i == micro - 1)
        def _():
            fill(gav_in, 1)
            sum_gav.start()

        pl.when(i == micro)(sum_gav.scatter_far)

    repeat(0, 2 * micro, backward_step)
    fill(gah_in, 0)
    sum_gah.start()
    sum_gav.gather_near()
    sum_gah.scatter()
    sum_gb.relay()

    def last_step(m):
        swap_p.wait(m)
        grad_normed = part_w[m] + mm(hot_in[...], p_in[m])
        unit, inverse = unit_rows(x_ref[m].astype(F32))
        ing_ref[m] = (gm[m] + norm_back(grad_normed, vec_ref[0:1], unit, inverse)).astype(BF16)

    last_step(0)
    sum_gah.gather()
    sum_gav.relay()
    repeat(1, micro, last_step)
    sum_gah.relay()
    sum_gb.finish()
    sum_gav.finish()
    sum_gah.finish()


def block_call(x, top, owners, w_qkv, w_proj, w_fc1, w_fc2, vectors, nb, nx, length):
    micro, tokens, _ = x.shape
    packed = nb * PIECE
    nq = nb // 2 * nx
    unit = 32 * nq
    ra, rb, rg = up(ROWS_A, unit), up(ROWS_B + 16, unit), up(ROWS_G, unit)
    vm = pltpu.VMEM
    windows = 2 * micro

    def steps(rows, cols):
        return [vm((rows // 2, cols), BF16)] * 3

    def deep_steps(rows, cols):
        return steps(rows, cols) + [vm((rows // (4 * nx), cols), BF16)] * 2

    scratch = (
        [vm((ra, 128), BF16), vm((rb, 256), BF16), vm((ra, 128), BF16), vm((rb, 256), BF16)]
        + [vm((rb, 256), BF16), vm((rg, 128), BF16), vm((rg, 128), BF16)]
        + deep_steps(rb, 256) + deep_steps(ra, 128) + deep_steps(rb, 256) + deep_steps(rg, 128)
        + steps(rg, 128)
        + [vm((tokens, packed), BF16), vm((packed, tokens), BF16)]
        + [vm((micro, packed, 256), BF16)] * 2
        + [vm((micro, packed, 128), BF16)] * 3
        + [vm((micro, packed, 256), BF16)]
        + [
            vm((windows, tokens, 256), BF16),
            vm((windows, tokens, 256), BF16),
            vm((windows, tokens, 128), BF16),
            vm((windows, tokens, 128), BF16),
            vm((windows, tokens, 128), F32),
            vm((windows, tokens, 128), BF16),
            vm((tokens, 256), BF16),
            vm((tokens, 256), BF16),
            vm((tokens, 256), F32),
            vm((tokens, 256), F32),
            vm((micro, tokens, 256), F32),
            vm((windows, tokens, 128), BF16),
            vm((micro + 1, tokens, 256), F32),
            vm((2, 16, 128), F32),
            vm((256, 256), F32),
            vm((256, 1024), F32),
            vm((256, 1024), F32),
            vm((8, 256), F32),
            vm((2, 256, 384), F32),
            vm((2, 16, 128), F32),
            vm((tokens, 256), BF16),
        ]
        + [pltpu.SemaphoreType.DMA((micro,))] * 8
        + [pltpu.SemaphoreType.DMA((k,)) for k in (12, 12, 12, 12, 8)]
        + [vm(top.shape, BF16)]
        + [vm(w.shape, F32) for w in (w_proj, w_fc1, w_fc2)]
        + [pltpu.SemaphoreType.DMA((4,))]
    )
    whole_vmem = pl.BlockSpec(memory_space=vm)
    return pl.pallas_call(
        functools.partial(block_kernel, nb, nx, length),
        in_specs=[pl.BlockSpec(memory_space=pltpu.SMEM)]
        + [whole_vmem] * 3
        + [pl.BlockSpec(memory_space=pl.ANY)] * 4,
        out_specs=[whole_vmem] * 5,
        out_shape=[
            shape_of(BF16, micro, tokens, 256), shape_of(BF16, micro, tokens, 256),
            shape_of(BF16, rb, 256), shape_of(BF16, rg, 128), shape_of(BF16, rg, 128),
        ],
        scratch_shapes=scratch,
        compiler_params=pltpu.CompilerParams(
            collective_id=0, has_side_effects=True, vmem_limit_bytes=VMEM_LIMIT
        ),
        name="block",
    )(owners, x, w_qkv, vectors, top, w_proj, w_fc1, w_fc2)


def adam_kernel(
    own_ref, gb_ref, gav_ref, gah_ref, vec_ref, vf_ref, vs_ref, *refs,
):
    through = refs[0:2]
    moments = refs[2:14]
    bases = refs[14:22]
    grads_hbm = refs[22:26]
    outs = refs[26:38]
    vg_ref, vfn_ref, vsn_ref, vn_ref = refs[38:42]
    through_out = refs[42:44]
    held = refs[44:56]
    left = refs[56:64]
    grads = refs[64:68]
    zeros_ref, in_sem, out_sem, grad_sem, through_sem = refs[68:73]
    device = lax.axis_index("band") * lax.axis_size("batch") + lax.axis_index("batch")
    is_own = [own_ref[i] == device for i in range(4)]
    any_own = is_own[0] | is_own[1] | is_own[2] | is_own[3]

    def load(i):
        pairs = [(moments[3 * i + j].at[0], held[3 * i + j], 5 * i + j) for j in range(3)]
        pairs += [(bases[2 * i + j], left[2 * i + j], 5 * i + 3 + j) for j in range(2)]
        return [pltpu.make_async_copy(a, b, in_sem.at[s]) for a, b, s in pairs]

    def store(i, j):
        at = 3 * i + j
        return pltpu.make_async_copy(held[at], outs[at].at[0], out_sem.at[at])

    def blank(i):
        copies = []
        for j in range(3):
            shape = outs[3 * i + j].shape
            copies.append(
                pltpu.make_async_copy(
                    zeros_ref.at[pl.ds(0, shape[1]), pl.ds(0, shape[2])],
                    outs[3 * i + j].at[0],
                    out_sem.at[3 * i + j],
                )
            )
        return copies

    def start_blanks():
        for i in range(4):
            @pl.when(jnp.logical_not(is_own[i]))
            def _():
                for c in blank(i):
                    c.start()

    for i in range(4):
        @pl.when(is_own[i])
        def _():
            for c in load(i):
                c.start()

    zeros_ref[...] = jnp.zeros_like(zeros_ref)
    pl.when(jnp.logical_not(any_own))(start_blanks)
    passing = [
        pltpu.make_async_copy(a, b, through_sem.at[i])
        for i, (a, b) in enumerate(zip(through, through_out))
    ]
    for c in passing:
        c.start()

    for b in range(3):
        for half, ref in ((0, gah_ref), (1, gav_ref)):
            at = 256 * b + 128 * half
            grads[0][:, at : at + 128] = ref[256 * b : 256 * b + 256, :].astype(F32)
    grads[1][...] = gb_ref[0:256, :].astype(F32)
    for f in range(4):
        grads[2][:, 256 * f : 256 * f + 256] = gb_ref[256 * (f + 1) : 256 * (f + 2), :].astype(F32)
    grads[3][...] = gb_ref[1280:ROWS_B, :].astype(F32)
    giving = [pltpu.make_async_copy(grads[i], grads_hbm[i], grad_sem.at[i]) for i in range(4)]
    for c in giving:
        c.start()

    mid = gb_ref[ROWS_B : ROWS_B + 8, :].astype(F32) + gb_ref[ROWS_B + 8 : ROWS_B + 16, :].astype(F32)
    side = [r[768:784, :].astype(F32) + r[784:800, :].astype(F32) for r in (gah_ref, gav_ref)]
    both = side[0] + side[1]
    for i in range(2):
        vg_ref[0:1, 128 * i : 128 * i + 128] = both[12 + i : 13 + i]
        vg_ref[1:2, 128 * i : 128 * i + 128] = both[14 + i : 15 + i]
        vg_ref[2:4, 128 * i : 128 * i + 128] = side[i][0:2]
        vg_ref[21:22, 128 * i : 128 * i + 128] = side[i][11:12]
        for t in range(9):
            row = 12 + (t if i == 0 else 3 * (t % 3) + t // 3)
            vg_ref[row : row + 1, 128 * i : 128 * i + 128] = side[i][2 + t : 3 + t]
    vg_ref[4:12, :] = mid
    grad = vg_ref[...]
    first_new = BETA_ONE * vf_ref[...] + (1.0 - BETA_ONE) * grad
    second_new = BETA_TWO * vs_ref[...] + (1.0 - BETA_TWO) * grad * grad
    vfn_ref[...] = first_new
    vsn_ref[...] = second_new
    vn_ref[...] = vec_ref[...] - RATE_VECTORS * (first_new / (1.0 - BETA_ONE**STEP)) / (
        jnp.sqrt(second_new / (1.0 - BETA_TWO**STEP)) + EPS_ADAM
    )

    for i in range(4):
        @pl.when(is_own[i])
        def _():
            for c in load(i):
                c.wait()

    pl.when(any_own)(start_blanks)

    for i in range(4):
        @pl.when(is_own[i])
        def _():
            first, second, weight = held[3 * i], held[3 * i + 1], held[3 * i + 2]
            g = grads[i][...].astype(BF16)
            lh, rh = left[2 * i][...].astype(BF16), left[2 * i + 1][...].astype(BF16)
            once = jnp.transpose(mm_tn(g, lh)) if i == 3 else mm_tn(lh, g)
            turned_grad = mm(once.astype(BF16), rh)
            first_new = BETA_ONE * first[...] + (1.0 - BETA_ONE) * turned_grad
            second_new = BETA_TWO * second[...] + (1.0 - BETA_TWO) * turned_grad * turned_grad
            first[...] = first_new
            second[...] = second_new
            store(i, 0).start()
            store(i, 1).start()
            step = (first_new / (1.0 - BETA_ONE**STEP)) / (
                jnp.sqrt(second_new / (1.0 - BETA_TWO**STEP)) + EPS_ADAM
            )
            back = mm_nt(mm(lh, step.astype(BF16)).astype(BF16), rh)
            weight[...] = weight[...] - RATE * back - RATE * DECAY * weight[...]
            store(i, 2).start()

    for c in giving + passing:
        c.wait()
    for i in range(4):
        for j in range(3):
            store(i, j).wait()


def adam_call(
    owners, gb, gav, gah, vectors, vectors_first, vectors_second, through, slots, bases
):
    vm = pltpu.VMEM
    any_space = pl.BlockSpec(memory_space=pl.ANY)
    vspec = pl.BlockSpec(memory_space=vm)
    sizes = [(s.shape[1], s.shape[2]) for s in slots[::3]]
    vshape = shape_of(F32, *vectors.shape)
    tallest = max(a for a, _ in sizes)
    widest = max(b for _, b in sizes)
    dma = pltpu.SemaphoreType.DMA
    return pl.pallas_call(
        adam_kernel,
        in_specs=[pl.BlockSpec(memory_space=pltpu.SMEM)] + [vspec] * 8 + [any_space] * 20,
        out_specs=[any_space] * 16 + [vspec] * 4 + [any_space] * 2,
        out_shape=[shape_of(F32, *s) for s in sizes]
        + [shape_of(F32, *s.shape) for s in slots]
        + [vshape] * 4
        + [shape_of(t.dtype, *t.shape) for t in through],
        scratch_shapes=[vm((s.shape[1], s.shape[2]), F32) for s in slots]
        + [vm(b.shape, F32) for b in bases]
        + [vm(s, F32) for s in sizes]
        + [vm((tallest, widest), F32), dma((20,)), dma((12,)), dma((4,)), dma((2,))],
        compiler_params=pltpu.CompilerParams(vmem_limit_bytes=VMEM_LIMIT),
        name="adam",
    )(owners, gb, gav, gah, vectors, vectors_first, vectors_second, *through, *slots, *bases)


def wide_to_stack(w):
    n = w.shape[1] // 256
    return w.reshape(256, n, 256).transpose(1, 0, 2).reshape(256 * n, 256)


def by_steps(x, top, owners, slots, vectors, nb, nx, length):
    device_index = lax.axis_index(("band", "batch"))

    def own(slot, which):
        return jnp.where(device_index == owners[which], slot[0], 0.0).astype(BF16)

    stacked = jnp.concatenate(
        [
            wide_to_stack(own(slots[0], 0)),
            own(slots[1], 1),
            wide_to_stack(own(slots[2], 2)),
            own(slots[3], 3),
        ],
        axis=0,
    )
    weights = sum_everywhere(stacked, nb, nx, 0)[:ROW_END]

    def swap(packed, cid):
        m, rows, ch = packed.shape
        swapped = packed.reshape(m, nb, PIECE, ch).transpose(1, 0, 2, 3).reshape(m * rows, ch)
        got = exchange(swapped, nb, cid)
        return got.reshape(nb, m, PIECE, ch).transpose(1, 0, 2, 3).reshape(m, rows, ch)

    columns = swap(pack_tokens(x, nb, length), 1)
    qa_v, k_v, v_v, o_v, att_v, x_v = forward_call(columns, 1, nb, length, weights, vectors)
    qa_h, k_h, v_h, o_h, att_h = forward_call(x, 0, nb, length, weights, vectors)
    att_v = swap(att_v, 2)
    block_out, grad_middle, grad_h, grad_v, gp_t, g1, g2_t, rows_mid = middle_call(
        x, att_h, att_v, top, nb, length, weights, vectors
    )
    grad_v = swap(grad_v, 3)
    part_v, gw_v, rows_v = backward_call(
        x_v, grad_v, qa_v, k_v, v_v, o_v, 1, nb, length, weights, vectors
    )
    part_h, gw_h, rows_h = backward_call(
        x, grad_h, qa_h, k_h, v_h, o_h, 0, nb, length, weights, vectors
    )
    part_v = swap(part_v, 4)
    input_grad = last_call(x, grad_middle, part_h, part_v, nb, length, vectors)

    def two(rows):
        high = rows.astype(BF16)
        return [high, (rows - high.astype(F32)).astype(BF16)]

    gb = jnp.concatenate(
        [gp_t.T.astype(BF16), wide_to_stack(g1.astype(BF16)), g2_t.T.astype(BF16)] + two(rows_mid),
        axis=0,
    )

    def side(gw, rows):
        return jnp.concatenate(
            [gw[:, 128 * b : 128 * b + 128].astype(BF16) for b in range(3)] + two(rows), axis=0
        )

    gb = sum_everywhere(gb, nb, nx, 5)
    gav = sum_everywhere(side(gw_v, rows_v), nb, nx, 6)
    gah = sum_everywhere(side(gw_h, rows_h), nb, nx, 7)
    return block_out, input_grad, gb, gav, gah


def per_device(
    tokens_in, cotangent, owners,
    weight_qkv, weight_proj, weight_fc1, weight_fc2,
    first_qkv, second_qkv, first_proj, second_proj, first_fc1, second_fc1, first_fc2, second_fc2,
    left_qkv, right_qkv, left_proj, right_proj, left_fc1, right_fc1, left_fc2, right_fc2,
    vectors, vectors_first, vectors_second,
    *, nb, nx,
):
    micro, images, band_rows, length, channels = tokens_in.shape
    tokens = band_rows * length
    x = tokens_in.reshape(micro * images, tokens, channels)
    top = cotangent.reshape(micro * images, tokens, channels)
    weights = (weight_qkv, weight_proj, weight_fc1, weight_fc2)
    if tokens <= LONGEST:
        block_out, input_grad, gb, gav, gah = block_call(
            x, top, owners, *weights, vectors, nb, nx, length
        )
    else:
        block_out, input_grad, gb, gav, gah = by_steps(
            x, top, owners, weights, vectors, nb, nx, length
        )
    slots = (
        first_qkv, second_qkv, weight_qkv, first_proj, second_proj, weight_proj,
        first_fc1, second_fc1, weight_fc1, first_fc2, second_fc2, weight_fc2,
    )
    bases = (left_qkv, right_qkv, left_proj, right_proj, left_fc1, right_fc1, left_fc2, right_fc2)
    done = adam_call(
        owners, gb, gav, gah, vectors, vectors_first, vectors_second,
        (block_out, input_grad), slots, bases,
    )
    results = [done[20].reshape(tokens_in.shape), done[21].reshape(tokens_in.shape)]
    for i in range(4):
        results.append(done[i])
        results += list(done[4 + 3 * i : 7 + 3 * i])
    return tuple(results) + tuple(done[16:20])


def solution(mesh):
    tokens_spec = P(None, "batch", "band", None, None)
    slot_spec = P(("band", "batch"), None, None)
    return jax.shard_map(
        functools.partial(per_device, nb=mesh.shape["band"], nx=mesh.shape["batch"]),
        mesh=mesh,
        in_specs=(tokens_spec, tokens_spec, P()) + (slot_spec,) * 12 + (P(),) * 11,
        out_specs=(tokens_spec, tokens_spec)
        + (P(), slot_spec, slot_spec, slot_spec) * 4
        + (P(),) * 4,
        check_vma=False,
    )
```

```python
import functools

import jax
import jax.numpy as jnp
from jax import lax
from jax.experimental import pallas as pl
from jax.experimental.pallas import tpu as pltpu
from jax.sharding import PartitionSpec as P

HEAD_DIM = 32
STRIPE = 7
STEP = 10
EPS_NORM = 1e-05
BETA_ONE = 0.5
BETA_TWO = 0.6
RATE = 0.04
RATE_VECTORS = 0.2
DECAY = 0.01
EPS_ADAM = 1e-08
MESH = pl.DeviceIdType.MESH
F32 = jnp.float32
BF16 = jnp.bfloat16
PIECE = 64
LOG2E = 1.4426950408889634
LN2 = 0.6931471805599453
Q_SCALE = LOG2E * HEAD_DIM**-0.5
LONGEST = 1024
VMEM_LIMIT = 60 * 1024 * 1024
ROW_QKV, ROW_PROJ, ROW_FC1, ROW_FC2, ROW_END = 0, 768, 1024, 2048, 3072


def mm(a, b):
    return lax.dot_general(a, b, (((1,), (0,)), ((), ())), preferred_element_type=F32)


def mm_nt(a, b):
    return lax.dot_general(a, b, (((1,), (1,)), ((), ())), preferred_element_type=F32)


def mm_tn(a, b):
    return lax.dot_general(a, b, (((0,), (0,)), ((), ())), preferred_element_type=F32)


def exchange_kernel(n, piece, x_ref, o_ref, send_sem, recv_sem, loc_sem):
    me = lax.axis_index("band")
    bar = pltpu.get_barrier_semaphore()

    def greet(k, c):
        pl.semaphore_signal(
            bar, inc=1, device_id={"band": lax.rem(me + k, n)}, device_id_type=MESH
        )
        return c

    lax.fori_loop(1, n, greet, 0)
    pl.semaphore_wait(bar, n - 1)

    def rows(i):
        return pl.ds(pl.multiple_of(i * piece, piece), piece)

    def send(k, c):
        d = lax.rem(me + k, n)
        pltpu.make_async_remote_copy(
            src_ref=x_ref.at[rows(d)],
            dst_ref=o_ref.at[rows(me)],
            send_sem=send_sem.at[k],
            recv_sem=recv_sem.at[k],
            device_id={"band": d},
            device_id_type=MESH,
        ).start()
        return c

    lax.fori_loop(1, n, send, 0)
    local = pltpu.make_async_copy(x_ref.at[rows(me)], o_ref.at[rows(me)], loc_sem)
    local.start()
    local.wait()

    def take(k, c):
        s = lax.rem(me - k + n, n)
        pltpu.make_async_remote_copy(
            src_ref=x_ref.at[rows(s)],
            dst_ref=o_ref.at[rows(s)],
            send_sem=send_sem.at[k],
            recv_sem=recv_sem.at[k],
            device_id={"band": s},
            device_id_type=MESH,
        ).wait()
        return c

    lax.fori_loop(1, n, take, 0)


def exchange(x, n, cid):
    return pl.pallas_call(
        functools.partial(exchange_kernel, n, x.shape[0] // n),
        out_shape=jax.ShapeDtypeStruct(x.shape, x.dtype),
        in_specs=[pl.BlockSpec(memory_space=pltpu.VMEM)],
        out_specs=pl.BlockSpec(memory_space=pltpu.VMEM),
        scratch_shapes=[
            pltpu.SemaphoreType.DMA((n,)),
            pltpu.SemaphoreType.DMA((n,)),
            pltpu.SemaphoreType.DMA,
        ],
        compiler_params=pltpu.CompilerParams(
            collective_id=cid, has_side_effects=True, vmem_limit_bytes=VMEM_LIMIT
        ),
        name="exchange",
    )(x)


def sum_kernel(nb, nx, total_rows, x_ref, o_ref, got, half, recv, s1, r1, s2, r2, s3, r3, s4, r4):
    nq = (nb // 2) * nx
    p = total_rows // (2 * nq)
    band = lax.axis_index("band")
    core = lax.rem(band, 2)
    q = (band // 2) * nx + lax.axis_index("batch")
    sibling = {"band": band + 1 - 2 * core}
    bar = pltpu.get_barrier_semaphore()

    def chip(t):
        return {"band": (t // nx) * 2 + core, "batch": lax.rem(t, nx)}

    def ahead(k):
        return lax.rem(q + k, nq)

    def behind(k):
        return lax.rem(q - k + nq, nq)

    def copy(src, dst, ss, rs, dev):
        return pltpu.make_async_remote_copy(
            src_ref=src, dst_ref=dst, send_sem=ss, recv_sem=rs, device_id=dev, device_id_type=MESH
        )

    def loop(lo, hi, body):
        def step(k, c):
            body(k)
            return c

        lax.fori_loop(lo, hi, step, 0)

    pl.semaphore_signal(bar, inc=1, device_id=sibling, device_id_type=MESH)
    loop(
        1,
        nq,
        lambda k: pl.semaphore_signal(
            bar, inc=1, device_id=chip(ahead(k)), device_id_type=MESH
        ),
    )
    pl.semaphore_wait(bar, nq)

    def whole_rows(c, t):
        return pl.ds(pl.multiple_of((c * nq + t) * p, 16), p)

    def half_rows(t):
        return pl.ds(pl.multiple_of(t * p, 16), p)

    def pair_copy(k, side):
        t = ahead(k)
        return copy(
            x_ref.at[whole_rows(side, t)], got.at[half_rows(t)], s1.at[t], r1.at[t], sibling
        )

    loop(1, nq + 1, lambda k: pair_copy(k, 1 - core).start())

    def scatter_copy(k):
        t = ahead(k)
        return copy(half.at[half_rows(t)], recv.at[half_rows(q)], s2.at[k], r2.at[k], chip(t))

    def pair_sum(k):
        t = ahead(k)
        pair_copy(k, core).wait()
        half[half_rows(t)] = (
            x_ref[whole_rows(core, t)].astype(F32) + got[half_rows(t)].astype(F32)
        ).astype(BF16)

        @pl.when(k < nq)
        def _():
            scatter_copy(k).start()

    loop(1, nq + 1, pair_sum)

    def add_piece(k, acc):
        t = behind(k)
        copy(half.at[half_rows(t)], recv.at[half_rows(t)], s2.at[k], r2.at[k], chip(t)).wait()
        return acc + recv[half_rows(t)].astype(F32)

    total = lax.fori_loop(1, nq, add_piece, half[half_rows(q)].astype(F32))
    mine = o_ref.at[whole_rows(core, q)]
    o_ref[whole_rows(core, q)] = total.astype(BF16)

    def gather_copy(k):
        return copy(mine, mine, s3.at[k], r3.at[k], chip(ahead(k)))

    def pass_on(t, side):
        return copy(
            o_ref.at[whole_rows(core, t)],
            o_ref.at[whole_rows(side, t)],
            s4.at[t],
            r4.at[t],
            sibling,
        )

    loop(1, nq, lambda k: gather_copy(k).start())
    pass_on(q, core).start()

    def relay(k):
        t = behind(k)
        copy(mine, o_ref.at[whole_rows(core, t)], s3.at[k], r3.at[k], chip(t)).wait()
        pass_on(t, core).start()

    loop(1, nq, relay)
    loop(0, nq, lambda t: pass_on(t, 1 - core).wait())


def sum_everywhere(x, nb, nx, cid):
    rows, cols = x.shape
    nq = nb // 2 * nx
    unit = 32 * nq
    padded = -(-rows // unit) * unit
    if padded != rows:
        x = jnp.concatenate([x, jnp.zeros((padded - rows, cols), x.dtype)], axis=0)
    sems = [pltpu.SemaphoreType.DMA((nq,)) for _ in range(8)]
    out = pl.pallas_call(
        functools.partial(sum_kernel, nb, nx, padded),
        out_shape=jax.ShapeDtypeStruct(x.shape, x.dtype),
        in_specs=[pl.BlockSpec(memory_space=pltpu.VMEM)],
        out_specs=pl.BlockSpec(memory_space=pltpu.VMEM),
        scratch_shapes=[pltpu.VMEM((padded // 2, cols), x.dtype)] * 3 + sems,
        compiler_params=pltpu.CompilerParams(
            collective_id=cid, has_side_effects=True, vmem_limit_bytes=VMEM_LIMIT
        ),
        name="sum_everywhere",
    )(x)
    return out


def order_out(pieces_n, length):
    row = lax.broadcasted_iota(jnp.int32, (pieces_n * PIECE, 1), 0)
    s = row // PIECE
    m = row % PIECE
    a = (m * 37) // 256
    b = m - STRIPE * a
    token = jnp.where(m < STRIPE * STRIPE, a * length + STRIPE * s + b, -1)
    column = lax.broadcasted_iota(jnp.int32, (pieces_n * PIECE, STRIPE * length), 1)
    return jnp.where(column == token, 1.0, 0.0).astype(BF16)


def order_in(pieces_n, length):
    row = lax.broadcasted_iota(jnp.int32, (1, pieces_n * PIECE), 1)
    s = row // PIECE
    m = row % PIECE
    a = (m * 37) // 256
    b = m - STRIPE * a
    token = jnp.where(m < STRIPE * STRIPE, b * length + STRIPE * s + a, -1)
    column = lax.broadcasted_iota(jnp.int32, (STRIPE * length, pieces_n * PIECE), 0)
    return jnp.where(column == token, 1.0, 0.0).astype(BF16)


def unit_rows(values):
    centred = values - jnp.mean(values, axis=-1, keepdims=True)
    inverse = lax.rsqrt(jnp.mean(centred * centred, axis=-1, keepdims=True) + EPS_NORM)
    return centred * inverse, inverse


def norm_back(grad_normed, gain, unit, inverse):
    scaled = grad_normed * gain
    first_mean = jnp.mean(scaled, axis=-1, keepdims=True)
    second_mean = jnp.mean(scaled * unit, axis=-1, keepdims=True)
    return inverse * (scaled - first_mean - unit * second_mean)


def shifted_columns(v, length):
    tokens = v.shape[0]
    column = lax.broadcasted_iota(jnp.int32, v.shape, 0) % length
    before = jnp.where(column == 0, 0.0, pltpu.roll(v, 1, 0))
    after = jnp.where(column == length - 1, 0.0, pltpu.roll(v, tokens - 1, 0))
    return before, v, after


def shifted_rows(v, length):
    zeros = jnp.zeros((length, v.shape[1]), v.dtype)
    above = jnp.concatenate([zeros, v[: v.shape[0] - length]], axis=0)
    below = jnp.concatenate([v[length:], zeros], axis=0)
    return above, v, below


def half_rows(vec_ref, half):
    def get(i):
        if 2 <= i < 11:
            a, b = divmod(i - 2, 3)
            row = 12 + (3 * a + b if half == 0 else 3 * b + a)
        else:
            row = {0: 2, 1: 3, 11: 21}[i]
        return vec_ref[row : row + 1, 128 * half : 128 * half + 128]

    return get


def conv(v, hv, length, flipped):
    total = jnp.zeros_like(v)
    for b, col in enumerate(shifted_columns(v, length)):
        for a, val in enumerate(shifted_rows(col, length)):
            total = total + val * hv(2 + (8 - 3 * a - b if flipped else 3 * a + b))
    return total


def head_mask(shape, h, offset=0):
    lane = lax.broadcasted_iota(jnp.int32, shape, len(shape) - 1) - offset
    return (lane >= h * HEAD_DIM) & (lane < (h + 1) * HEAD_DIM)


def three_parts(x):
    lane = lax.broadcasted_iota(jnp.int32, x.shape, len(x.shape) - 1) % HEAD_DIM
    hi = x.astype(BF16).astype(F32)
    mid = (x - hi).astype(BF16).astype(F32)
    low = x - hi - mid
    parts = jnp.where(lane == 0, hi, jnp.where(lane == 1, mid, jnp.where(lane == 2, low, 0.0)))
    return parts.astype(BF16)


def head_lanes(h, width):
    lane = lax.broadcasted_iota(jnp.int32, (1, width), 1) % 128
    keep = (lane >= h * HEAD_DIM) & (lane < (h + 1) * HEAD_DIM)
    return jnp.where(keep, 1.0, 0.0).astype(BF16)


def beside_parts(block):
    lane = lax.broadcasted_iota(jnp.int32, block.shape, 1) % HEAD_DIM
    return jnp.concatenate([block, jnp.where(lane < 3, 1.0, 0.0).astype(BF16)], axis=1)


def turned(block):
    return jnp.transpose(block.astype(F32)).astype(BF16)


def lane_blocks(w_ref, half):
    return lambda b: w_ref[256 * b : 256 * b + 256, 128 * half : 128 * half + 128]


def attention_forward(
    x, hv, length, wb, vec_ref, qa_ref, k_ref, v_ref, o_ref, att_ref, between=None
):
    tokens = x.shape[0]
    unit, _ = unit_rows(x)
    normed = (unit * vec_ref[0:1] + vec_ref[1:2]).astype(BF16)
    qa_ref[:, 0:128] = ((mm(normed, wb(0)) + hv(0)) * Q_SCALE).astype(BF16)
    k_ref[...] = mm(normed, wb(1)).astype(BF16)
    v = (mm(normed, wb(2)) + hv(1)).astype(BF16)
    v_ref[...] = v

    def heads(v_turned, weighted, totals, tops):
        v_turned[...] = turned(v)

        def head_scores(h):
            return mm_nt(k_ref[...] * head_lanes(h, 128), qa_ref[:, 0:128])

        following = head_scores(0)
        ones = jnp.ones((HEAD_DIM, tokens), BF16)
        for h in range(4):
            scores = following
            if h < 3:
                following = head_scores(h + 1)
            highest = jnp.max(scores, axis=0, keepdims=True)
            probs = jnp.exp2(scores - highest).astype(BF16)
            rows = slice(HEAD_DIM * h, HEAD_DIM * h + HEAD_DIM)
            both = mm(jnp.concatenate([v_turned[rows, :], ones], axis=0), probs)
            weighted[rows, :] = both[:HEAD_DIM]
            totals[rows, :] = both[HEAD_DIM:]
            tops[rows, :] = jnp.broadcast_to(highest, (HEAD_DIM, tokens))

        if between is not None:
            between()
        o_ref[...] = jnp.transpose(weighted[...] / totals[...])
        log_total = tops[...] + jnp.log2(totals[...])
        qa_ref[:, 128:256] = three_parts(-jnp.transpose(log_total))

    pl.run_scoped(heads, pltpu.VMEM((128, tokens), BF16), *[pltpu.VMEM((128, tokens), F32)] * 3)
    lepe = conv(v_ref[...].astype(F32), hv, length, False)
    att_ref[...] = (o_ref[...] + lepe + hv(11)).astype(BF16)


def attention_backward(
    x, hv, length, grad, wb, vec_ref, qa_ref, k_ref, v_ref, o_ref, da_ref, gw_ref, rows_ref,
    between=None,
):
    tokens = x.shape[0]
    grad_f = grad.astype(F32)
    product = grad_f * o_ref[...]
    inner = jnp.zeros_like(product)
    for h in range(4):
        keep = head_mask(product.shape, h)
        inner = jnp.where(
            keep, jnp.sum(jnp.where(keep, product, 0.0), axis=-1, keepdims=True), inner
        )
    da_ref[:, 0:128] = grad
    da_ref[:, 128:256] = three_parts(-inner)

    def heads(k_turned, q_turned, grad_turned, k_wide, v_wide, dqs, dks, dvs):
        k_turned[...] = turned(k_ref[...])
        q_turned[...] = turned(qa_ref[:, 0:128])
        grad_turned[...] = turned(grad)
        k_wide[...] = beside_parts(k_ref[...])
        v_wide[...] = beside_parts(v_ref[...])

        def head_products(h):
            mask = head_lanes(h, 256)
            return mm_nt(qa_ref[...] * mask, k_wide[...]), mm_nt(da_ref[...] * mask, v_wide[...])

        early = tokens <= LONGEST
        following = head_products(0) if early else None
        for h in range(4):
            scores, grad_probs = following if early else head_products(h)
            if early and h < 3:
                following = head_products(h + 1)
            probs = jnp.exp2(scores)
            grad_scores = (probs * grad_probs).astype(BF16)
            rows = slice(HEAD_DIM * h, HEAD_DIM * h + HEAD_DIM)
            dvs[rows, :] = mm(grad_turned[rows, :], probs.astype(BF16))
            dks[rows, :] = mm(q_turned[rows, :], grad_scores)
            dqs[rows, :] = mm_nt(k_turned[rows, :], grad_scores)

        if between is not None:
            between()
        dq = (jnp.transpose(dqs[...]) * HEAD_DIM**-0.5).astype(BF16)
        dk = (jnp.transpose(dks[...]) * LN2).astype(BF16)
        dv = (jnp.transpose(dvs[...]) + conv(grad_f, hv, length, True)).astype(BF16)
        unit, _ = unit_rows(x)
        normed = (unit * vec_ref[0:1] + vec_ref[1:2]).astype(BF16)
        gw_ref[...] += mm_tn(normed, jnp.concatenate([dq, dk, dv], axis=1))
        rows_ref[0:1, :] += jnp.sum(dq.astype(F32), axis=0, keepdims=True)
        rows_ref[1:2, :] += jnp.sum(dv.astype(F32), axis=0, keepdims=True)
        for b, col in enumerate(shifted_columns(v_ref[...].astype(F32), length)):
            for a, val in enumerate(shifted_rows(col, length)):
                row = 2 + 3 * a + b
                rows_ref[row : row + 1, :] += jnp.sum(grad_f * val, axis=0, keepdims=True)
        rows_ref[11:12, :] += jnp.sum(grad_f, axis=0, keepdims=True)
        part = mm_nt(dq, wb(0)) + mm_nt(dk, wb(1)) + mm_nt(dv, wb(2))
        gain_row = jnp.sum(part * unit, axis=0, keepdims=True)
        shift_row = jnp.sum(part, axis=0, keepdims=True)
        for i in range(2):
            rows_ref[12 + i : 13 + i, :] += gain_row[:, 128 * i : 128 * i + 128]
            rows_ref[14 + i : 15 + i, :] += shift_row[:, 128 * i : 128 * i + 128]
        return part

    return pl.run_scoped(
        heads,
        *[pltpu.VMEM((128, tokens), BF16)] * 3,
        *[pltpu.VMEM((tokens, 256), BF16)] * 2,
        *[pltpu.VMEM((128, tokens), F32)] * 3,
    )


def feed_forward(x, att, top, w_ref, base, vec_ref, n2_ref, acc_ref, gn_ref, gp_ref, g1_ref, g2_ref, rows_ref):
    middle = x + mm(att, w_ref[base : base + 256, :]) + vec_ref[4:5]
    unit, inverse = unit_rows(middle)
    n2_ref[...] = (unit * vec_ref[5:6] + vec_ref[6:7]).astype(BF16)
    acc_ref[...] = middle + vec_ref[11:12]
    gn_ref[...] = jnp.zeros_like(gn_ref)
    for f in range(4):
        w1 = w_ref[base + 256 * (1 + f) : base + 256 * (2 + f), :]
        w2 = w_ref[base + 256 * (5 + f) : base + 256 * (6 + f), :]
        cols = slice(256 * f, 256 * f + 256)
        hidden = mm(n2_ref[...], w1) + vec_ref[7 + f : 8 + f]
        below = 0.5 * (1.0 + lax.erf(hidden * (0.5**0.5)))
        active = (hidden * below).astype(BF16)
        slope = below + hidden * jnp.exp(-0.5 * hidden * hidden) * 0.3989422804014327
        grad_hidden = (mm_nt(top, w2) * slope).astype(BF16)
        acc_ref[...] += mm(active, w2)
        gn_ref[...] += mm_nt(grad_hidden, w1)
        g1_ref[:, cols] += mm_tn(n2_ref[...], grad_hidden)
        g2_ref[:, cols] += mm_tn(top, active)
        rows_ref[3 + f : 4 + f, :] += jnp.sum(grad_hidden.astype(F32), axis=0, keepdims=True)
    grad_normed = gn_ref[...]
    top_f = top.astype(F32)
    grad_middle = top_f + norm_back(grad_normed, vec_ref[5:6], unit, inverse)
    branch = grad_middle.astype(BF16)
    gp_ref[...] += mm_tn(branch, att)
    rows_ref[0:1, :] += jnp.sum(branch.astype(F32), axis=0, keepdims=True)
    rows_ref[1:2, :] += jnp.sum(grad_normed * unit, axis=0, keepdims=True)
    rows_ref[2:3, :] += jnp.sum(grad_normed, axis=0, keepdims=True)
    rows_ref[7:8, :] += jnp.sum(top_f, axis=0, keepdims=True)
    grad_att = mm_nt(branch, w_ref[base : base + 256, :]).astype(BF16)
    return acc_ref[...].astype(BF16), grad_middle, grad_att


PARAMS = pltpu.CompilerParams(
    dimension_semantics=("arbitrary",), vmem_limit_bytes=VMEM_LIMIT
)


def whole(shape):
    return pl.BlockSpec(shape, lambda m: (0,) * len(shape))


def each(shape):
    return pl.BlockSpec((None,) + shape, lambda m: (m,) + (0,) * len(shape))


def shape_of(dtype, *shape):
    return jax.ShapeDtypeStruct(shape, dtype)


def pack_tokens(x, nb, length):
    micro, tokens, channels = x.shape

    def kernel(x_ref, o_ref, hot):
        @pl.when(pl.program_id(0) == 0)
        def _():
            hot[...] = order_out(nb, length)

        o_ref[...] = mm(hot[...], x_ref[...]).astype(BF16)

    return pl.pallas_call(
        kernel,
        grid=(micro,),
        in_specs=[each((tokens, channels))],
        out_specs=each((nb * PIECE, channels)),
        out_shape=shape_of(BF16, micro, nb * PIECE, channels),
        scratch_shapes=[pltpu.VMEM((nb * PIECE, tokens), BF16)],
        compiler_params=PARAMS,
        name="pack_tokens",
    )(x)


def forward_call(x, half, nb, length, weights, vectors):
    micro = x.shape[0]
    tokens = STRIPE * length
    packed = nb * PIECE

    def kernel(x_ref, w_ref, vec_ref, qa_ref, k_ref, v_ref, o_ref, att_ref, xs_ref, *scr):
        if half == 0:
            attention_forward(
                x_ref[...].astype(F32), half_rows(vec_ref, half), length, lane_blocks(w_ref, half), vec_ref, qa_ref, k_ref, v_ref, o_ref, att_ref
            )
        else:
            att_s, hot_in, hot_out = scr

            @pl.when(pl.program_id(0) == 0)
            def _():
                hot_in[...] = order_in(nb, length)
                hot_out[...] = order_out(nb, length)

            xs_ref[...] = mm(hot_in[...], x_ref[...]).astype(BF16)
            attention_forward(
                xs_ref[...].astype(F32), half_rows(vec_ref, half), length, lane_blocks(w_ref, half), vec_ref, qa_ref, k_ref, v_ref, o_ref, att_s
            )
            att_ref[...] = mm(hot_out[...], att_s[...]).astype(BF16)

    rows = tokens if half == 0 else packed
    scratch = []
    if half == 1:
        scratch += [
            pltpu.VMEM((tokens, 128), BF16),
            pltpu.VMEM((tokens, packed), BF16),
            pltpu.VMEM((packed, tokens), BF16),
        ]
    if half == 0:
        def body(x_ref, w_ref, vec_ref, qa_ref, k_ref, v_ref, o_ref, att_ref, *scr):
            kernel(x_ref, w_ref, vec_ref, qa_ref, k_ref, v_ref, o_ref, att_ref, None, *scr)
        extra_specs, extra_shapes = [], []
    else:
        body = kernel
        extra_specs = [each((tokens, 256))]
        extra_shapes = [shape_of(BF16, micro, tokens, 256)]
    return pl.pallas_call(
        body,
        grid=(micro,),
        in_specs=[each((rows, 256)), whole(weights.shape), whole(vectors.shape)],
        out_specs=[
            each((tokens, 256)),
            each((tokens, 128)),
            each((tokens, 128)),
            each((tokens, 128)),
            each((rows, 128)),
        ] + extra_specs,
        out_shape=[
            shape_of(BF16, micro, tokens, 256),
            shape_of(BF16, micro, tokens, 128),
            shape_of(BF16, micro, tokens, 128),
            shape_of(F32, micro, tokens, 128),
            shape_of(BF16, micro, rows, 128),
        ] + extra_shapes,
        scratch_shapes=scratch,
        compiler_params=PARAMS,
        name="attention_forward_%d" % half,
    )(x, weights, vectors)


def middle_call(x, att_h, att_v, top, nb, length, weights, vectors):
    micro, tokens, _ = x.shape
    packed = nb * PIECE

    def kernel(
        x_ref, h_ref, v_ref, top_ref, w_ref, vec_ref,
        out_ref, gm_ref, gh_ref, gv_ref, gp_ref, g1_ref, g2_ref, rows_ref,
        hot_in, hot_out, att, n2, acc, gn,
    ):
        @pl.when(pl.program_id(0) == 0)
        def _():
            hot_in[...] = order_in(nb, length)
            hot_out[...] = order_out(nb, length)
            for ref in (gp_ref, g1_ref, g2_ref, rows_ref):
                ref[...] = jnp.zeros_like(ref)

        att[:, 0:128] = h_ref[...]
        att[:, 128:256] = mm(hot_in[...], v_ref[...]).astype(BF16)
        out, grad_middle, grad_att = feed_forward(
            x_ref[...].astype(F32), att[...], top_ref[...], w_ref, ROW_PROJ, vec_ref, n2, acc, gn, gp_ref, g1_ref, g2_ref, rows_ref
        )
        out_ref[...] = out
        gm_ref[...] = grad_middle
        gh_ref[...] = grad_att[:, 0:128]
        gv_ref[...] = mm(hot_out[...], grad_att[:, 128:256]).astype(BF16)

    return pl.pallas_call(
        kernel,
        grid=(micro,),
        in_specs=[
            each((tokens, 256)), each((tokens, 128)), each((packed, 128)), each((tokens, 256)),
            whole(weights.shape), whole(vectors.shape),
        ],
        out_specs=[
            each((tokens, 256)), each((tokens, 256)), each((tokens, 128)), each((packed, 128)),
            whole((256, 256)), whole((256, 1024)), whole((256, 1024)), whole((8, 256)),
        ],
        out_shape=[
            shape_of(BF16, micro, tokens, 256), shape_of(F32, micro, tokens, 256),
            shape_of(BF16, micro, tokens, 128), shape_of(BF16, micro, packed, 128),
            shape_of(F32, 256, 256), shape_of(F32, 256, 1024), shape_of(F32, 256, 1024), shape_of(F32, 8, 256),
        ],
        scratch_shapes=[
            pltpu.VMEM((tokens, packed), BF16), pltpu.VMEM((packed, tokens), BF16),
            pltpu.VMEM((tokens, 256), BF16), pltpu.VMEM((tokens, 256), BF16),
            pltpu.VMEM((tokens, 256), F32), pltpu.VMEM((tokens, 256), F32),
        ],
        compiler_params=PARAMS,
        name="feed_forward",
    )(x, att_h, att_v, top, weights, vectors)


def backward_call(x, grad, qa, k, v, o, half, nb, length, weights, vectors):
    micro, tokens, _ = x.shape
    packed = nb * PIECE

    def kernel(
        x_ref, g_ref, qa_ref, k_ref, v_ref, o_ref, w_ref, vec_ref, gn_ref, gw_ref, rows_ref,
        da, *scr,
    ):
        @pl.when(pl.program_id(0) == 0)
        def _():
            gw_ref[...] = jnp.zeros_like(gw_ref)
            rows_ref[...] = jnp.zeros_like(rows_ref)
            if half == 1:
                scr[0][...] = order_in(nb, length)
                scr[1][...] = order_out(nb, length)

        grad_in = g_ref[...] if half == 0 else mm(scr[0][...], g_ref[...]).astype(BF16)
        part = attention_backward(
            x_ref[...].astype(F32), half_rows(vec_ref, half), length, grad_in, lane_blocks(w_ref, half), vec_ref, qa_ref, k_ref, v_ref, o_ref,
            da, gw_ref, rows_ref,
        )
        if half == 0:
            gn_ref[...] = part
        else:
            gn_ref[...] = mm(scr[1][...], part.astype(BF16)).astype(BF16)

    rows = tokens if half == 0 else packed
    scratch = [pltpu.VMEM((tokens, 256), BF16)]
    if half == 1:
        scratch += [pltpu.VMEM((tokens, packed), BF16), pltpu.VMEM((packed, tokens), BF16)]
    return pl.pallas_call(
        kernel,
        grid=(micro,),
        in_specs=[
            each((tokens, 256)), each((rows, 128)), each((tokens, 256)), each((tokens, 128)),
            each((tokens, 128)), each((tokens, 128)), whole(weights.shape), whole(vectors.shape),
        ],
        out_specs=[each((rows, 256)), whole((256, 384)), whole((16, 128))],
        out_shape=[
            shape_of(F32 if half == 0 else BF16, micro, rows, 256),
            shape_of(F32, 256, 384), shape_of(F32, 16, 128),
        ],
        scratch_shapes=scratch,
        compiler_params=PARAMS,
        name="attention_backward_%d" % half,
    )(x, grad, qa, k, v, o, weights, vectors)


def last_call(x, grad_middle, part_h, part_v, nb, length, vectors):
    micro, tokens, _ = x.shape
    packed = nb * PIECE

    def kernel(x_ref, gm_ref, h_ref, v_ref, vec_ref, out_ref, hot_in):
        @pl.when(pl.program_id(0) == 0)
        def _():
            hot_in[...] = order_in(nb, length)

        grad_normed = h_ref[...] + mm(hot_in[...], v_ref[...])
        unit, inverse = unit_rows(x_ref[...].astype(F32))
        out_ref[...] = (
            gm_ref[...] + norm_back(grad_normed, vec_ref[0:1], unit, inverse)
        ).astype(BF16)

    return pl.pallas_call(
        kernel,
        grid=(micro,),
        in_specs=[
            each((tokens, 256)), each((tokens, 256)), each((tokens, 256)), each((packed, 256)), whole(vectors.shape),
        ],
        out_specs=each((tokens, 256)),
        out_shape=shape_of(BF16, micro, tokens, 256),
        scratch_shapes=[pltpu.VMEM((tokens, packed), BF16)],
        compiler_params=PARAMS,
        name="input_gradient",
    )(x, grad_middle, part_h, part_v, vectors)


def repeat(lo, hi, body):
    def step(k, c):
        body(k)
        return c

    lax.fori_loop(lo, hi, step, 0)


def remote(src, dst, ss, rs, dev):
    return pltpu.make_async_remote_copy(
        src_ref=src, dst_ref=dst, send_sem=ss, recv_sem=rs, device_id=dev, device_id_type=MESH
    )


def await_bytes(ref, sem):
    pltpu.make_async_copy(ref, ref, sem).wait()


class Swap:
    def __init__(self, n, out_ref, in_ref, send_sem, recv_sem):
        self.n, self.out, self.into, self.ss, self.rs = n, out_ref, in_ref, send_sem, recv_sem
        self.me = lax.axis_index("band")

    def rows(self, i):
        return pl.ds(pl.multiple_of(i * PIECE, PIECE), PIECE)

    def send(self, m):
        mine = self.rows(self.me)

        def one(k):
            d = lax.rem(self.me + k, self.n)
            remote(
                self.out.at[m, self.rows(d)],
                self.into.at[m, mine],
                self.ss.at[m],
                self.rs.at[m],
                {"band": d},
            ).start()

        repeat(1, self.n, one)
        self.into[m, mine, :] = self.out[m, mine, :]

    def wait(self, m):
        others = pl.ds(0, (self.n - 1) * PIECE)
        await_bytes(self.out.at[m, others], self.ss.at[m])
        await_bytes(self.into.at[m, others], self.rs.at[m])


class Sum:
    def __init__(self, nb, nx, x_ref, o_ref, got, half, recv, sems):
        self.nx = nx
        self.nq = (nb // 2) * nx
        self.p = x_ref.shape[0] // (2 * self.nq)
        band = lax.axis_index("band")
        self.core = lax.rem(band, 2)
        self.q = (band // 2) * nx + lax.axis_index("batch")
        self.sibling = {"band": band + 1 - 2 * self.core}
        self.x, self.o, self.got, self.half, self.recv = x_ref, o_ref, got, half, recv
        self.sems = sems

    def chip(self, t):
        return {"band": (t // self.nx) * 2 + self.core, "batch": lax.rem(t, self.nx)}

    def ahead(self, k):
        return lax.rem(self.q + k, self.nq)

    def behind(self, k):
        return lax.rem(self.q - k + self.nq, self.nq)

    def side(self, c):
        rows = self.nq * self.p
        return pl.ds(pl.multiple_of(c * rows, 16), rows)

    def wide(self, c, t):
        return pl.ds(pl.multiple_of((c * self.nq + t) * self.p, 16), self.p)

    def thin(self, t):
        return pl.ds(pl.multiple_of(t * self.p, 16), self.p)

    def sem(self, i):
        return self.sems.at[2 * i], self.sems.at[2 * i + 1]

    def arrived(self, i, sent, came):
        await_bytes(sent, self.sems.at[2 * i])
        await_bytes(came, self.sems.at[2 * i + 1])

    def pair_copy(self, c):
        return remote(self.x.at[self.side(c)], self.got, *self.sem(0), self.sibling)

    def start(self):
        self.pair_copy(1 - self.core).start()

    def scatter(self):
        self.pair_copy(self.core).wait()
        self.half[...] = (
            self.x[self.side(self.core)].astype(F32) + self.got[...].astype(F32)
        ).astype(BF16)

        def one(k):
            t = self.ahead(k)
            remote(
                self.half.at[self.thin(t)],
                self.recv.at[self.thin(self.q)],
                *self.sem(1),
                self.chip(t),
            ).start()

        repeat(1, self.nq, one)
        self.recv[self.thin(self.q)] = self.half[self.thin(self.q)]

    def gather(self):
        others = pl.ds(0, (self.nq - 1) * self.p)
        self.arrived(1, self.half.at[others], self.recv.at[others])
        total = self.recv[0 : self.p].astype(F32)
        for t in range(1, self.nq):
            total = total + self.recv[t * self.p : (t + 1) * self.p].astype(F32)
        mine = self.wide(self.core, self.q)
        self.o[mine] = total.astype(BF16)

        def give(k):
            remote(
                self.o.at[mine], self.o.at[mine], *self.sem(2), self.chip(self.ahead(k))
            ).start()

        repeat(1, self.nq, give)

    def pass_on(self, c):
        return remote(
            self.o.at[self.side(self.core)], self.o.at[self.side(c)], *self.sem(3), self.sibling
        )

    def relay(self):
        others = pl.ds(0, (self.nq - 1) * self.p)
        self.arrived(2, self.o.at[others], self.o.at[others])
        self.pass_on(self.core).start()

    def finish(self):
        self.pass_on(1 - self.core).wait()


class DeepSum:
    def __init__(self, nb, nx, x_ref, o_ref, got, half, recv, deep, deep_recv, sems):
        self.nx = nx
        self.n1, self.n2 = 2 * nx, nb // 4
        self.p = x_ref.shape[0] // (2 * self.n1 * self.n2)
        band = lax.axis_index("band")
        self.core = lax.rem(band, 2)
        self.j1 = lax.rem(band // 2, 2) * nx + lax.axis_index("batch")
        self.j2 = band // 4
        self.sibling = {"band": band + 1 - 2 * self.core}
        self.x, self.o, self.got, self.half, self.recv = x_ref, o_ref, got, half, recv
        self.deep, self.deep_recv = deep, deep_recv
        self.sems = sems

    def near(self, t):
        return {
            "band": self.j2 * 4 + (t // self.nx) * 2 + self.core,
            "batch": lax.rem(t, self.nx),
        }

    def far(self, t):
        return {"band": t * 4 + lax.rem(lax.axis_index("band"), 4)}

    def near_at(self, k):
        return lax.rem(self.j1 + k, self.n1)

    def far_at(self, k):
        return lax.rem(self.j2 + k, self.n2)

    def block(self, c, t):
        rows = self.n2 * self.p
        return pl.ds(pl.multiple_of((c * self.n1 + t) * rows, 16), rows)

    def thin(self, t):
        rows = self.n2 * self.p
        return pl.ds(pl.multiple_of(t * rows, 16), rows)

    def piece(self, t):
        return pl.ds(pl.multiple_of(t * self.p, 16), self.p)

    def o_piece(self, t):
        at = (self.core * self.n1 + self.j1) * self.n2 + t
        return self.o.at[pl.ds(pl.multiple_of(at * self.p, 16), self.p)]

    def sem(self, i):
        return self.sems.at[2 * i], self.sems.at[2 * i + 1]

    def arrived(self, i, sent, came):
        await_bytes(sent, self.sems.at[2 * i])
        await_bytes(came, self.sems.at[2 * i + 1])

    def side(self, c):
        rows = self.n1 * self.n2 * self.p
        return pl.ds(pl.multiple_of(c * rows, 16), rows)

    def pair_copy(self, c):
        return remote(self.x.at[self.side(c)], self.got, *self.sem(0), self.sibling)

    def start(self):
        self.pair_copy(1 - self.core).start()

    def scatter(self):
        self.pair_copy(self.core).wait()
        self.half[...] = (
            self.x[self.side(self.core)].astype(F32) + self.got[...].astype(F32)
        ).astype(BF16)

        def one(k):
            t = self.near_at(k)
            remote(
                self.half.at[self.thin(t)],
                self.recv.at[self.thin(self.j1)],
                *self.sem(1),
                self.near(t),
            ).start()

        repeat(1, self.n1, one)

    def scatter_far(self):
        others = pl.ds(0, (self.n1 - 1) * self.n2 * self.p)
        self.arrived(1, self.half.at[others], self.recv.at[others])
        total = self.half[self.thin(self.j1)].astype(F32)
        for k in range(1, self.n1):
            total = total + self.recv[self.thin(self.near_at(k))].astype(F32)
        self.deep[...] = total.astype(BF16)

        def give(k):
            t = self.far_at(k)
            remote(
                self.deep.at[self.piece(t)],
                self.deep_recv.at[self.piece(self.j2)],
                *self.sem(2),
                self.far(t),
            ).start()

        repeat(1, self.n2, give)

    def gather(self):
        others = pl.ds(0, (self.n2 - 1) * self.p)
        self.arrived(2, self.deep.at[others], self.deep_recv.at[others])
        total = self.deep[self.piece(self.j2)].astype(F32)
        for k in range(1, self.n2):
            total = total + self.deep_recv[self.piece(self.far_at(k))].astype(F32)
        at = (self.core * self.n1 + self.j1) * self.n2 + self.j2
        self.o[pl.ds(pl.multiple_of(at * self.p, 16), self.p)] = total.astype(BF16)
        mine = self.o_piece(self.j2)
        repeat(
            1,
            self.n2,
            lambda k: remote(mine, mine, *self.sem(3), self.far(self.far_at(k))).start(),
        )

    def gather_near(self):
        others = pl.ds(0, (self.n2 - 1) * self.p)
        self.arrived(3, self.o.at[others], self.o.at[others])
        mine = self.o.at[self.block(self.core, self.j1)]
        repeat(
            1,
            self.n1,
            lambda k: remote(mine, mine, *self.sem(4), self.near(self.near_at(k))).start(),
        )

    def pass_on(self, c):
        return remote(
            self.o.at[self.side(self.core)], self.o.at[self.side(c)], *self.sem(5), self.sibling
        )

    def relay(self):
        others = pl.ds(0, (self.n1 - 1) * self.n2 * self.p)
        self.arrived(4, self.o.at[others], self.o.at[others])
        self.pass_on(self.core).start()

    def finish(self):
        self.pass_on(1 - self.core).wait()


ROWS_A = 1536
ROWS_B = 2304
ROWS_G = 800


def up(rows, unit):
    return -(-rows // unit) * unit


def split_rows(ref, at, rows):
    n = rows.shape[0]
    high = rows.astype(BF16)
    ref[at : at + n, :] = high
    ref[at + n : at + 2 * n, :] = (rows - high.astype(F32)).astype(BF16)


def block_kernel(
    nb, nx, length,
    own_ref, x_ref, wq_ref, vec_ref, top_hbm, wp_hbm, w1_hbm, w2_hbm,
    out_ref, ing_ref, gb_ref, gav_ref, gah_ref,
    wa_in, wb_in, wa, wb, gb_in, gav_in, gah_in,
    wide_got, wide_half, wide_recv, wide_deep, wide_deep_recv,
    a_got, a_half, a_recv, a_deep, a_deep_recv,
    gb_got, gb_half, gb_recv, gb_deep, gb_deep_recv,
    v_got, v_half, v_recv, v_deep, v_deep_recv, h_got, h_half, h_recv,
    hot_in, hot_out, x_out, x_in, a_out, a_in, g_in, p_in,
    xs, qa, ks, vs, os, att_w, att, n2, acc, gn, gm, grad_w, part_w, hv_ref,
    gp, g1, g2, rows_mid, gw, rows, da,
    x_ss, x_rs, a_ss, a_rs, g_ss, g_rs, p_ss, p_rs,
    wa_sem, wb_sem, gb_sem, gav_sem, gah_sem,
    top_ref, wp_ref, w1_ref, w2_ref, fetch_sem,
):
    fetches = [
        pltpu.make_async_copy(src, dst, fetch_sem.at[i])
        for i, (src, dst) in enumerate(
            ((wp_hbm, wp_ref), (w1_hbm, w1_ref), (w2_hbm, w2_ref), (top_hbm, top_ref))
        )
    ]
    for c in fetches:
        c.start()
    band = lax.axis_index("band")
    batch = lax.axis_index("batch")
    device = band * nx + batch
    micro = x_ref.shape[0]
    core = lax.rem(band, 2)
    bar = pltpu.get_barrier_semaphore()
    repeat(
        1,
        nb,
        lambda k: pl.semaphore_signal(
            bar, inc=1, device_id={"band": lax.rem(band + k, nb)}, device_id_type=MESH
        ),
    )

    def greet(t):
        other = lax.rem(batch + 1 + t // (nb // 2), nx)
        pl.semaphore_signal(
            bar,
            inc=1,
            device_id={"band": lax.rem(t, nb // 2) * 2 + core, "batch": other},
            device_id_type=MESH,
        )

    repeat(0, (nb // 2) * (nx - 1), greet)

    sum_wa = DeepSum(
        nb, nx, wa_in, wa, a_got, a_half, a_recv, a_deep, a_deep_recv, wa_sem
    )
    sum_wb = DeepSum(
        nb, nx, wb_in, wb, wide_got, wide_half, wide_recv, wide_deep, wide_deep_recv, wb_sem
    )
    sum_gb = DeepSum(
        nb, nx, gb_in, gb_ref, gb_got, gb_half, gb_recv, gb_deep, gb_deep_recv, gb_sem
    )
    sum_gav = DeepSum(
        nb, nx, gav_in, gav_ref, v_got, v_half, v_recv, v_deep, v_deep_recv, gav_sem
    )
    sum_gah = Sum(nb, nx, gah_in, gah_ref, h_got, h_half, h_recv, gah_sem)
    swap_x = Swap(nb, x_out, x_in, x_ss, x_rs)
    swap_a = Swap(nb, a_out, a_in, a_ss, a_rs)
    swap_g = Swap(nb, a_out, g_in, g_ss, g_rs)
    swap_p = Swap(nb, x_out, p_in, p_ss, p_rs)

    def own(ref, which, cols):
        return jnp.where(own_ref[which] == device, ref[0, :, cols], 0.0).astype(BF16)

    for b in range(6):
        wa_in[256 * b : 256 * b + 256, :] = own(wq_ref, 0, slice(128 * b, 128 * b + 128))
    if wa_in.shape[0] > ROWS_A:
        wa_in[ROWS_A:, :] = jnp.zeros((wa_in.shape[0] - ROWS_A, 128), BF16)
    pl.semaphore_wait(bar, nb - 1 + (nb // 2) * (nx - 1))
    sum_wa.start()
    sum_wa.scatter()
    for c in fetches[:3]:
        c.wait()
    wb_in[0:256, :] = own(wp_ref, 1, slice(0, 256))
    for f in range(4):
        wb_in[256 * (f + 1) : 256 * (f + 2), :] = own(w1_ref, 2, slice(256 * f, 256 * f + 256))
    wb_in[1280:ROWS_B, :] = own(w2_ref, 3, slice(0, 256))
    wb_in[ROWS_B:, :] = jnp.zeros((wb_in.shape[0] - ROWS_B, 256), BF16)
    sum_wb.start()
    hot_out[...] = order_out(nb, length)
    x_out[0] = mm(hot_out[...], x_ref[0]).astype(BF16)
    sum_wa.scatter_far()
    swap_x.send(0)
    sum_wb.scatter()
    sum_wa.gather()
    hot_in[...] = order_in(nb, length)
    for m in range(1, micro):
        x_out[m] = mm(hot_out[...], x_ref[m]).astype(BF16)
    sum_wa.gather_near()
    for m in range(1, micro):
        swap_x.send(m)
    sum_wa.relay()
    for ref in (gp, g1, g2, rows_mid, gw, rows):
        ref[...] = jnp.zeros_like(ref)
    for half in range(2):
        get = half_rows(vec_ref, half)
        for i in range(12):
            hv_ref[half, i : i + 1, :] = get(i)
    for m in range(micro):
        xs[m] = x_ref[m]
    sum_wa.finish()

    def blocks(half):
        return lambda b: wa[pl.ds(pl.multiple_of(256 * (2 * b + half), 256), 256), :]

    def vectors_of(half):
        return lambda i: hv_ref[half, i : i + 1, :]

    def forward_step(w):
        half, m = w // micro, lax.rem(w, micro)

        @pl.when(w >= micro)
        def _():
            swap_x.wait(m)
            xs[w] = mm(hot_in[...], x_in[m]).astype(BF16)

        def between():
            pl.when(w == 0)(sum_wb.scatter_far)
            pl.when(w == micro - 1)(sum_wb.gather)
            pl.when(w == micro)(sum_wb.gather_near)
            pl.when(w == 2 * micro - 1)(sum_wb.relay)

        attention_forward(
            xs[w].astype(F32), vectors_of(half), length, blocks(half), vec_ref,
            qa.at[w], ks.at[w], vs.at[w], os.at[w], att_w.at[w], between,
        )

        @pl.when(w >= micro)
        def _():
            a_out[m] = mm(hot_out[...], att_w[w]).astype(BF16)
            swap_a.send(m)

    repeat(0, 2 * micro, forward_step)
    sum_wb.finish()
    fetches[3].wait()

    def middle_step(m):
        swap_a.wait(m)
        att[:, 0:128] = att_w[m]
        att[:, 128:256] = mm(hot_in[...], a_in[m]).astype(BF16)
        out, grad_middle, grad_att = feed_forward(
            x_ref[m].astype(F32), att[...], top_ref[m], wb, 0, vec_ref, n2, acc, gn,
            gp, g1, g2, rows_mid,
        )
        out_ref[m] = out
        gm[m] = grad_middle
        grad_w[m] = grad_att[:, 0:128]
        a_out[m] = mm(hot_out[...], grad_att[:, 128:256]).astype(BF16)
        swap_g.send(m)

    repeat(0, micro, middle_step)
    gb_in[0:256, :] = jnp.transpose(gp[...]).astype(BF16)
    for f in range(4):
        cols = slice(256 * f, 256 * f + 256)
        gb_in[256 * (f + 1) : 256 * (f + 2), :] = g1[:, cols].astype(BF16)
        gb_in[1280 + 256 * f : 1536 + 256 * f, :] = jnp.transpose(g2[:, cols]).astype(BF16)
    gb_in[ROWS_B:, :] = jnp.zeros((gb_in.shape[0] - ROWS_B, 256), BF16)
    split_rows(gb_in, ROWS_B, rows_mid[...])
    sum_gb.start()

    def fill(ref, half):
        for b in range(3):
            ref[256 * b : 256 * b + 256, :] = gw[half, :, 128 * b : 128 * b + 128].astype(BF16)
        split_rows(ref, 768, rows[half])
        ref[ROWS_G:, :] = jnp.zeros((ref.shape[0] - ROWS_G, 128), BF16)

    def backward_step(i):
        w = lax.rem(i + micro, 2 * micro)
        half, m = w // micro, lax.rem(w, micro)

        @pl.when(w >= micro)
        def _():
            swap_g.wait(m)
            grad_w[w] = mm(hot_in[...], g_in[m]).astype(BF16)

        def between():
            pl.when(i == 0)(sum_gb.scatter)
            pl.when(i == micro - 1)(sum_gb.scatter_far)

            @pl.when(i == micro)
            def _():
                sum_gb.gather()
                sum_gav.scatter()

            @pl.when(i == 2 * micro - 1)
            def _():
                sum_gb.gather_near()
                sum_gav.gather()

        into = jnp.where(w >= micro, micro, m)
        part_w[into] = attention_backward(
            xs[w].astype(F32), vectors_of(half), length, grad_w[w], blocks(half), vec_ref,
            qa.at[w], ks.at[w], vs.at[w], os.at[w], da, gw.at[half], rows.at[half],
            between,
        )

        @pl.when(w >= micro)
        def _():
            x_out[m] = mm(hot_out[...], part_w[micro].astype(BF16)).astype(BF16)
            swap_p.send(m)

        @pl.when(i == micro - 1)
        def _():
            fill(gav_in, 1)
            sum_gav.start()

        pl.when(i == micro)(sum_gav.scatter_far)

    repeat(0, 2 * micro, backward_step)
    fill(gah_in, 0)
    sum_gah.start()
    sum_gav.gather_near()
    sum_gah.scatter()
    sum_gb.relay()

    def last_step(m):
        swap_p.wait(m)
        grad_normed = part_w[m] + mm(hot_in[...], p_in[m])
        unit, inverse = unit_rows(x_ref[m].astype(F32))
        ing_ref[m] = (gm[m] + norm_back(grad_normed, vec_ref[0:1], unit, inverse)).astype(BF16)

    last_step(0)
    sum_gah.gather()
    sum_gav.relay()
    repeat(1, micro, last_step)
    sum_gah.relay()
    sum_gb.finish()
    sum_gav.finish()
    sum_gah.finish()


def block_call(x, top, owners, w_qkv, w_proj, w_fc1, w_fc2, vectors, nb, nx, length):
    micro, tokens, _ = x.shape
    packed = nb * PIECE
    nq = nb // 2 * nx
    unit = 32 * nq
    ra, rb, rg = up(ROWS_A, unit), up(ROWS_B + 16, unit), up(ROWS_G, unit)
    vm = pltpu.VMEM
    windows = 2 * micro

    def steps(rows, cols):
        return [vm((rows // 2, cols), BF16)] * 3

    def deep_steps(rows, cols):
        return steps(rows, cols) + [vm((rows // (4 * nx), cols), BF16)] * 2

    scratch = (
        [vm((ra, 128), BF16), vm((rb, 256), BF16), vm((ra, 128), BF16), vm((rb, 256), BF16)]
        + [vm((rb, 256), BF16), vm((rg, 128), BF16), vm((rg, 128), BF16)]
        + deep_steps(rb, 256) + deep_steps(ra, 128) + deep_steps(rb, 256) + deep_steps(rg, 128)
        + steps(rg, 128)
        + [vm((tokens, packed), BF16), vm((packed, tokens), BF16)]
        + [vm((micro, packed, 256), BF16)] * 2
        + [vm((micro, packed, 128), BF16)] * 3
        + [vm((micro, packed, 256), BF16)]
        + [
            vm((windows, tokens, 256), BF16),
            vm((windows, tokens, 256), BF16),
            vm((windows, tokens, 128), BF16),
            vm((windows, tokens, 128), BF16),
            vm((windows, tokens, 128), F32),
            vm((windows, tokens, 128), BF16),
            vm((tokens, 256), BF16),
            vm((tokens, 256), BF16),
            vm((tokens, 256), F32),
            vm((tokens, 256), F32),
            vm((micro, tokens, 256), F32),
            vm((windows, tokens, 128), BF16),
            vm((micro + 1, tokens, 256), F32),
            vm((2, 16, 128), F32),
            vm((256, 256), F32),
            vm((256, 1024), F32),
            vm((256, 1024), F32),
            vm((8, 256), F32),
            vm((2, 256, 384), F32),
            vm((2, 16, 128), F32),
            vm((tokens, 256), BF16),
        ]
        + [pltpu.SemaphoreType.DMA((micro,))] * 8
        + [pltpu.SemaphoreType.DMA((k,)) for k in (12, 12, 12, 12, 8)]
        + [vm(top.shape, BF16)]
        + [vm(w.shape, F32) for w in (w_proj, w_fc1, w_fc2)]
        + [pltpu.SemaphoreType.DMA((4,))]
    )
    whole_vmem = pl.BlockSpec(memory_space=vm)
    return pl.pallas_call(
        functools.partial(block_kernel, nb, nx, length),
        in_specs=[pl.BlockSpec(memory_space=pltpu.SMEM)]
        + [whole_vmem] * 3
        + [pl.BlockSpec(memory_space=pl.ANY)] * 4,
        out_specs=[whole_vmem] * 5,
        out_shape=[
            shape_of(BF16, micro, tokens, 256), shape_of(BF16, micro, tokens, 256),
            shape_of(BF16, rb, 256), shape_of(BF16, rg, 128), shape_of(BF16, rg, 128),
        ],
        scratch_shapes=scratch,
        compiler_params=pltpu.CompilerParams(
            collective_id=0, has_side_effects=True, vmem_limit_bytes=VMEM_LIMIT
        ),
        name="block",
    )(owners, x, w_qkv, vectors, top, w_proj, w_fc1, w_fc2)


def adam_kernel(
    own_ref, gb_ref, gav_ref, gah_ref, vec_ref, vf_ref, vs_ref, *refs,
):
    through = refs[0:2]
    moments = refs[2:14]
    bases = refs[14:22]
    grads_hbm = refs[22:26]
    outs = refs[26:38]
    vg_ref, vfn_ref, vsn_ref, vn_ref = refs[38:42]
    through_out = refs[42:44]
    held = refs[44:56]
    left = refs[56:64]
    grads = refs[64:68]
    zeros_ref, in_sem, out_sem, grad_sem, through_sem = refs[68:73]
    device = lax.axis_index("band") * lax.axis_size("batch") + lax.axis_index("batch")
    is_own = [own_ref[i] == device for i in range(4)]
    any_own = is_own[0] | is_own[1] | is_own[2] | is_own[3]

    def load(i):
        pairs = [(moments[3 * i + j].at[0], held[3 * i + j], 5 * i + j) for j in range(3)]
        pairs += [(bases[2 * i + j], left[2 * i + j], 5 * i + 3 + j) for j in range(2)]
        return [pltpu.make_async_copy(a, b, in_sem.at[s]) for a, b, s in pairs]

    def store(i, j):
        at = 3 * i + j
        return pltpu.make_async_copy(held[at], outs[at].at[0], out_sem.at[at])

    def blank(i):
        copies = []
        for j in range(3):
            shape = outs[3 * i + j].shape
            copies.append(
                pltpu.make_async_copy(
                    zeros_ref.at[pl.ds(0, shape[1]), pl.ds(0, shape[2])],
                    outs[3 * i + j].at[0],
                    out_sem.at[3 * i + j],
                )
            )
        return copies

    def start_blanks():
        for i in range(4):
            @pl.when(jnp.logical_not(is_own[i]))
            def _():
                for c in blank(i):
                    c.start()

    for i in range(4):
        @pl.when(is_own[i])
        def _():
            for c in load(i):
                c.start()

    zeros_ref[...] = jnp.zeros_like(zeros_ref)
    pl.when(jnp.logical_not(any_own))(start_blanks)
    passing = [
        pltpu.make_async_copy(a, b, through_sem.at[i])
        for i, (a, b) in enumerate(zip(through, through_out))
    ]
    for c in passing:
        c.start()

    for b in range(3):
        for half, ref in ((0, gah_ref), (1, gav_ref)):
            at = 256 * b + 128 * half
            grads[0][:, at : at + 128] = ref[256 * b : 256 * b + 256, :].astype(F32)
    grads[1][...] = gb_ref[0:256, :].astype(F32)
    for f in range(4):
        grads[2][:, 256 * f : 256 * f + 256] = gb_ref[256 * (f + 1) : 256 * (f + 2), :].astype(F32)
    grads[3][...] = gb_ref[1280:ROWS_B, :].astype(F32)
    giving = [pltpu.make_async_copy(grads[i], grads_hbm[i], grad_sem.at[i]) for i in range(4)]
    for c in giving:
        c.start()

    mid = gb_ref[ROWS_B : ROWS_B + 8, :].astype(F32) + gb_ref[ROWS_B + 8 : ROWS_B + 16, :].astype(F32)
    side = [r[768:784, :].astype(F32) + r[784:800, :].astype(F32) for r in (gah_ref, gav_ref)]
    both = side[0] + side[1]
    for i in range(2):
        vg_ref[0:1, 128 * i : 128 * i + 128] = both[12 + i : 13 + i]
        vg_ref[1:2, 128 * i : 128 * i + 128] = both[14 + i : 15 + i]
        vg_ref[2:4, 128 * i : 128 * i + 128] = side[i][0:2]
        vg_ref[21:22, 128 * i : 128 * i + 128] = side[i][11:12]
        for t in range(9):
            row = 12 + (t if i == 0 else 3 * (t % 3) + t // 3)
            vg_ref[row : row + 1, 128 * i : 128 * i + 128] = side[i][2 + t : 3 + t]
    vg_ref[4:12, :] = mid
    grad = vg_ref[...]
    first_new = BETA_ONE * vf_ref[...] + (1.0 - BETA_ONE) * grad
    second_new = BETA_TWO * vs_ref[...] + (1.0 - BETA_TWO) * grad * grad
    vfn_ref[...] = first_new
    vsn_ref[...] = second_new
    vn_ref[...] = vec_ref[...] - RATE_VECTORS * (first_new / (1.0 - BETA_ONE**STEP)) / (
        jnp.sqrt(second_new / (1.0 - BETA_TWO**STEP)) + EPS_ADAM
    )

    for i in range(4):
        @pl.when(is_own[i])
        def _():
            for c in load(i):
                c.wait()

    pl.when(any_own)(start_blanks)

    for i in range(4):
        @pl.when(is_own[i])
        def _():
            first, second, weight = held[3 * i], held[3 * i + 1], held[3 * i + 2]
            g = grads[i][...].astype(BF16)
            lh, rh = left[2 * i][...].astype(BF16), left[2 * i + 1][...].astype(BF16)
            once = jnp.transpose(mm_tn(g, lh)) if i == 3 else mm_tn(lh, g)
            turned_grad = mm(once.astype(BF16), rh)
            first_new = BETA_ONE * first[...] + (1.0 - BETA_ONE) * turned_grad
            second_new = BETA_TWO * second[...] + (1.0 - BETA_TWO) * turned_grad * turned_grad
            first[...] = first_new
            second[...] = second_new
            store(i, 0).start()
            store(i, 1).start()
            step = (first_new / (1.0 - BETA_ONE**STEP)) / (
                jnp.sqrt(second_new / (1.0 - BETA_TWO**STEP)) + EPS_ADAM
            )
            back = mm_nt(mm(lh, step.astype(BF16)).astype(BF16), rh)
            weight[...] = weight[...] - RATE * back - RATE * DECAY * weight[...]
            store(i, 2).start()

    for c in giving + passing:
        c.wait()
    for i in range(4):
        for j in range(3):
            store(i, j).wait()


def adam_call(
    owners, gb, gav, gah, vectors, vectors_first, vectors_second, through, slots, bases
):
    vm = pltpu.VMEM
    any_space = pl.BlockSpec(memory_space=pl.ANY)
    vspec = pl.BlockSpec(memory_space=vm)
    sizes = [(s.shape[1], s.shape[2]) for s in slots[::3]]
    vshape = shape_of(F32, *vectors.shape)
    tallest = max(a for a, _ in sizes)
    widest = max(b for _, b in sizes)
    dma = pltpu.SemaphoreType.DMA
    return pl.pallas_call(
        adam_kernel,
        in_specs=[pl.BlockSpec(memory_space=pltpu.SMEM)] + [vspec] * 8 + [any_space] * 20,
        out_specs=[any_space] * 16 + [vspec] * 4 + [any_space] * 2,
        out_shape=[shape_of(F32, *s) for s in sizes]
        + [shape_of(F32, *s.shape) for s in slots]
        + [vshape] * 4
        + [shape_of(t.dtype, *t.shape) for t in through],
        scratch_shapes=[vm((s.shape[1], s.shape[2]), F32) for s in slots]
        + [vm(b.shape, F32) for b in bases]
        + [vm(s, F32) for s in sizes]
        + [vm((tallest, widest), F32), dma((20,)), dma((12,)), dma((4,)), dma((2,))],
        compiler_params=pltpu.CompilerParams(vmem_limit_bytes=VMEM_LIMIT),
        name="adam",
    )(owners, gb, gav, gah, vectors, vectors_first, vectors_second, *through, *slots, *bases)


def wide_to_stack(w):
    n = w.shape[1] // 256
    return w.reshape(256, n, 256).transpose(1, 0, 2).reshape(256 * n, 256)


def by_steps(x, top, owners, slots, vectors, nb, nx, length):
    device_index = lax.axis_index(("band", "batch"))

    def own(slot, which):
        return jnp.where(device_index == owners[which], slot[0], 0.0).astype(BF16)

    stacked = jnp.concatenate(
        [
            wide_to_stack(own(slots[0], 0)),
            own(slots[1], 1),
            wide_to_stack(own(slots[2], 2)),
            own(slots[3], 3),
        ],
        axis=0,
    )
    weights = sum_everywhere(stacked, nb, nx, 0)[:ROW_END]

    def swap(packed, cid):
        m, rows, ch = packed.shape
        swapped = packed.reshape(m, nb, PIECE, ch).transpose(1, 0, 2, 3).reshape(m * rows, ch)
        got = exchange(swapped, nb, cid)
        return got.reshape(nb, m, PIECE, ch).transpose(1, 0, 2, 3).reshape(m, rows, ch)

    columns = swap(pack_tokens(x, nb, length), 1)
    qa_v, k_v, v_v, o_v, att_v, x_v = forward_call(columns, 1, nb, length, weights, vectors)
    qa_h, k_h, v_h, o_h, att_h = forward_call(x, 0, nb, length, weights, vectors)
    att_v = swap(att_v, 2)
    block_out, grad_middle, grad_h, grad_v, gp_t, g1, g2_t, rows_mid = middle_call(
        x, att_h, att_v, top, nb, length, weights, vectors
    )
    grad_v = swap(grad_v, 3)
    part_v, gw_v, rows_v = backward_call(
        x_v, grad_v, qa_v, k_v, v_v, o_v, 1, nb, length, weights, vectors
    )
    part_h, gw_h, rows_h = backward_call(
        x, grad_h, qa_h, k_h, v_h, o_h, 0, nb, length, weights, vectors
    )
    part_v = swap(part_v, 4)
    input_grad = last_call(x, grad_middle, part_h, part_v, nb, length, vectors)

    def two(rows):
        high = rows.astype(BF16)
        return [high, (rows - high.astype(F32)).astype(BF16)]

    gb = jnp.concatenate(
        [gp_t.T.astype(BF16), wide_to_stack(g1.astype(BF16)), g2_t.T.astype(BF16)] + two(rows_mid),
        axis=0,
    )

    def side(gw, rows):
        return jnp.concatenate(
            [gw[:, 128 * b : 128 * b + 128].astype(BF16) for b in range(3)] + two(rows), axis=0
        )

    gb = sum_everywhere(gb, nb, nx, 5)
    gav = sum_everywhere(side(gw_v, rows_v), nb, nx, 6)
    gah = sum_everywhere(side(gw_h, rows_h), nb, nx, 7)
    return block_out, input_grad, gb, gav, gah


def per_device(
    tokens_in, cotangent, owners,
    weight_qkv, weight_proj, weight_fc1, weight_fc2,
    first_qkv, second_qkv, first_proj, second_proj, first_fc1, second_fc1, first_fc2, second_fc2,
    left_qkv, right_qkv, left_proj, right_proj, left_fc1, right_fc1, left_fc2, right_fc2,
    vectors, vectors_first, vectors_second,
    *, nb, nx,
):
    micro, images, band_rows, length, channels = tokens_in.shape
    tokens = band_rows * length
    x = tokens_in.reshape(micro * images, tokens, channels)
    top = cotangent.reshape(micro * images, tokens, channels)
    weights = (weight_qkv, weight_proj, weight_fc1, weight_fc2)
    if tokens <= LONGEST:
        block_out, input_grad, gb, gav, gah = block_call(
            x, top, owners, *weights, vectors, nb, nx, length
        )
    else:
        block_out, input_grad, gb, gav, gah = by_steps(
            x, top, owners, weights, vectors, nb, nx, length
        )
    slots = (
        first_qkv, second_qkv, weight_qkv, first_proj, second_proj, weight_proj,
        first_fc1, second_fc1, weight_fc1, first_fc2, second_fc2, weight_fc2,
    )
    bases = (left_qkv, right_qkv, left_proj, right_proj, left_fc1, right_fc1, left_fc2, right_fc2)
    done = adam_call(
        owners, gb, gav, gah, vectors, vectors_first, vectors_second,
        (block_out, input_grad), slots, bases,
    )
    results = [done[20].reshape(tokens_in.shape), done[21].reshape(tokens_in.shape)]
    for i in range(4):
        results.append(done[i])
        results += list(done[4 + 3 * i : 7 + 3 * i])
    return tuple(results) + tuple(done[16:20])


def solution(mesh):
    tokens_spec = P(None, "batch", "band", None, None)
    slot_spec = P(("band", "batch"), None, None)
    return jax.shard_map(
        functools.partial(per_device, nb=mesh.shape["band"], nx=mesh.shape["batch"]),
        mesh=mesh,
        in_specs=(tokens_spec, tokens_spec, P()) + (slot_spec,) * 12 + (P(),) * 11,
        out_specs=(tokens_spec, tokens_spec)
        + (P(), slot_spec, slot_spec, slot_spec) * 4
        + (P(),) * 4,
        check_vma=False,
    )
```
